128 devices in a mesh: dp: 16 (over y_hi, x, core), row: 2 (over y_lo), col: 4 (over z).
Axes of the slice: x: 4, y: 4 (y_hi: 2, y_lo: 2; y = y_hi * 2 + y_lo), z: 4, core: 2. Of those that a mesh axis runs over, the one named last changes fastest.
Arguments:
- tokens: bfloat16 [16384, 1024], P(('dp', 'col'), 'row'), may hold values from -13 to 13
- segment_ids: int32 [16384], P('dp'), may hold values from 0 to 2, as said below
- w_qkv: bfloat16 [3, 1024, 1024], P(None, 'row', 'col'), may hold values from -0.1875 to 0.1875
- b_qkv: bfloat16 [3, 1024], P(None, 'col'), may hold values from -3 to 3
- w_out: bfloat16 [1024, 1024], P('col', 'row'), may hold values from -0.75 to 0.75
- b_out: bfloat16 [1024], P('row'), may hold values from -2 to 2
- w_up: bfloat16 [1024, 4096], P('row', 'col'), may hold values from -0.1875 to 0.1875
- b_up: bfloat16 [4096], P('col'), may hold values from -3 to 3
- w_down: bfloat16 [4096, 1024], P('col', 'row'), may hold values from -0.09375 to 0.09375
- b_down: bfloat16 [1024], P('row'), may hold values from -2 to 2
- norm_gain: bfloat16 [2, 1024], P(None, 'row'), may hold values from 0.2 to 2.5
- norm_bias: bfloat16 [2, 1024], P(None, 'row'), may hold values from -2 to 2
- cotangent: bfloat16 [16384, 1024], P(('dp', 'col'), 'row'), may hold values from -6 to 6
Outputs:
- output: bfloat16 [16384, 1024], P(('dp', 'col'), 'row')
- tokens_grad: bfloat16 [16384, 1024], P(('dp', 'col'), 'row')
- w_qkv_grad: float32 [3, 1024, 1024], P(None, 'row', 'col')
- b_qkv_grad: float32 [3, 1024], P(None, 'col')
- w_out_grad: float32 [1024, 1024], P('col', 'row')
- b_out_grad: float32 [1024], P('row')
- w_up_grad: float32 [1024, 4096], P('row', 'col')
- b_up_grad: float32 [4096], P('col')
- w_down_grad: float32 [4096, 1024], P('col', 'row')
- b_down_grad: float32 [1024], P('row')
- norm_gain_grad: float32 [2, 1024], P(None, 'row')
- norm_bias_grad: float32 [2, 1024], P(None, 'row')
The draws below stay inside these ranges and needn't reach their ends.
Inputs may be any that keep to these rules, and one draw needn't show every extreme that they name: `segment_ids`: within each packed sequence of 1024 tokens the ids never fall, the first token has 0 and the last 2.
All inputs are finite; a program needn't handle non-finite values.
Results may differ from the reference program's by a relative error of at most 0.012.
The reference program's roundings to bfloat16 on the way count: a program that leaves them out, or rounds other values in their place, can miss the bound.
Values may be sent and summed in bfloat16 or wider, within the bound.
A program may use at most 128 MiB of HBM per device.

```python
import math
import jax
import jax.numpy as jnp
from jax import lax

D = 1024
H = 16
HD = 64
ROT = 16
FF = 4096
SEQ_LEN = 1024
TOKENS = 16384


def draw_segment_ids(key, part):
    key = jax.random.fold_in(key, 7)
    seq_count = TOKENS // SEQ_LEN
    key_start, key_end = jax.random.split(key)
    start_cut = jax.random.randint(key_start, (seq_count, 1), 1, SEQ_LEN // 8 + 1)
    end_cut = SEQ_LEN - jax.random.randint(key_end, (seq_count, 1), 1, SEQ_LEN // 8 + 1)
    position = jnp.arange(SEQ_LEN, dtype=jnp.int32)[None, :]
    seg_ids = (position >= start_cut).astype(jnp.int32) + (position >= end_cut).astype(jnp.int32)
    return seg_ids.reshape(-1).astype(jnp.int32)


def draw_tokens(key, part):
    key = jax.random.fold_in(key, 11)
    key_noise, key_shift = jax.random.split(key)
    column = jnp.arange(D, dtype=jnp.float32) / (D - 1)
    scale_col = 0.5 * 4.0 ** column
    noise = jnp.clip(jax.random.normal(key_noise, (TOKENS, D), jnp.float32), -6.0, 6.0)
    shift_col = 0.4 * jax.random.uniform(key_shift, (1, D), jnp.float32, -1.0, 1.0) + 0.3
    values = scale_col[None, :] * (noise + shift_col)
    return jnp.clip(values, -13.0, 13.0).astype(jnp.bfloat16)


def draw_norm_gain(key, part):
    key = jax.random.fold_in(key, 13)
    column = jnp.arange(D, dtype=jnp.float32) / (D - 1)
    ramp = 0.5 * 3.0 ** column
    jitter = 1.0 + 0.1 * jnp.clip(jax.random.normal(key, (2, D), jnp.float32), -3.0, 3.0)
    return jnp.clip(ramp[None, :] * jitter, 0.2, 2.5).astype(jnp.bfloat16)


def block_levels(key, dims, cuts, least, top_value):
    def one(axis_at, blocks):
        steps = jax.random.uniform(jax.random.fold_in(jax.random.fold_in(key, 6), axis_at), (blocks,), jnp.float32, least / len(cuts), top_value / len(cuts))
        return jnp.repeat(jnp.exp(steps), dims[axis_at] // blocks).reshape((-1,) + (1,) * (len(dims) - axis_at - 1))

    factor_of = one(*cuts[0])
    for cut in cuts[1:]:
        factor_of = factor_of * one(*cut)
    return factor_of


def normal_values(key, shape, scale, limit, cuts=(), kind=jnp.bfloat16):
    drawn = jax.random.normal(key, shape, jnp.float32) * scale
    if len(cuts) > 0:
        drawn = block_levels(key, shape, cuts, -0.22, 0.18) * drawn
    return jnp.clip(drawn, min=-limit, max=limit).astype(kind)


def setup_inputs(seed: int = 0) -> dict:
    streams_of = jax.random.split(jax.random.key(seed), 14)
    return {
        "tokens": draw_tokens(jax.random.fold_in(streams_of[13], 71), 0),
        "segment_ids": draw_segment_ids(jax.random.fold_in(streams_of[13], 71), 0),
        "w_qkv": normal_values(streams_of[2], (3, D, D), D ** -0.5, 0.1875, ((1, 2), (2, 4))),
        "b_qkv": normal_values(streams_of[3], (3, D), 0.5, 3.0, ((1, 4),)),
        "w_out": normal_values(streams_of[4], (D, D), (D // 16) ** -0.5, 0.75, ((0, 4), (1, 2))),
        "b_out": normal_values(streams_of[5], (D,), 0.3, 2.0, ((0, 2),)),
        "w_up": normal_values(streams_of[6], (D, FF), D ** -0.5, 0.1875, ((0, 2), (1, 4))),
        "b_up": normal_values(streams_of[7], (FF,), 0.5, 3.0, ((0, 4),)),
        "w_down": normal_values(streams_of[8], (FF, D), FF ** -0.5, 0.09375, ((0, 4), (1, 2))),
        "b_down": normal_values(streams_of[9], (D,), 0.3, 2.0, ((0, 2),)),
        "norm_gain": draw_norm_gain(jax.random.fold_in(streams_of[13], 71), 0),
        "norm_bias": normal_values(streams_of[11], (2, D), 0.3, 2.0, ((1, 2),)),
        "cotangent": normal_values(streams_of[12], (TOKENS, D), 1.0, 6.0, ((0, 64), (1, 2))),
    }


@jax.custom_vjp
def low(v):
    return lax.optimization_barrier(v.astype(jnp.bfloat16)).astype(jnp.float32)

@jax.custom_vjp
def low_back(v):
    return v

def low_keep(v):
    return (low(v), None)

def low_pass(kept, grad):
    return (grad,)

def back_keep(v):
    return (v, None)

def back_low(kept, grad):
    return (low(grad),)
low.defvjp(low_keep, low_pass)
low_back.defvjp(back_keep, back_low)
EPSILON = 1e-05

def rotary_tables(position):
    freq_index = jnp.arange(ROT // 2, dtype=jnp.float32)
    inverse = 10000.0 ** (-2.0 * freq_index / ROT)
    angles = position[:, None] * inverse[None, :]
    return (jnp.cos(angles), jnp.sin(angles))

def rotate(values_in, cosine_tab, sine_tab, rotation_sign):
    length = values_in.shape[0]
    shaped = values_in.reshape(length, -1, HD)
    half_rot = ROT // 2
    front_part = shaped[:, :, :half_rot]
    behind = shaped[:, :, half_rot:ROT]
    remain = shaped[:, :, ROT:]
    cos_b = cosine_tab[:, None, :]
    sin_b = sine_tab[:, None, :]
    turned_front = front_part * cos_b - rotation_sign * behind * sin_b
    turned_back = behind * cos_b + rotation_sign * front_part * sin_b
    return jnp.concatenate([turned_front, turned_back, remain], axis=2).reshape(values_in.shape)

def attend_head(query_h, key_h, value_h, allowed):
    highest = lax.Precision.HIGHEST
    scores = low_back(jnp.einsum('qd,kd->qk', query_h, key_h, precision=highest) * (1.0 / math.sqrt(HD)))
    scores = jnp.where(allowed, scores, -1e+30)
    shifted = scores - lax.optimization_barrier(jnp.max(scores, axis=-1, keepdims=True))
    expo_val = jnp.exp(shifted)
    prob_full = expo_val / lax.optimization_barrier(jnp.sum(expo_val, axis=-1, keepdims=True))
    return jnp.dot(low(prob_full), value_h, precision=highest)

def block_forward(x_row, segment, params):
    w_qkv, b_qkv, w_out, b_out, w_up, b_up, w_down, b_down, norm_gain, norm_bias = params
    highest = lax.Precision.HIGHEST
    mean_val = lax.optimization_barrier(jnp.mean(x_row, axis=-1, keepdims=True))
    square = lax.optimization_barrier(jnp.mean(x_row * x_row, axis=-1, keepdims=True))
    normed = (x_row - mean_val) * lax.rsqrt(square - mean_val * mean_val + EPSILON)
    attn_in = low(normed * norm_gain[0] + norm_bias[0])
    mlp_in = low(normed * norm_gain[1] + norm_bias[1])
    qkv_pre = jnp.einsum('td,kde->kte', attn_in, w_qkv, precision=highest) + b_qkv[:, None, :]
    length = x_row.shape[0]
    cosine_tab, sine_tab = rotary_tables(jnp.arange(length, dtype=jnp.float32))
    query_all = low(rotate(low_back(qkv_pre[0]), cosine_tab, sine_tab, 1.0))
    key_all = low(rotate(low_back(qkv_pre[1]), cosine_tab, sine_tab, 1.0))
    value_all = low(low_back(qkv_pre[2]))
    row_ids = jnp.arange(length)
    allowed = (row_ids[None, :] <= row_ids[:, None]) & (segment[:, None] == segment[None, :])

    def to_heads(values_in):
        return values_in.reshape(length, H, HD).transpose(1, 0, 2)

    def one_head(triple):
        return jax.checkpoint(attend_head)(triple[0], triple[1], triple[2], allowed)
    mixed = lax.map(one_head, (to_heads(query_all), to_heads(key_all), to_heads(value_all)))
    mixed = low(low_back(mixed.transpose(1, 0, 2).reshape(length, D)))
    attn_branch = jnp.dot(mixed, w_out, precision=highest) + b_out
    hidden_pre = low_back(jnp.dot(mlp_in, w_up, precision=highest) + b_up)
    hidden = low(jax.nn.gelu(hidden_pre, approximate=False))
    mlp_branch = jnp.dot(hidden, w_down, precision=highest) + b_down
    return x_row + attn_branch + mlp_branch

def forward(x_all, segments, params):
    seq_count = TOKENS // SEQ_LEN
    stacked = x_all.reshape(seq_count, SEQ_LEN, D)
    seg_stack = segments.reshape(seq_count, SEQ_LEN)

    def scan_step(state_in, pair_in):
        return (state_in, jax.checkpoint(block_forward)(pair_in[0], pair_in[1], params))
    state_out, result = lax.scan(scan_step, jnp.zeros((), jnp.float32), (stacked, seg_stack))
    return result.reshape(TOKENS, D)

def reference(tokens, segment_ids, w_qkv, b_qkv, w_out, b_out, w_up, b_up, w_down, b_down, norm_gain, norm_bias, cotangent):
    params = tuple((weight_arr.astype(jnp.float32) for weight_arr in (w_qkv, b_qkv, w_out, b_out, w_up, b_up, w_down, b_down, norm_gain, norm_bias)))

    def apply_all(x_val, weight_set):
        return forward(x_val, segment_ids, weight_set)
    output, pullback = jax.vjp(apply_all, tokens.astype(jnp.float32), params)
    x_grad, grads = pullback(cotangent.astype(jnp.float32))
    return (output.astype(jnp.bfloat16), x_grad.astype(jnp.bfloat16), grads[0], grads[1], grads[2], grads[3], grads[4], grads[5], grads[6], grads[7], grads[8], grads[9])
```

```python
from types import SimpleNamespace
import math

import numpy as np
import jax
import jax.numpy as jnp
from jax import lax
from jax.experimental import pallas as pl
from jax.experimental.pallas import tpu as pltpu
from jax.sharding import PartitionSpec as P

MESH = pl.DeviceIdType.MESH
BF = jnp.bfloat16
F32 = jnp.float32
T = 1024
D = 1024
HD = 64
ROT = 16
E = 128
F = 512
B = 256
EPSILON = 1e-05
NSEM = 96


def nn(a, b):
    return jnp.dot(a, b, preferred_element_type=F32)


def nt(a, b):
    return lax.dot_general(a, b, (((1,), (1,)), ((), ())), preferred_element_type=F32)


def tn(a, b):
    return lax.dot_general(a, b, (((0,), (0,)), ((), ())), preferred_element_type=F32)


def rows(block, size=B):
    return pl.ds(pl.multiple_of(block * size, size), size)


class Net:
    def __init__(self, send, recv):
        self.send, self.recv, self.count, self.sent = send, recv, 0, []

    def go(self, src, dst, device):
        k = self.count
        self.count += 1
        assert k < NSEM
        copy = pltpu.make_async_remote_copy(
            src_ref=src,
            dst_ref=dst,
            send_sem=self.send.at[k],
            recv_sem=self.recv.at[k],
            device_id=device,
            device_id_type=MESH,
        )
        copy.start()
        self.sent.append(copy)
        return copy

    def local(self, src, dst):
        k = self.count
        self.count += 1
        assert k < NSEM
        copy = pltpu.make_async_copy(src, dst, self.send.at[k])
        copy.start()
        return copy


def gather_tokens(net, own, full, at, half, col, row):
    right, left, peer = at["z1"], at["z3"], at["y1"]

    def place(c, h):
        return full.at[rows(c), pl.ds(pl.multiple_of(h * half, half), half)]

    mine, other = place(col, row), place(col, 1 - row)
    lcol, rcol = lax.rem(col + 3, 4), lax.rem(col + 1, 4)
    c0 = net.go(own, mine, peer)
    c1 = net.go(own, mine, right)
    c2 = net.go(own, mine, left)
    keep = net.local(own, mine)
    yield
    c0.wait_recv()
    c3 = net.go(other, other, right)
    c4 = net.go(other, other, left)
    yield
    c1.wait_recv()
    c5 = net.go(place(lcol, row), place(lcol, row), right)
    yield
    c4.wait_recv()
    c6 = net.go(place(rcol, 1 - row), place(rcol, 1 - row), left)
    yield
    keep.wait()
    c2.wait_recv()
    c3.wait_recv()
    yield
    c5.wait_recv()
    c6.wait_recv()


def ring_scatter(net, part, bufs, me, right, left, size, width):
    ta, tb, inl, inr = bufs
    lo, hi = pl.ds(0, width), pl.ds(width, width)
    far, rb, lb = lax.rem(me + 2, 4), lax.rem(me + 1, 4), lax.rem(me + 3, 4)
    a = net.go(part(far, lo), ta, right)
    b = net.go(part(far, hi), tb, left)
    c = net.go(part(rb, hi), inl.at[:, hi], right)
    d = net.go(part(lb, lo), inr.at[:, lo], left)
    yield
    a.wait_recv()
    view = part(rb, lo)
    view[...] = (view[...].astype(F32) + ta[...].astype(F32)).astype(BF)
    e = net.go(view, inl.at[:, lo], right)
    b.wait_recv()
    view = part(lb, hi)
    view[...] = (view[...].astype(F32) + tb[...].astype(F32)).astype(BF)
    f = net.go(view, inr.at[:, hi], left)
    yield
    for copy in (c, d, e, f):
        copy.wait_recv()


def reduce_weights(net, grad, s, at, me, n):
    core, x, row = me["core"], me["x"], me["row"]
    half, size = n // 2, n // 8
    base = core * half
    away = (1 - core) * half
    c = net.go(grad.at[pl.ds(pl.multiple_of(away, half), half)], s.rc, at["core"])
    yield
    c.wait_recv()
    own = grad.at[pl.ds(pl.multiple_of(base, half), half)]
    own[...] = (own[...].astype(F32) + s.rc[...].astype(F32)).astype(BF)

    def part(block, cols):
        return grad.at[pl.ds(pl.multiple_of(base + block * size, size), size), cols]

    yield from ring_scatter(
        net, part, (s.ta, s.tb, s.inl, s.inr), x, at["x1"], at["x3"], size, D // 2
    )
    for h in range(2):
        cols = pl.ds(h * (D // 2), D // 2)
        total = (
            part(x, cols)[...].astype(F32) + s.inl[:, cols].astype(F32) + s.inr[:, cols].astype(F32)
        )
        s.sy[h] = total.astype(BF)
    g0 = net.go(s.sy.at[row], s.ry.at[0], at["y2"])
    g1 = net.go(s.sy.at[1 - row], s.ry.at[1], at["y1"])
    g2 = net.go(s.sy.at[1 - row], s.ry.at[2], at["y3"])
    yield
    g0.wait_recv()
    s.fin[core, x, row] = (s.sy[row].astype(F32) + s.ry[0].astype(F32)).astype(BF)
    g1.wait_recv()
    g2.wait_recv()
    s.fin[core, x, 1 - row] = (s.ry[1].astype(F32) + s.ry[2].astype(F32)).astype(BF)
    h0 = s.fin.at[core, x, 0]
    h1 = s.fin.at[core, x, 1]
    a0 = net.go(h0, h0, at["x1"])
    a1 = net.go(h1, h1, at["x3"])
    a2 = net.go(h1, h1, at["x1"])
    a3 = net.go(h0, h0, at["x3"])
    k0 = net.go(s.fin.at[core, x], s.fin.at[core, x], at["core"])
    yield
    lx, rx = lax.rem(x + 3, 4), lax.rem(x + 1, 4)
    a0.wait_recv()
    v = s.fin.at[core, lx, 0]
    a4 = net.go(v, v, at["x1"])
    a1.wait_recv()
    v = s.fin.at[core, rx, 1]
    a5 = net.go(v, v, at["x3"])
    a2.wait_recv()
    v = s.fin.at[core, lx]
    k1 = net.go(v, v, at["core"])
    a3.wait_recv()
    v = s.fin.at[core, rx]
    k2 = net.go(v, v, at["core"])
    yield
    a4.wait_recv()
    a5.wait_recv()
    v = s.fin.at[core, lax.rem(x + 2, 4)]
    k3 = net.go(v, v, at["core"])
    for copy in (k0, k1, k2):
        copy.wait_recv()
    yield
    k3.wait_recv()


def reduce_vectors(net, s, at):
    c = net.go(s.vec, s.vr.at[0], at["core"])
    yield
    c.wait_recv()
    s.vs[0] = s.vec[...] + s.vr[0]
    for n, axis in enumerate("xyz"):
        copies = [net.go(s.vs.at[n], s.vr.at[3 * n + k], at[axis + str(k)]) for k in (1, 2, 3)]
        yield
        for copy in copies:
            copy.wait_recv()
        s.vs[n + 1] = (s.vs[n] + s.vr[3 * n + 1]) + (s.vr[3 * n + 2] + s.vr[3 * n + 3])


def step(gen):
    next(gen, None)


def finish(gen):
    for _ in gen:
        pass


def interleave(*gens):
    live = list(gens)
    while live:
        for gen in list(live):
            try:
                next(gen)
            except StopIteration:
                live.remove(gen)


def turn(values, cos, sin):
    lane = lax.broadcasted_iota(jnp.int32, values.shape, 1)
    other = jnp.where(lane % HD < ROT // 2, pltpu.roll(values, E - ROT // 2, 1), pltpu.roll(values, ROT // 2, 1))
    return values * cos + other * sin


def split_heads(ref, at_rows, values):
    lane = lax.broadcasted_iota(jnp.int32, values.shape, 1)
    zero = jnp.zeros_like(values)
    ref[0, at_rows, :] = jnp.where(lane < HD, values, zero).astype(BF)
    ref[1, at_rows, :] = jnp.where(lane < HD, zero, values).astype(BF)


SCRATCH = dict(
    xall=((T, D), BF),
    gall=((T, D), BF),
    ain=((T, D), BF),
    mim=((T, D), BF),
    wq=((D, 3 * E), BF),
    wo=((E, D), BF),
    wu=((D, F), BF),
    wd=((F, D), BF),
    nb=((2, 8, D // 2), F32),
    mean=((T, 1), F32),
    inv=((T, 1), F32),
    hid=((T, F), BF),
    hpg=((T, F), BF),
    qs=((T, E), BF),
    qsm=((2, T, E), BF),
    km=((2, T, E), BF),
    vm=((2, T, E), BF),
    kt=((E, T), BF),
    vt=((E, T), BF),
    do=((T, E), BF),
    dom=((2, T, E), BF),
    probs=((2, 2560, B), F32),
    mt=((E, T), BF),
    mixed=((T, E), BF),
    dqt=((E, T), F32),
    dk=((T, E), F32),
    dv=((T, E), F32),
    qkvg=((T, 3 * E), BF),
    op=((T, D), BF),
    ng=((T, D), BF),
    ota=((B, D // 2), BF),
    otb=((B, D // 2), BF),
    oinl=((B, D), BF),
    oinr=((B, D), BF),
    nta=((B, D // 2), BF),
    ntb=((B, D // 2), BF),
    ninl=((B, D), BF),
    ninr=((B, D), BF),
    ysend=((2, B, D // 2), BF),
    yrecv=((2, B, D // 2), BF),
    ssend=((B, 128), F32),
    srecv=((B, 128), F32),
    gm=((2 * F, D), BF),
    ga=((4 * E, D), BF),
    mrc=((F, D), BF),
    mta=((F // 4, D // 2), BF),
    mtb=((F // 4, D // 2), BF),
    minl=((F // 4, D), BF),
    minr=((F // 4, D), BF),
    msy=((2, F // 4, D // 2), BF),
    mry=((3, F // 4, D // 2), BF),
    arc=((2 * E, D), BF),
    ata=((E // 2, D // 2), BF),
    atb=((E // 2, D // 2), BF),
    ainl=((E // 2, D), BF),
    ainr=((E // 2, D), BF),
    asy=((2, E // 2, D // 2), BF),
    ary=((3, E // 2, D // 2), BF),
    vec=((8, D), F32),
    vr=((10, 8, D), F32),
    vs=((4, 8, D), F32),
)


def body(
    tok, cot, wqkv, wout, wup, wdown, small, segc, segr, ctab, stab,
    out, tgrad, fm, fa, vout, *scratch,
):
    s = SimpleNamespace(**dict(zip(SCRATCH, scratch)))
    send, recv = scratch[len(SCRATCH) :]
    net = Net(send, recv)
    dp, row, col = lax.axis_index("dp"), lax.axis_index("row"), lax.axis_index("col")
    core, x, yh = lax.rem(dp, 2), lax.rem(dp // 2, 4), dp // 8
    half = D // 2

    def dev(core=core, x=x, yh=yh, row=row, col=col):
        return (yh * 8 + x * 2 + core, row, col)

    at = {"core": dev(core=1 - core)}
    for k in (1, 2, 3):
        at[f"x{k}"] = dev(x=lax.rem(x + k, 4))
        at[f"z{k}"] = dev(col=lax.rem(col + k, 4))
    at["y1"] = dev(row=1 - row)
    at["y2"] = dev(yh=1 - yh)
    at["y3"] = dev(yh=1 - yh, row=1 - row)

    barrier = pltpu.get_barrier_semaphore()
    for device in at.values():
        pl.semaphore_signal(barrier, inc=1, device_id=device, device_id_type=MESH)
    pl.semaphore_wait(barrier, len(at))

    gx = gather_tokens(net, tok, s.xall, at, half, col, row)
    gg = gather_tokens(net, cot, s.gall, at, half, col, row)
    step(gx)

    mine, theirs = row, 1 - row
    drows = rows(row, half)
    y1, y3 = at["y1"], at["y3"]
    nbc = net.go(small.at[pl.ds(8, 8), pl.ds(0, half)], s.nb.at[row], y1)

    def shares(which):
        ecols = pl.ds(pl.multiple_of(which * E, E), E)
        fcols = pl.ds(pl.multiple_of(which * F, F), F)
        pairs = [(wqkv.at[k, :, ecols], s.wq.at[drows, pl.ds(k * E, E)]) for k in range(3)]
        pairs.append((wup.at[:, fcols], s.wu.at[drows]))
        pairs.append((wout.at[ecols], s.wo.at[:, drows]))
        pairs.append((wdown.at[fcols], s.wd.at[:, drows]))
        return pairs

    far = [y1, y1, y1, y3, y1, y3]
    wc = [net.go(a, b, d) for (a, b), d in zip(shares(theirs), far)]
    wl = [net.local(a, b) for a, b in shares(mine)]
    step(gx)
    s.nb[row] = small[pl.ds(8, 8), pl.ds(0, half)]
    s.vec[...] = jnp.zeros_like(s.vec)
    s.dk[...] = jnp.zeros_like(s.dk)
    s.dv[...] = jnp.zeros_like(s.dv)
    step(gg)
    step(gx)
    step(gx)
    step(gg)
    nbc.wait_recv()
    finish(gx)

    def wide(k):
        return jnp.concatenate([s.nb[0, k : k + 1, :], s.nb[1, k : k + 1, :]], axis=1)

    gain0, gain1, bias0, bias1 = wide(0), wide(1), wide(2), wide(3)

    @pl.loop(0, 8)
    def _(b):
        r = rows(b, 128)
        xv = s.xall[r, :].astype(F32)
        mean = jnp.sum(xv, axis=1, keepdims=True) * (1.0 / D)
        square = jnp.sum(xv * xv, axis=1, keepdims=True) * (1.0 / D)
        inv = lax.rsqrt(square - mean * mean + EPSILON)
        normed = (xv - mean) * inv
        s.mean[r, :] = mean
        s.inv[r, :] = inv
        s.ain[r, :] = (normed * gain0 + bias0).astype(BF)
        s.mim[r, :] = (normed * gain1 + bias1).astype(BF)

    step(gg)
    for copy in wl:
        copy.wait()
    for copy in wc:
        copy.wait_recv()

    ecols = pl.ds(pl.multiple_of(row * E, E), E)
    bq = jnp.concatenate([small[k : k + 1, ecols] for k in range(3)], axis=1)
    bu = small[3:4, pl.ds(pl.multiple_of(row * F, F), F)]

    @pl.loop(0, 4)
    def _(b):
        r = rows(b)
        pre = nn(s.ain[r, :], s.wq[...]) + bq
        cos, sin = ctab[r, :], stab[r, :]
        query = (turn(pre[:, :E], cos, sin)).astype(BF).astype(F32) * (1.0 / math.sqrt(HD))
        key = turn(pre[:, E : 2 * E], cos, sin).astype(BF).astype(F32)
        value = pre[:, 2 * E :].astype(BF).astype(F32)
        s.qs[r, :] = query.astype(BF)
        split_heads(s.qsm, r, query)
        split_heads(s.km, r, key)
        split_heads(s.vm, r, value)
        s.kt[:, r] = key.T.astype(BF)
        s.vt[:, r] = value.T.astype(BF)

    finish(gg)

    @pl.loop(0, 4)
    def _(b):
        r = rows(b)
        pre = nn(s.mim[r, :], s.wu[...]) + bu
        cdf = 0.5 * (1.0 + lax.erf(pre * math.sqrt(0.5)))
        s.hid[r, :] = (pre * cdf).astype(BF)
        slope = cdf + pre * jnp.exp(-0.5 * pre * pre) * (1.0 / math.sqrt(2.0 * math.pi))
        back = (nt(s.gall[r, :], s.wd[...]) * slope).astype(BF)
        s.hpg[r, :] = back
        fcols = pl.ds(pl.multiple_of(row * F, F), F)
        s.vec[6:7, fcols] += jnp.sum(back.astype(F32), axis=0, keepdims=True)
        gcols = pl.ds(pl.multiple_of(row * half, half), half)
        s.vec[4:5, gcols] += jnp.sum(s.gall[r, gcols].astype(F32), axis=0, keepdims=True)
        dout = nt(s.gall[r, :], s.wo[...]).astype(BF).astype(F32)
        s.do[r, :] = dout.astype(BF)
        split_heads(s.dom, r, dout)

    @pl.loop(0, 4)
    def _(b):
        r = rows(b, 128)
        s.gm[r, :] = tn(s.hid[:, r], s.gall[...]).astype(BF)
        r2 = pl.ds(pl.multiple_of(F + b * 128, 128), 128)
        s.gm[r2, :] = tn(s.hpg[:, r], s.mim[...]).astype(BF)

    sm = SimpleNamespace(
        rc=s.mrc, ta=s.mta, tb=s.mtb, inl=s.minl, inr=s.minr, sy=s.msy, ry=s.mry, fin=fm
    )
    sa = SimpleNamespace(
        rc=s.arc, ta=s.ata, tb=s.atb, inl=s.ainl, inr=s.ainr, sy=s.asy, ry=s.ary, fin=fa
    )
    where = dict(core=core, x=x, row=row)
    rm = reduce_weights(net, s.gm, sm, at, where, 2 * F)
    step(rm)

    first = [0, 256, 768, 1536]
    for i in range(4):
        n = (i + 1) * B
        q = pl.ds(i * B, B)

        @pl.loop(0, 2)
        def _(h):
            scores = nt(s.km[h, pl.ds(0, n), :], s.qs[q, :])
            kid = lax.broadcasted_iota(jnp.int32, (n, B), 0)
            qid = lax.broadcasted_iota(jnp.int32, (n, B), 1) + i * B
            allowed = (kid <= qid) & (segc[pl.ds(0, n), :] == segr[:, q])
            scores = jnp.where(allowed, scores, -1e30)
            top = jnp.max(scores, axis=0, keepdims=True)
            expo = jnp.exp(scores - top)
            probs = expo * (1.0 / jnp.sum(expo, axis=0, keepdims=True))
            s.probs[h, pl.ds(first[i], n), :] = probs
            hrows = rows(h, HD)
            s.mt[hrows, q] = nn(s.vt[hrows, pl.ds(0, n)], probs.astype(BF)).astype(BF)

        s.mixed[q, :] = s.mt[:, q].astype(F32).T.astype(BF)
        step(rm) if i in (0, 2, 3) else None

    @pl.loop(0, 4)
    def _(b):
        r = rows(b)
        s.op[r, :] = (nn(s.mixed[r, :], s.wo[...]) + nn(s.hid[r, :], s.wd[...])).astype(BF)

    def opart(block, cols):
        return s.op.at[rows(block), cols]

    def npart(block, cols):
        return s.ng.at[rows(block), cols]

    ro = ring_scatter(
        net, opart, (s.ota, s.otb, s.oinl, s.oinr), col, at["z1"], at["z3"], B, half
    )
    step(ro)
    s.ga[0:E, :] = nn(s.mt[...], s.gall[...]).astype(BF)

    for i in range(4):
        n = (i + 1) * B
        q = pl.ds(i * B, B)

        @pl.loop(0, 2)
        def _(h):
            probs = s.probs[h, pl.ds(first[i], n), :]
            dprob = nt(s.vm[h, pl.ds(0, n), :], s.do[q, :])
            inner = jnp.sum(probs * dprob, axis=0, keepdims=True)
            dscore = (probs * (dprob - inner)).astype(BF)
            s.dv[pl.ds(0, n), :] += nn(probs.astype(BF), s.dom[h, q, :])
            s.dk[pl.ds(0, n), :] += nn(dscore, s.qsm[h, q, :])
            hrows = rows(h, HD)
            s.dqt[hrows, q] = nn(s.kt[hrows, pl.ds(0, n)], dscore) * (1.0 / math.sqrt(HD))

        step(rm) if i in (0, 2) else None
        step(ro) if i == 1 else None

    @pl.loop(0, 4)
    def _(b):
        r = rows(b)
        cos, sin = ctab[r, :], -stab[r, :]
        dq = turn(s.dqt[:, r].T, cos, sin).astype(BF)
        dk = turn(s.dk[r, :], cos, sin).astype(BF)
        dv = s.dv[r, :].astype(BF)
        both = jnp.concatenate([dq, dk, dv], axis=1)
        s.qkvg[r, :] = both
        ecols3 = pl.ds(pl.multiple_of(row * 3 * E, 3 * E), 3 * E)
        s.vec[5:6, ecols3] += jnp.sum(both.astype(F32), axis=0, keepdims=True)

    @pl.loop(0, 4)
    def _(b):
        r = rows(b)
        attn = nt(s.qkvg[r, :], s.wq[...])
        mlp = nt(s.hpg[r, :], s.wu[...])
        normed = (s.xall[r, :].astype(F32) - s.mean[r, :]) * s.inv[r, :]
        s.ng[r, :] = (attn * gain0 + mlp * gain1).astype(BF)
        s.vec[0:1, :] += jnp.sum(attn * normed, axis=0, keepdims=True)
        s.vec[1:2, :] += jnp.sum(mlp * normed, axis=0, keepdims=True)
        s.vec[2:3, :] += jnp.sum(attn, axis=0, keepdims=True)
        s.vec[3:4, :] += jnp.sum(mlp, axis=0, keepdims=True)

    rn = ring_scatter(
        net, npart, (s.nta, s.ntb, s.ninl, s.ninr), col, at["z1"], at["z3"], B, half
    )
    step(rn)

    @pl.loop(0, 3)
    def _(b):
        r = rows(b, E)
        r2 = pl.ds(pl.multiple_of(E + b * E, E), E)
        s.ga[r2, :] = tn(s.qkvg[:, r], s.ain[...]).astype(BF)

    ra = reduce_weights(net, s.ga, sa, at, where, 4 * E)
    step(ra)
    rv = reduce_vectors(net, s, at)
    step(rv)
    finish(ro)

    def summed(part, inl, inr, h):
        cols = pl.ds(h * half, half)
        return (
            part(col, cols)[...].astype(F32) + inl[:, cols].astype(F32) + inr[:, cols].astype(F32)
        )

    for h in range(2):
        s.ysend[h] = summed(opart, s.oinl, s.oinr, h).astype(BF)
    yo = net.go(s.ysend.at[1 - row], s.yrecv.at[0], y1)
    step(rv)
    step(ra)
    step(rm)
    step(rn)
    yo.wait_recv()
    out[...] = (
        tok[...].astype(F32)
        + s.ysend[row].astype(F32)
        + s.yrecv[0].astype(F32)
        + small[4:5, pl.ds(0, half)]
        + small[5:6, pl.ds(0, half)]
    ).astype(BF)
    step(rv)
    step(ra)
    step(rv)
    step(ra)
    finish(rn)
    r = rows(col)
    mean, inv = s.mean[r, :], s.inv[r, :]
    first_sum = jnp.zeros((B, 1), F32)
    second_sum = jnp.zeros((B, 1), F32)
    for h in range(2):
        total = summed(npart, s.ninl, s.ninr, h)
        normed = (s.xall[r, pl.ds(h * half, half)].astype(F32) - mean) * inv
        first_sum += jnp.sum(total, axis=1, keepdims=True)
        second_sum += jnp.sum(total * normed, axis=1, keepdims=True)
        npart(col, pl.ds(h * half, half))[...] = total.astype(BF)
    lane = lax.broadcasted_iota(jnp.int32, (B, 128), 1)
    s.ssend[...] = jnp.where(lane < 64, first_sum, second_sum)
    rhalf = pl.ds(pl.multiple_of(row * half, half), half)
    ohalf = pl.ds(pl.multiple_of((1 - row) * half, half), half)
    yn = net.go(npart(col, ohalf), s.yrecv.at[1], y1)
    ys = net.go(s.ssend, s.srecv, y1)
    interleave(rv, ra, rm)
    vout[0] = s.vs[2]
    vout[1] = s.vs[3]
    yn.wait_recv()
    ys.wait_recv()
    sums = (s.ssend[...] + s.srecv[...]) * (1.0 / D)
    normed = (tok[...].astype(F32) - mean) * inv
    total = npart(col, rhalf)[...].astype(F32) + s.yrecv[1].astype(F32)
    tgrad[...] = (
        cot[...].astype(F32) + inv * (total - sums[:, 0:1] - normed * sums[:, 64:65])
    ).astype(BF)
    for copy in net.sent:
        copy.wait_send()


def tables():
    freq = np.arange(ROT // 2, dtype=np.float32)
    inverse = np.float32(10000.0) ** (np.float32(-2.0) * freq / np.float32(ROT))
    angle = np.arange(T, dtype=np.float32)[:, None] * inverse[None, :].astype(np.float32)
    cos, sin = np.cos(angle), np.sin(angle)
    ones, zeros = np.ones((T, HD - ROT), np.float32), np.zeros((T, HD - ROT), np.float32)
    ctab = np.concatenate([cos, cos, ones] * 2, axis=1)
    stab = np.concatenate([-sin, sin, zeros] * 2, axis=1)
    return ctab.astype(np.float32), stab.astype(np.float32)


def on_device(
    tokens, segment_ids, w_qkv, b_qkv, w_out, b_out, w_up, b_up, w_down, b_down, norm_gain, norm_bias, cotangent
):
    def line(values):
        values = values.astype(F32).reshape(-1, values.shape[-1])
        return jnp.pad(values, ((0, 0), (0, D - values.shape[1])))

    small = jnp.concatenate(
        [line(v) for v in (b_qkv, b_up, b_out, b_down)]
        + [jnp.zeros((2, D), F32), line(norm_gain), line(norm_bias), jnp.zeros((4, D), F32)]
    )
    ctab, stab = tables()
    vmem = pl.BlockSpec(memory_space=pltpu.VMEM)
    hbm = pl.BlockSpec(memory_space=pl.ANY)
    shape = jax.ShapeDtypeStruct
    out, tgrad, fm, fa, vec = pl.pallas_call(
        body,
        out_shape=[
            shape((B, D // 2), BF),
            shape((B, D // 2), BF),
            shape((2, 4, 2, F // 4, D // 2), BF),
            shape((2, 4, 2, E // 2, D // 2), BF),
            shape((2, 8, D), F32),
        ],
        in_specs=[vmem, vmem, hbm, hbm, hbm, hbm, vmem, vmem, vmem, vmem, vmem],
        out_specs=[vmem] * 5,
        scratch_shapes=[pltpu.VMEM(*spec) for spec in SCRATCH.values()]
        + [pltpu.SemaphoreType.DMA((NSEM,)), pltpu.SemaphoreType.DMA((NSEM,))],
        compiler_params=pltpu.CompilerParams(
            collective_id=0, has_side_effects=True, vmem_limit_bytes=60 * 1024 * 1024
        ),
        name="block",
    )(
        tokens, cotangent, w_qkv, w_out, w_up, w_down, small,
        segment_ids.reshape(T, 1), segment_ids.reshape(1, T), jnp.asarray(ctab), jnp.asarray(stab),
    )
    row = lax.axis_index("row")
    fm = fm.astype(F32)
    w_down_grad = fm[0].transpose(1, 0, 2, 3).reshape(2 * F, D // 2)
    w_up_grad = fm[1].transpose(3, 1, 0, 2).reshape(D // 2, 2 * F)
    fa = fa.astype(F32).reshape(4, 2, 2, E // 2, D // 2)
    w_out_grad = fa[0].transpose(1, 0, 2, 3).reshape(2 * E, D // 2)
    w_qkv_grad = fa[1:].transpose(0, 4, 2, 1, 3).reshape(3, D // 2, 2 * E)
    rhalf = lambda v: lax.dynamic_slice_in_dim(v, row * (D // 2), D // 2, axis=-1)
    b_out_grad = rhalf(vec[0, 4])
    b_qkv_grad = vec[0, 5, : 6 * E].reshape(2, 3, E).transpose(1, 0, 2).reshape(3, 2 * E)
    b_up_grad = vec[0, 6]
    gain_grad = rhalf(vec[1, 0:2])
    bias_grad = rhalf(vec[1, 2:4])
    return (
        out, tgrad, w_qkv_grad, b_qkv_grad, w_out_grad, b_out_grad,
        w_up_grad, b_up_grad, w_down_grad, b_out_grad, gain_grad, bias_grad,
    )


def solution(mesh):
    in_specs = (
        P(("dp", "col"), "row"),
        P("dp"),
        P(None, "row", "col"),
        P(None, "col"),
        P("col", "row"),
        P("row"),
        P("row", "col"),
        P("col"),
        P("col", "row"),
        P("row"),
        P(None, "row"),
        P(None, "row"),
        P(("dp", "col"), "row"),
    )
    out_specs = (
        P(("dp", "col"), "row"),
        P(("dp", "col"), "row"),
        P(None, "row", "col"),
        P(None, "col"),
        P("col", "row"),
        P("row"),
        P("row", "col"),
        P("col"),
        P("col", "row"),
        P("row"),
        P(None, "row"),
        P(None, "row"),
    )
    return jax.shard_map(
        on_device, mesh=mesh, in_specs=in_specs, out_specs=out_specs, check_vma=False
    )
```

```python
from types import SimpleNamespace
import math

import numpy as np
import jax
import jax.numpy as jnp
from jax import lax
from jax.experimental import pallas as pl
from jax.experimental.pallas import tpu as pltpu
from jax.sharding import PartitionSpec as P

MESH = pl.DeviceIdType.MESH
BF = jnp.bfloat16
F32 = jnp.float32
T = 1024
D = 1024
HD = 64
ROT = 16
E = 128
F = 512
B = 256
EPSILON = 1e-05
NSEM = 128


def nn(a, b):
    return jnp.dot(a, b, preferred_element_type=F32)


def nt(a, b):
    return lax.dot_general(a, b, (((1,), (1,)), ((), ())), preferred_element_type=F32)


def tn(a, b):
    return lax.dot_general(a, b, (((0,), (0,)), ((), ())), preferred_element_type=F32)


def rows(block, size=B):
    return pl.ds(pl.multiple_of(block * size, size), size)


class Net:
    def __init__(self, send, recv):
        self.send, self.recv, self.count, self.sent = send, recv, 0, []

    def go(self, src, dst, device):
        k = self.count
        self.count += 1
        assert k < NSEM
        copy = pltpu.make_async_remote_copy(
            src_ref=src,
            dst_ref=dst,
            send_sem=self.send.at[k],
            recv_sem=self.recv.at[k],
            device_id=device,
            device_id_type=MESH,
        )
        copy.start()
        self.sent.append(copy)
        return copy

    def local(self, src, dst):
        k = self.count
        self.count += 1
        assert k < NSEM
        copy = pltpu.make_async_copy(src, dst, self.send.at[k])
        copy.start()
        return copy


def gather_tokens(net, own, full, at, half, col, row):
    right, left, peer = at["z1"], at["z3"], at["y1"]

    def place(c, h):
        return full.at[rows(c), pl.ds(pl.multiple_of(h * half, half), half)]

    mine, other = place(col, row), place(col, 1 - row)
    lcol, rcol = lax.rem(col + 3, 4), lax.rem(col + 1, 4)
    c0 = net.go(own, mine, peer)
    keep = net.local(own, mine)
    yield
    c1 = net.go(own, mine, right)
    c2 = net.go(own, mine, left)
    yield
    keep.wait()
    c0.wait_recv()
    c3 = net.go(other, other, right)
    c4 = net.go(other, other, left)
    yield
    c1.wait_recv()
    c5 = net.go(place(lcol, row), place(lcol, row), right)
    yield
    c4.wait_recv()
    c6 = net.go(place(rcol, 1 - row), place(rcol, 1 - row), left)
    yield
    c2.wait_recv()
    c3.wait_recv()
    yield
    c5.wait_recv()
    c6.wait_recv()


def gather_weights(net, wqkv, wup, wout, wdown, s, at, core, row):
    half, part = D // 2, D // 4
    mine, theirs = row, 1 - row
    drows = rows(row, half)

    def cut(which, size):
        return pl.ds(pl.multiple_of(which * size, size), size)

    local = []
    for k in range(3):
        kcols = pl.ds(k * E, E)
        local.append(net.local(wqkv.at[k, :, cut(mine, E)], s.wq.at[drows, kcols]))
    local.append(net.local(wup.at[:, cut(mine, F)], s.wu.at[drows]))
    local.append(net.local(wout.at[cut(mine, E)], s.wo.at[:, drows]))
    local.append(net.local(wdown.at[cut(mine, F)], s.wd.at[:, drows]))
    src = cut(core, part)
    dst = cut(row * 2 + core, part)
    got = cut((1 - row) * 2 + core, part)
    ocols = rows(1 - row, half)
    far, near = at["y3"], at["core"]
    q = [
        net.go(wqkv.at[k, src, cut(theirs, E)], s.wq.at[dst, pl.ds(k * E, E)], far)
        for k in range(3)
    ]
    u = net.go(wup.at[src, cut(theirs, F)], s.wu.at[dst], far)
    o = net.go(wout.at[cut(theirs * 2 + core, E // 2)], s.wo.at[cut(core, E // 2), drows], far)
    d = net.go(wdown.at[cut(theirs * 2 + core, F // 2)], s.wd.at[cut(core, F // 2), drows], far)
    yield
    for copy in q:
        copy.wait_recv()
    q2 = net.go(s.wq.at[got], s.wq.at[got], near)
    yield
    u.wait_recv()
    u2 = net.go(s.wu.at[got], s.wu.at[got], near)
    yield
    q2.wait_recv()
    for copy in local[:3]:
        copy.wait()
    yield
    u2.wait_recv()
    local[3].wait()
    yield
    o.wait_recv()
    ov = s.wo.at[cut(core, E // 2), ocols]
    o2 = net.go(ov, ov, near)
    d.wait_recv()
    dv = s.wd.at[cut(core, F // 2), ocols]
    d2 = net.go(dv, dv, near)
    yield
    local[4].wait()
    local[5].wait()
    o2.wait_recv()
    d2.wait_recv()


def ring_scatter(net, part, bufs, me, right, left, size, width):
    ta, tb, inl, inr = bufs
    lo, hi = pl.ds(0, width), pl.ds(width, width)
    far, rb, lb = lax.rem(me + 2, 4), lax.rem(me + 1, 4), lax.rem(me + 3, 4)
    a = net.go(part(far, lo), ta, right)
    b = net.go(part(far, hi), tb, left)
    c = net.go(part(rb, hi), inl.at[:, hi], right)
    d = net.go(part(lb, lo), inr.at[:, lo], left)
    yield
    a.wait_recv()
    view = part(rb, lo)
    view[...] = (view[...].astype(F32) + ta[...].astype(F32)).astype(BF)
    e = net.go(view, inl.at[:, lo], right)
    b.wait_recv()
    view = part(lb, hi)
    view[...] = (view[...].astype(F32) + tb[...].astype(F32)).astype(BF)
    f = net.go(view, inr.at[:, hi], left)
    yield
    for copy in (c, d, e, f):
        copy.wait_recv()


def reduce_weights(net, grad, s, at, me, n):
    core, x, row = me["core"], me["x"], me["row"]
    half, size = n // 2, n // 8
    base = core * half
    away = (1 - core) * half
    c = net.go(grad.at[pl.ds(pl.multiple_of(away, half), half)], s.rc, at["core"])
    yield
    c.wait_recv()
    own = grad.at[pl.ds(pl.multiple_of(base, half), half)]
    own[...] = (own[...].astype(F32) + s.rc[...].astype(F32)).astype(BF)

    def part(block, cols):
        return grad.at[pl.ds(pl.multiple_of(base + block * size, size), size), cols]

    yield from ring_scatter(
        net, part, (s.ta, s.tb, s.inl, s.inr), x, at["x1"], at["x3"], size, D // 2
    )
    for h in range(2):
        cols = pl.ds(h * (D // 2), D // 2)
        total = (
            part(x, cols)[...].astype(F32) + s.inl[:, cols].astype(F32) + s.inr[:, cols].astype(F32)
        )
        s.sy[h] = total.astype(BF)
    g0 = net.go(s.sy.at[row], s.ry.at[0], at["y2"])
    g1 = net.go(s.sy.at[1 - row], s.ry.at[1], at["y1"])
    g2 = net.go(s.sy.at[1 - row], s.ry.at[2], at["y3"])
    yield
    g0.wait_recv()
    s.fin[core, x, row] = (s.sy[row].astype(F32) + s.ry[0].astype(F32)).astype(BF)
    g1.wait_recv()
    g2.wait_recv()
    s.fin[core, x, 1 - row] = (s.ry[1].astype(F32) + s.ry[2].astype(F32)).astype(BF)
    h0 = s.fin.at[core, x, 0]
    h1 = s.fin.at[core, x, 1]
    a0 = net.go(h0, h0, at["x1"])
    a1 = net.go(h1, h1, at["x3"])
    a2 = net.go(h1, h1, at["x1"])
    a3 = net.go(h0, h0, at["x3"])
    k0 = net.go(s.fin.at[core, x], s.fin.at[core, x], at["core"])
    yield
    lx, rx = lax.rem(x + 3, 4), lax.rem(x + 1, 4)
    a0.wait_recv()
    v = s.fin.at[core, lx, 0]
    a4 = net.go(v, v, at["x1"])
    a1.wait_recv()
    v = s.fin.at[core, rx, 1]
    a5 = net.go(v, v, at["x3"])
    a2.wait_recv()
    v = s.fin.at[core, lx]
    k1 = net.go(v, v, at["core"])
    a3.wait_recv()
    v = s.fin.at[core, rx]
    k2 = net.go(v, v, at["core"])
    yield
    a4.wait_recv()
    a5.wait_recv()
    v = s.fin.at[core, lax.rem(x + 2, 4)]
    k3 = net.go(v, v, at["core"])
    for copy in (k0, k1, k2):
        copy.wait_recv()
    yield
    k3.wait_recv()


def reduce_vectors(net, s, at):
    c = net.go(s.vec, s.vr.at[0], at["core"])
    yield
    c.wait_recv()
    s.vs[0] = s.vec[...] + s.vr[0]
    for n, axis in enumerate("xyz"):
        copies = [net.go(s.vs.at[n], s.vr.at[3 * n + k], at[axis + str(k)]) for k in (1, 2, 3)]
        yield
        for copy in copies:
            copy.wait_recv()
        s.vs[n + 1] = (s.vs[n] + s.vr[3 * n + 1]) + (s.vr[3 * n + 2] + s.vr[3 * n + 3])


def step(gen):
    next(gen, None)


def finish(gen):
    for _ in gen:
        pass


def interleave(*gens):
    live = list(gens)
    while live:
        for gen in list(live):
            try:
                next(gen)
            except StopIteration:
                live.remove(gen)


def turn(values, cos, sin):
    lane = lax.broadcasted_iota(jnp.int32, values.shape, 1)
    other = jnp.where(lane % HD < ROT // 2, pltpu.roll(values, E - ROT // 2, 1), pltpu.roll(values, ROT // 2, 1))
    return values * cos + other * sin


def split_heads(ref, at_rows, values):
    lane = lax.broadcasted_iota(jnp.int32, values.shape, 1)
    zero = jnp.zeros_like(values)
    ref[0, at_rows, :] = jnp.where(lane < HD, values, zero).astype(BF)
    ref[1, at_rows, :] = jnp.where(lane < HD, zero, values).astype(BF)


SCRATCH = dict(
    xall=((T, D), BF),
    gall=((T, D), BF),
    ain=((T, D), BF),
    mim=((T, D), BF),
    wq=((D, 3 * E), BF),
    wo=((E, D), BF),
    wu=((D, F), BF),
    wd=((F, D), BF),
    nb=((2, 8, D // 2), F32),
    mean=((T, 1), F32),
    inv=((T, 1), F32),
    hid=((T, F), BF),
    slope=((T, F), F32),
    segc=((T, 8), F32),
    nbs=((8, D // 2), F32),
    hpg=((T, F), BF),
    qs=((T, E), BF),
    qsm=((2, T, E), BF),
    km=((2, T, E), BF),
    vm=((2, T, E), BF),
    kt=((E, T), BF),
    vt=((E, T), BF),
    do=((T, E), BF),
    dom=((2, T, E), BF),
    probs=((2, 2560, B), F32),
    mt=((E, T), BF),
    mixed=((T, E), BF),
    dqt=((E, T), F32),
    dk=((T, E), F32),
    dv=((T, E), F32),
    qkvg=((T, 3 * E), BF),
    op=((T, D), BF),
    ng=((T, D), BF),
    ota=((B, D // 2), BF),
    otb=((B, D // 2), BF),
    oinl=((B, D), BF),
    oinr=((B, D), BF),
    nta=((B, D // 2), BF),
    ntb=((B, D // 2), BF),
    ninl=((B, D), BF),
    ninr=((B, D), BF),
    ysend=((2, B, D // 2), BF),
    yrecv=((2, B, D // 2), BF),
    ssend=((B, 128), F32),
    srecv=((B, 128), F32),
    gm=((2 * F, D), BF),
    ga=((4 * E, D), BF),
    mrc=((F, D), BF),
    mta=((F // 4, D // 2), BF),
    mtb=((F // 4, D // 2), BF),
    minl=((F // 4, D), BF),
    minr=((F // 4, D), BF),
    msy=((2, F // 4, D // 2), BF),
    mry=((3, F // 4, D // 2), BF),
    arc=((2 * E, D), BF),
    ata=((E // 2, D // 2), BF),
    atb=((E // 2, D // 2), BF),
    ainl=((E // 2, D), BF),
    ainr=((E // 2, D), BF),
    asy=((2, E // 2, D // 2), BF),
    ary=((3, E // 2, D // 2), BF),
    vec=((8, D), F32),
    vr=((10, 8, D), F32),
    vs=((4, 8, D), F32),
)


def body(
    tok, cot, wqkv, wout, wup, wdown, bqkv, bup, bout, bdown, gain, bias, seg, ctab, stab,
    out, tgrad, fm, fa, vout, *scratch,
):
    s = SimpleNamespace(**dict(zip(SCRATCH, scratch)))
    send, recv = scratch[len(SCRATCH) :]
    net = Net(send, recv)
    dp, row, col = lax.axis_index("dp"), lax.axis_index("row"), lax.axis_index("col")
    core, x, yh = lax.rem(dp, 2), lax.rem(dp // 2, 4), dp // 8
    half = D // 2

    def dev(core=core, x=x, yh=yh, row=row, col=col):
        return (yh * 8 + x * 2 + core, row, col)

    at = {"core": dev(core=1 - core)}
    for k in (1, 2, 3):
        at[f"x{k}"] = dev(x=lax.rem(x + k, 4))
        at[f"z{k}"] = dev(col=lax.rem(col + k, 4))
    at["y1"] = dev(row=1 - row)
    at["y2"] = dev(yh=1 - yh)
    at["y3"] = dev(yh=1 - yh, row=1 - row)
    y1 = at["y1"]

    s.nbs[...] = jnp.concatenate(
        [gain[...].astype(F32), bias[...].astype(F32), jnp.zeros((4, half), F32)]
    )
    barrier = pltpu.get_barrier_semaphore()
    for device in at.values():
        pl.semaphore_signal(barrier, inc=1, device_id=device, device_id_type=MESH)
    pl.semaphore_wait(barrier, len(at))

    gx = gather_tokens(net, tok, s.xall, at, half, col, row)
    gg = gather_tokens(net, cot, s.gall, at, half, col, row)
    gw = gather_weights(net, wqkv, wup, wout, wdown, s, at, core, row)
    nbc = net.go(s.nbs, s.nb.at[row], y1)
    step(gx)
    step(gx)
    step(gw)
    s.nb[row] = s.nbs[...]
    s.vec[...] = jnp.zeros_like(s.vec)
    s.dk[...] = jnp.zeros_like(s.dk)
    s.dv[...] = jnp.zeros_like(s.dv)

    def flat(values):
        values = values.astype(F32)
        return jnp.concatenate([values[k : k + 1, :] for k in range(values.shape[0])], axis=1)

    segr = flat(seg[...])
    s.segc[...] = jnp.broadcast_to(segr, (8, T)).T
    bq_all = bqkv[...].astype(F32)
    mine = row == 0
    bq = jnp.concatenate(
        [jnp.where(mine, bq_all[k : k + 1, :E], bq_all[k : k + 1, E:]) for k in range(3)], axis=1
    )
    bu_all = flat(bup[...])
    bu = jnp.where(mine, bu_all[:, :F], bu_all[:, F:])
    fcols = pl.ds(pl.multiple_of(row * F, F), F)
    gcols = pl.ds(pl.multiple_of(row * half, half), half)

    nbc.wait_recv()

    def wide(k):
        return jnp.concatenate([s.nb[0, k : k + 1, :], s.nb[1, k : k + 1, :]], axis=1)

    gain0, gain1, bias0, bias1 = wide(0), wide(1), wide(2), wide(3)

    def norm(c):
        @pl.loop(0, 2)
        def _(b):
            r = rows(c * 2 + b, 128)
            xv = s.xall[r, :].astype(F32)
            mean = jnp.sum(xv, axis=1, keepdims=True) * (1.0 / D)
            square = jnp.sum(xv * xv, axis=1, keepdims=True) * (1.0 / D)
            inv = lax.rsqrt(square - mean * mean + EPSILON)
            normed = (xv - mean) * inv
            s.mean[r, :] = mean
            s.inv[r, :] = inv
            s.ain[r, :] = (normed * gain0 + bias0).astype(BF)
            s.mim[r, :] = (normed * gain1 + bias1).astype(BF)

    def project(c):
        r = rows(c)
        pre = nn(s.ain[r, :], s.wq[...]) + bq
        cos, sin = ctab[r, :], stab[r, :]
        query = (turn(pre[:, :E], cos, sin)).astype(BF).astype(F32) * (1.0 / math.sqrt(HD))
        key = turn(pre[:, E : 2 * E], cos, sin).astype(BF).astype(F32)
        value = pre[:, 2 * E :].astype(BF).astype(F32)
        s.qs[r, :] = query.astype(BF)
        split_heads(s.qsm, r, query)
        split_heads(s.km, r, key)
        split_heads(s.vm, r, value)
        s.kt[:, r] = key.T.astype(BF)
        s.vt[:, r] = value.T.astype(BF)

    def expand(c):
        r = rows(c)
        pre = nn(s.mim[r, :], s.wu[...]) + bu
        cdf = 0.5 * (1.0 + lax.erf(pre * math.sqrt(0.5)))
        s.hid[r, :] = (pre * cdf).astype(BF)
        s.slope[r, :] = cdf + pre * jnp.exp(-0.5 * pre * pre) * (1.0 / math.sqrt(2.0 * math.pi))

    def contract(c):
        r = rows(c)
        back = (nt(s.gall[r, :], s.wd[...]) * s.slope[r, :]).astype(BF)
        s.hpg[r, :] = back
        s.vec[6:7, fcols] += jnp.sum(back.astype(F32), axis=0, keepdims=True)
        s.vec[4:5, gcols] += jnp.sum(s.gall[r, gcols].astype(F32), axis=0, keepdims=True)
        dout = nt(s.gall[r, :], s.wo[...]).astype(BF).astype(F32)
        s.do[r, :] = dout.astype(BF)
        split_heads(s.dom, r, dout)

    rb, lb, fb = lax.rem(col + 1, 4), lax.rem(col + 3, 4), lax.rem(col + 2, 4)
    step(gx)
    step(gg)
    norm(col)
    step(gx)
    step(gw)
    step(gx)
    step(gx)
    step(gg)
    norm(lb)
    norm(rb)
    step(gw)
    step(gw)
    project(col)
    step(gg)
    project(lb)
    project(rb)
    step(gw)
    expand(col)
    expand(lb)
    expand(rb)
    step(gw)
    finish(gx)
    norm(fb)
    project(fb)
    expand(fb)

    first = [0, 256, 768, 1536]
    for i in range(4):
        n = (i + 1) * B
        q = pl.ds(i * B, B)

        @pl.loop(0, 2)
        def _(h):
            scores = nt(s.km[h, pl.ds(0, n), :], s.qs[q, :])
            kid = lax.broadcasted_iota(jnp.int32, (n, B), 0)
            qid = lax.broadcasted_iota(jnp.int32, (n, B), 1) + i * B
            allowed = (kid <= qid) & (s.segc[pl.ds(0, n), 0:1] == segr[:, i * B : (i + 1) * B])
            scores = jnp.where(allowed, scores, -1e30)
            top = jnp.max(scores, axis=0, keepdims=True)
            expo = jnp.exp(scores - top)
            probs = expo * (1.0 / jnp.sum(expo, axis=0, keepdims=True))
            s.probs[h, pl.ds(first[i], n), :] = probs
            hrows = rows(h, HD)
            s.mt[hrows, q] = nn(s.vt[hrows, pl.ds(0, n)], probs.astype(BF)).astype(BF)

        s.mixed[q, :] = s.mt[:, q].astype(F32).T.astype(BF)
        step(gg) if i in (1, 3) else None

    finish(gw)

    @pl.loop(0, 4)
    def _(b):
        r = rows(b)
        s.op[r, :] = (nn(s.mixed[r, :], s.wo[...]) + nn(s.hid[r, :], s.wd[...])).astype(BF)

    contract(col)
    step(gg)
    contract(lb)
    contract(rb)
    finish(gg)

    def opart(block, cols):
        return s.op.at[rows(block), cols]

    def npart(block, cols):
        return s.ng.at[rows(block), cols]

    ro = ring_scatter(
        net, opart, (s.ota, s.otb, s.oinl, s.oinr), col, at["z1"], at["z3"], B, half
    )
    step(ro)
    contract(fb)

    @pl.loop(0, 4)
    def _(b):
        r = rows(b, 128)
        s.gm[r, :] = tn(s.hid[:, r], s.gall[...]).astype(BF)
        r2 = pl.ds(pl.multiple_of(F + b * 128, 128), 128)
        s.gm[r2, :] = tn(s.hpg[:, r], s.mim[...]).astype(BF)

    sm = SimpleNamespace(
        rc=s.mrc, ta=s.mta, tb=s.mtb, inl=s.minl, inr=s.minr, sy=s.msy, ry=s.mry, fin=fm
    )
    sa = SimpleNamespace(
        rc=s.arc, ta=s.ata, tb=s.atb, inl=s.ainl, inr=s.ainr, sy=s.asy, ry=s.ary, fin=fa
    )
    where = dict(core=core, x=x, row=row)
    rm = reduce_weights(net, s.gm, sm, at, where, 2 * F)
    step(rm)

    s.ga[0:E, :] = nn(s.mt[...], s.gall[...]).astype(BF)

    for i in range(4):
        n = (i + 1) * B
        q = pl.ds(i * B, B)

        @pl.loop(0, 2)
        def _(h):
            probs = s.probs[h, pl.ds(first[i], n), :]
            dprob = nt(s.vm[h, pl.ds(0, n), :], s.do[q, :])
            inner = jnp.sum(probs * dprob, axis=0, keepdims=True)
            dscore = (probs * (dprob - inner)).astype(BF)
            s.dv[pl.ds(0, n), :] += nn(probs.astype(BF), s.dom[h, q, :])
            s.dk[pl.ds(0, n), :] += nn(dscore, s.qsm[h, q, :])
            hrows = rows(h, HD)
            s.dqt[hrows, q] = nn(s.kt[hrows, pl.ds(0, n)], dscore) * (1.0 / math.sqrt(HD))

        step(rm) if i == 0 else None
        step(ro) if i == 2 else None

    @pl.loop(0, 4)
    def _(b):
        r = rows(b)
        cos, sin = ctab[r, :], -stab[r, :]
        dq = turn(s.dqt[:, r].T, cos, sin).astype(BF)
        dk = turn(s.dk[r, :], cos, sin).astype(BF)
        dv = s.dv[r, :].astype(BF)
        both = jnp.concatenate([dq, dk, dv], axis=1)
        s.qkvg[r, :] = both
        ecols3 = pl.ds(pl.multiple_of(row * 3 * E, 3 * E), 3 * E)
        s.vec[5:6, ecols3] += jnp.sum(both.astype(F32), axis=0, keepdims=True)

    @pl.loop(0, 4)
    def _(b):
        r = rows(b)
        attn = nt(s.qkvg[r, :], s.wq[...])
        mlp = nt(s.hpg[r, :], s.wu[...])
        normed = (s.xall[r, :].astype(F32) - s.mean[r, :]) * s.inv[r, :]
        s.ng[r, :] = (attn * gain0 + mlp * gain1).astype(BF)
        s.vec[0:1, :] += jnp.sum(attn * normed, axis=0, keepdims=True)
        s.vec[1:2, :] += jnp.sum(mlp * normed, axis=0, keepdims=True)
        s.vec[2:3, :] += jnp.sum(attn, axis=0, keepdims=True)
        s.vec[3:4, :] += jnp.sum(mlp, axis=0, keepdims=True)

    step(rm)
    rn = ring_scatter(
        net, npart, (s.nta, s.ntb, s.ninl, s.ninr), col, at["z1"], at["z3"], B, half
    )
    step(rn)

    @pl.loop(0, 3)
    def _(b):
        r = rows(b, E)
        r2 = pl.ds(pl.multiple_of(E + b * E, E), E)
        s.ga[r2, :] = tn(s.qkvg[:, r], s.ain[...]).astype(BF)

    ra = reduce_weights(net, s.ga, sa, at, where, 4 * E)
    step(ra)
    rv = reduce_vectors(net, s, at)
    step(rv)
    step(rm)
    finish(ro)

    def summed(part, inl, inr, h):
        cols = pl.ds(h * half, half)
        return (
            part(col, cols)[...].astype(F32) + inl[:, cols].astype(F32) + inr[:, cols].astype(F32)
        )

    for h in range(2):
        s.ysend[h] = summed(opart, s.oinl, s.oinr, h).astype(BF)
    yo = net.go(s.ysend.at[1 - row], s.yrecv.at[0], y1)
    step(ra)
    step(rv)
    step(rn)
    step(rm)
    yo.wait_recv()
    out[...] = (
        tok[...].astype(F32)
        + s.ysend[row].astype(F32)
        + s.yrecv[0].astype(F32)
        + flat(bout[...])
        + flat(bdown[...])
    ).astype(BF)
    step(ra)
    step(rv)
    step(rm)
    step(ra)
    step(rv)
    finish(rn)
    r = rows(col)
    mean, inv = s.mean[r, :], s.inv[r, :]
    first_sum = jnp.zeros((B, 1), F32)
    second_sum = jnp.zeros((B, 1), F32)
    for h in range(2):
        total = summed(npart, s.ninl, s.ninr, h)
        normed = (s.xall[r, pl.ds(h * half, half)].astype(F32) - mean) * inv
        first_sum += jnp.sum(total, axis=1, keepdims=True)
        second_sum += jnp.sum(total * normed, axis=1, keepdims=True)
        npart(col, pl.ds(h * half, half))[...] = total.astype(BF)
    lane = lax.broadcasted_iota(jnp.int32, (B, 128), 1)
    s.ssend[...] = jnp.where(lane < 64, first_sum, second_sum)
    ohalf = pl.ds(pl.multiple_of((1 - row) * half, half), half)
    yn = net.go(npart(col, ohalf), s.yrecv.at[1], y1)
    ys = net.go(s.ssend, s.srecv, y1)
    interleave(rv, ra, rm)
    vout[0] = s.vs[2]
    vout[1] = s.vs[3]
    yn.wait_recv()
    ys.wait_recv()
    sums = (s.ssend[...] + s.srecv[...]) * (1.0 / D)
    normed = (tok[...].astype(F32) - mean) * inv
    total = npart(col, gcols)[...].astype(F32) + s.yrecv[1].astype(F32)
    tgrad[...] = (
        cot[...].astype(F32) + inv * (total - sums[:, 0:1] - normed * sums[:, 64:65])
    ).astype(BF)
    for copy in net.sent:
        copy.wait_send()


def tables():
    freq = np.arange(ROT // 2, dtype=np.float32)
    inverse = np.float32(10000.0) ** (np.float32(-2.0) * freq / np.float32(ROT))
    angle = np.arange(T, dtype=np.float32)[:, None] * inverse[None, :].astype(np.float32)
    cos, sin = np.cos(angle), np.sin(angle)
    ones, zeros = np.ones((T, HD - ROT), np.float32), np.zeros((T, HD - ROT), np.float32)
    ctab = np.concatenate([cos, cos, ones] * 2, axis=1)
    stab = np.concatenate([-sin, sin, zeros] * 2, axis=1)
    return ctab.astype(np.float32), stab.astype(np.float32)


def last(
    fm, fa, vec, out, tgrad,
    out_o, tgrad_o, wq_o, bq_o, wo_o, bo_o, wu_o, bu_o, wd_o, bd_o, gain_o, bias_o,
    wq, wo, wu, wd, sems,
):
    row = lax.axis_index("row")
    copies = []

    def write(src, dst):
        copy = pltpu.make_async_copy(src, dst, sems.at[len(copies)])
        copy.start()
        copies.append(copy)

    write(out, out_o)
    write(tgrad, tgrad_o)
    for r in range(2):
        for x in range(4):
            at = r * F + x * (F // 4)
            wd[pl.ds(at, F // 4), :] = fm[0, x, r].astype(F32)
        write(wd.at[pl.ds(r * F, F)], wd_o.at[pl.ds(r * F, F)])
    for r in range(2):
        for x in range(4):
            at = r * F + x * (F // 4)
            wu[:, pl.ds(at, F // 4)] = fm[1, x, r].astype(F32).T
        write(wu.at[:, pl.ds(r * F, F)], wu_o.at[:, pl.ds(r * F, F)])
    for r in range(2):
        for p in range(2):
            wo[pl.ds(r * E + p * (E // 2), E // 2), :] = fa[0, p, r].astype(F32)
    write(wo, wo_o)
    for k in range(3):
        for r in range(2):
            a = fa[(k + 1) // 2, 2 * ((k + 1) % 2), r].astype(F32)
            b = fa[(k + 1) // 2, 2 * ((k + 1) % 2) + 1, r].astype(F32)
            wq[k, :, pl.ds(r * E, E)] = jnp.concatenate([a, b], axis=0).T
        write(wq.at[k], wq_o.at[k])
    half = D // 2
    left = row == 0

    def cut(values):
        return jnp.where(left, values[:, :half], values[:, half:])

    bo_o[...] = cut(vec[0, 4:5, :])
    bd_o[...] = cut(vec[0, 4:5, :])
    for k in range(3):
        bq_o[k : k + 1, :E] = vec[0, 5:6, k * E : (k + 1) * E]
        bq_o[k : k + 1, E:] = vec[0, 5:6, (k + 3) * E : (k + 4) * E]
    bu_o[...] = vec[0, 6:7, :]
    gain_o[...] = cut(vec[1, 0:2, :])
    bias_o[...] = cut(vec[1, 2:4, :])
    for copy in copies:
        copy.wait()


def on_device(
    tokens, segment_ids, w_qkv, b_qkv, w_out, b_out, w_up, b_up, w_down, b_down, norm_gain, norm_bias, cotangent
):
    ctab, stab = tables()
    vmem = pl.BlockSpec(memory_space=pltpu.VMEM)
    hbm = pl.BlockSpec(memory_space=pl.ANY)
    shape = jax.ShapeDtypeStruct
    out, tgrad, fm, fa, vec = pl.pallas_call(
        body,
        out_shape=[
            shape((B, D // 2), BF),
            shape((B, D // 2), BF),
            shape((2, 4, 2, F // 4, D // 2), BF),
            shape((2, 4, 2, E // 2, D // 2), BF),
            shape((2, 8, D), F32),
        ],
        in_specs=[vmem, vmem, hbm, hbm, hbm, hbm] + [vmem] * 9,
        out_specs=[vmem] * 5,
        scratch_shapes=[pltpu.VMEM(*spec) for spec in SCRATCH.values()]
        + [pltpu.SemaphoreType.DMA((NSEM,)), pltpu.SemaphoreType.DMA((NSEM,))],
        compiler_params=pltpu.CompilerParams(
            collective_id=0, has_side_effects=True, vmem_limit_bytes=60 * 1024 * 1024
        ),
        name="block",
    )(
        tokens, cotangent, w_qkv, w_out, w_up, w_down, b_qkv, b_up.reshape(8, 128),
        b_out.reshape(4, 128), b_down.reshape(4, 128), norm_gain, norm_bias,
        segment_ids.reshape(8, 128), jnp.asarray(ctab), jnp.asarray(stab),
    )
    big = [
        ((3, D // 2, 2 * E), F32),
        ((2 * E, D // 2), F32),
        ((D // 2, 2 * F), F32),
        ((2 * F, D // 2), F32),
    ]
    results = pl.pallas_call(
        last,
        out_shape=[
            shape((B, D // 2), BF),
            shape((B, D // 2), BF),
            shape(*big[0]),
            shape((3, 2 * E), F32),
            shape(*big[1]),
            shape((1, D // 2), F32),
            shape(*big[2]),
            shape((1, 2 * F), F32),
            shape(*big[3]),
            shape((1, D // 2), F32),
            shape((2, D // 2), F32),
            shape((2, D // 2), F32),
        ],
        in_specs=[vmem] * 5,
        out_specs=[hbm, hbm, hbm, vmem, hbm, vmem, hbm, vmem, hbm, vmem, vmem, vmem],
        scratch_shapes=[pltpu.VMEM(*spec) for spec in big] + [pltpu.SemaphoreType.DMA((12,))],
        compiler_params=pltpu.CompilerParams(vmem_limit_bytes=40 * 1024 * 1024),
        name="last",
    )(fm, fa, vec, out, tgrad)
    out, tgrad, wq, bq, wo, bo, wu, bu, wd, bd, gain, bias = results
    bo, bu, bd = bo.reshape(-1), bu.reshape(-1), bd.reshape(-1)
    return (out, tgrad, wq, bq, wo, bo, wu, bu, wd, bd, gain, bias)


def solution(mesh):
    in_specs = (
        P(("dp", "col"), "row"),
        P("dp"),
        P(None, "row", "col"),
        P(None, "col"),
        P("col", "row"),
        P("row"),
        P("row", "col"),
        P("col"),
        P("col", "row"),
        P("row"),
        P(None, "row"),
        P(None, "row"),
        P(("dp", "col"), "row"),
    )
    out_specs = (
        P(("dp", "col"), "row"),
        P(("dp", "col"), "row"),
        P(None, "row", "col"),
        P(None, "col"),
        P("col", "row"),
        P("row"),
        P("row", "col"),
        P("col"),
        P("col", "row"),
        P("row"),
        P(None, "row"),
        P(None, "row"),
    )
    return jax.shard_map(
        on_device, mesh=mesh, in_specs=in_specs, out_specs=out_specs, check_vma=False
    )
```

```python
from types import SimpleNamespace
import math

import numpy as np
import jax
import jax.numpy as jnp
from jax import lax
from jax.experimental import pallas as pl
from jax.experimental.pallas import tpu as pltpu
from jax.sharding import PartitionSpec as P

MESH = pl.DeviceIdType.MESH
BF = jnp.bfloat16
F32 = jnp.float32
T = 1024
D = 1024
HD = 64
ROT = 16
E = 128
F = 512
B = 256
EPSILON = 1e-05
NSEM = 200
YR = 144
ZR = B - YR


def nn(a, b):
    return jnp.dot(a, b, preferred_element_type=F32)


def nt(a, b):
    return lax.dot_general(a, b, (((1,), (1,)), ((), ())), preferred_element_type=F32)


def tn(a, b):
    return lax.dot_general(a, b, (((0,), (0,)), ((), ())), preferred_element_type=F32)


def rows(block, size=B):
    return pl.ds(pl.multiple_of(block * size, size), size)


class Net:
    def __init__(self, send, recv):
        self.send, self.recv, self.count, self.sent = send, recv, 0, []

    def go(self, src, dst, device):
        k = self.count
        self.count += 1
        assert k < NSEM
        copy = pltpu.make_async_remote_copy(
            src_ref=src,
            dst_ref=dst,
            send_sem=self.send.at[k],
            recv_sem=self.recv.at[k],
            device_id=device,
            device_id_type=MESH,
        )
        copy.start()
        self.sent.append(copy)
        return copy

    def local(self, src, dst):
        k = self.count
        self.count += 1
        assert k < NSEM
        copy = pltpu.make_async_copy(src, dst, self.send.at[k])
        copy.start()
        return copy


def gather_tokens(net, own, full, at, half, col, row):
    right, left, peer = at["z1"], at["z3"], at["y1"]
    cut = YR + 48

    def place(c, h, start=0, size=B):
        r = pl.ds(pl.multiple_of(c * B + start, 16), size)
        return full.at[r, pl.ds(pl.multiple_of(h * half, half), half)]

    def move(device, *where):
        return net.go(place(*where), place(*where), device)

    mine = place(col, row)
    lcol, rcol, fcol = lax.rem(col + 3, 4), lax.rem(col + 1, 4), lax.rem(col + 2, 4)
    c0 = net.go(own, mine, peer)
    c1 = net.go(own, mine, right)
    c2 = net.go(own, mine, left)
    keep = net.local(own, mine)
    yield
    keep.wait()
    c0.wait_recv()
    c3 = move(right, col, 1 - row, 0, YR)
    c4 = move(left, col, 1 - row, 0, YR)
    yield
    c1.wait_recv()
    c5 = move(right, lcol, row, 0, cut)
    e5 = move(peer, lcol, row, YR, ZR)
    c2.wait_recv()
    d4 = move(left, rcol, row, cut, B - cut)
    e6 = move(peer, rcol, row, YR, ZR)
    yield
    c4.wait_recv()
    c6 = move(left, rcol, 1 - row, 0, YR)
    c3.wait_recv()
    yield
    e5.wait_recv()
    e6.wait_recv()
    yield
    c5.wait_recv()
    d4.wait_recv()
    e7 = move(peer, fcol, row, YR, ZR)
    yield
    c6.wait_recv()
    e7.wait_recv()


def gather_weights(net, wqkv, wup, wout, wdown, s, at, core, row):
    half, part = D // 2, D // 4
    mine, theirs = row, 1 - row
    drows = rows(row, half)

    def cut(which, size):
        return pl.ds(pl.multiple_of(which * size, size), size)

    local = []
    for k in range(3):
        kcols = pl.ds(k * E, E)
        local.append(net.local(wqkv.at[k, :, cut(mine, E)], s.wq.at[drows, kcols]))
    local.append(net.local(wup.at[:, cut(mine, F)], s.wu.at[drows]))
    local.append(net.local(wout.at[cut(mine, E)], s.wo.at[:, drows]))
    local.append(net.local(wdown.at[cut(mine, F)], s.wd.at[:, drows]))
    src = cut(core, part)
    dst = cut(row * 2 + core, part)
    got = cut((1 - row) * 2 + core, part)
    ocols = rows(1 - row, half)
    far, near = at["y3"], at["core"]
    q = [
        net.go(wqkv.at[k, src, cut(theirs, E)], s.wq.at[dst, pl.ds(k * E, E)], far)
        for k in range(3)
    ]
    u = net.go(wup.at[src, cut(theirs, F)], s.wu.at[dst], far)
    o = net.go(wout.at[cut(theirs * 2 + core, E // 2)], s.wo.at[cut(core, E // 2), drows], far)
    d = net.go(wdown.at[cut(theirs * 2 + core, F // 2)], s.wd.at[cut(core, F // 2), drows], far)
    yield
    for copy in q:
        copy.wait_recv()
    q2 = net.go(s.wq.at[got], s.wq.at[got], near)
    yield
    u.wait_recv()
    u2 = net.go(s.wu.at[got], s.wu.at[got], near)
    yield
    q2.wait_recv()
    for copy in local[:3]:
        copy.wait()
    yield
    u2.wait_recv()
    local[3].wait()
    yield
    o.wait_recv()
    ov = s.wo.at[cut(core, E // 2), ocols]
    o2 = net.go(ov, ov, near)
    d.wait_recv()
    dv = s.wd.at[cut(core, F // 2), ocols]
    d2 = net.go(dv, dv, near)
    yield
    local[4].wait()
    local[5].wait()
    o2.wait_recv()
    d2.wait_recv()


def ring_scatter(net, part, bufs, me, right, left, size, width):
    ta, tb, inl, inr = bufs
    lo, hi = pl.ds(0, width), pl.ds(width, width)
    far, rb, lb = lax.rem(me + 2, 4), lax.rem(me + 1, 4), lax.rem(me + 3, 4)
    a = net.go(part(far, lo), ta, right)
    b = net.go(part(far, hi), tb, left)
    c = net.go(part(rb, hi), inl.at[:, hi], right)
    d = net.go(part(lb, lo), inr.at[:, lo], left)
    yield
    a.wait_recv()
    view = part(rb, lo)
    view[...] = (view[...].astype(F32) + ta[...].astype(F32)).astype(BF)
    e = net.go(view, inl.at[:, lo], right)
    b.wait_recv()
    view = part(lb, hi)
    view[...] = (view[...].astype(F32) + tb[...].astype(F32)).astype(BF)
    f = net.go(view, inr.at[:, hi], left)
    yield
    for copy in (c, d, e, f):
        copy.wait_recv()


def scatter(net, p, s, at, col, row, look=None):
    half = D // 2
    far, rb, lb = lax.rem(col + 2, 4), lax.rem(col + 1, 4), lax.rem(col + 3, 4)
    mcols, ocols = rows(row, half), rows(1 - row, half)

    def yrows(b):
        return pl.ds(pl.multiple_of(b * B, B), YR)

    def zrows(b):
        return pl.ds(pl.multiple_of(b * B + YR, 16), ZR)

    def zpart(b, cols):
        return p.at[zrows(b), pl.ds(pl.multiple_of(row * half + cols.start, 256), cols.size)]

    order = (far, rb, lb, col)
    first = [net.go(p.at[zrows(b), ocols], s.ry.at[k], at["y1"]) for k, b in enumerate(order)]
    right, left = at["z1"], at["z3"]
    ring = ring_scatter(
        net, lambda b, cols: p.at[yrows(b), cols], (s.ta, s.tb, s.inl, s.inr), col, right, left, YR, half
    )
    step(ring)
    yield

    def add(k):
        first[k].wait_recv()
        view = p.at[zrows(order[k]), mcols]
        view[...] = (view[...].astype(F32) + s.ry[k].astype(F32)).astype(BF)

    step(ring)
    yield
    for k in range(3):
        add(k)
    ring2 = ring_scatter(
        net, zpart, (s.ta2, s.tb2, s.inl2, s.inr2), col, right, left, ZR, half // 2
    )
    step(ring2)
    yield
    add(3)
    finish(ring)
    for h in range(2):
        cols = pl.ds(h * half, half)
        total = (
            p[yrows(col), cols].astype(F32) + s.inl[:, cols].astype(F32) + s.inr[:, cols].astype(F32)
        )
        s.ysend[h] = total.astype(BF)
        if look is not None:
            look(h, total)
    last = net.go(s.ysend.at[1 - row], s.yrecv, at["y1"])
    yield
    step(ring2)
    yield
    finish(ring2)
    last.wait_recv()


def total_y(s, row):
    return s.ysend[row].astype(F32) + s.yrecv[...].astype(F32)


def total_z(p, s, col, row):
    own = p[pl.ds(pl.multiple_of(col * B + YR, 16), ZR), rows(row, D // 2)]
    return own.astype(F32) + s.inl2[...].astype(F32) + s.inr2[...].astype(F32)


def reduce_weights(net, grad, s, at, me, n):
    core, x, row = me["core"], me["x"], me["row"]
    half, size = n // 2, n // 8
    base = core * half
    away = (1 - core) * half
    c = net.go(grad.at[pl.ds(pl.multiple_of(away, half), half)], s.rc, at["core"])
    yield
    c.wait_recv()
    own = grad.at[pl.ds(pl.multiple_of(base, half), half)]
    own[...] = (own[...].astype(F32) + s.rc[...].astype(F32)).astype(BF)

    def part(block, cols):
        return grad.at[pl.ds(pl.multiple_of(base + block * size, size), size), cols]

    yield from ring_scatter(
        net, part, (s.ta, s.tb, s.inl, s.inr), x, at["x1"], at["x3"], size, D // 2
    )
    for h in range(2):
        cols = pl.ds(h * (D // 2), D // 2)
        total = (
            part(x, cols)[...].astype(F32) + s.inl[:, cols].astype(F32) + s.inr[:, cols].astype(F32)
        )
        s.sy[h] = total.astype(BF)
    g0 = net.go(s.sy.at[row], s.ry.at[0], at["y2"])
    g1 = net.go(s.sy.at[1 - row], s.ry.at[1], at["y1"])
    g2 = net.go(s.sy.at[1 - row], s.ry.at[2], at["y3"])
    yield
    g0.wait_recv()
    s.fin[core, x, row] = (s.sy[row].astype(F32) + s.ry[0].astype(F32)).astype(BF)
    g1.wait_recv()
    g2.wait_recv()
    s.fin[core, x, 1 - row] = (s.ry[1].astype(F32) + s.ry[2].astype(F32)).astype(BF)
    h0 = s.fin.at[core, x, 0]
    h1 = s.fin.at[core, x, 1]
    a0 = net.go(h0, h0, at["x1"])
    a1 = net.go(h1, h1, at["x3"])
    a2 = net.go(h1, h1, at["x1"])
    a3 = net.go(h0, h0, at["x3"])
    k0 = net.go(s.fin.at[core, x], s.fin.at[core, x], at["core"])
    yield
    lx, rx = lax.rem(x + 3, 4), lax.rem(x + 1, 4)
    a0.wait_recv()
    v = s.fin.at[core, lx, 0]
    a4 = net.go(v, v, at["x1"])
    a1.wait_recv()
    v = s.fin.at[core, rx, 1]
    a5 = net.go(v, v, at["x3"])
    a2.wait_recv()
    v = s.fin.at[core, lx]
    k1 = net.go(v, v, at["core"])
    a3.wait_recv()
    v = s.fin.at[core, rx]
    k2 = net.go(v, v, at["core"])
    yield
    a4.wait_recv()
    a5.wait_recv()
    v = s.fin.at[core, lax.rem(x + 2, 4)]
    k3 = net.go(v, v, at["core"])
    for copy in (k0, k1, k2):
        copy.wait_recv()
    yield
    k3.wait_recv()


def reduce_vectors(net, s, at):
    c = net.go(s.vec, s.vr.at[0], at["core"])
    yield
    c.wait_recv()
    s.vs[0] = s.vec[...] + s.vr[0]
    for n, axis in enumerate("xyz"):
        copies = [net.go(s.vs.at[n], s.vr.at[3 * n + k], at[axis + str(k)]) for k in (1, 2, 3)]
        yield
        for copy in copies:
            copy.wait_recv()
        s.vs[n + 1] = (s.vs[n] + s.vr[3 * n + 1]) + (s.vr[3 * n + 2] + s.vr[3 * n + 3])


def step(gen):
    next(gen, None)


def finish(gen):
    for _ in gen:
        pass


def interleave(*gens):
    live = list(gens)
    while live:
        for gen in list(live):
            try:
                next(gen)
            except StopIteration:
                live.remove(gen)


def turn(values, cos, sin):
    lane = lax.broadcasted_iota(jnp.int32, values.shape, 1)
    other = jnp.where(lane % HD < ROT // 2, pltpu.roll(values, E - ROT // 2, 1), pltpu.roll(values, ROT // 2, 1))
    return values * cos + other * sin


def split_heads(ref, at_rows, values):
    lane = lax.broadcasted_iota(jnp.int32, values.shape, 1)
    zero = jnp.zeros_like(values)
    ref[0, at_rows, :] = jnp.where(lane < HD, values, zero).astype(BF)
    ref[1, at_rows, :] = jnp.where(lane < HD, zero, values).astype(BF)


SCRATCH = dict(
    xall=((T, D), BF),
    gall=((T, D), BF),
    ain=((T, D), BF),
    mim=((T, D), BF),
    wq=((D, 3 * E), BF),
    wo=((E, D), BF),
    wu=((D, F), BF),
    wd=((F, D), BF),
    nb=((2, 8, D // 2), F32),
    mean=((T, 1), F32),
    inv=((T, 1), F32),
    hid=((T, F), BF),
    slope=((T, F), F32),
    segc=((T, 8), F32),
    nbs=((8, D // 2), F32),
    hpg=((T, F), BF),
    qs=((T, E), BF),
    qsm=((2, T, E), BF),
    km=((2, T, E), BF),
    vm=((2, T, E), BF),
    kt=((E, T), BF),
    vt=((E, T), BF),
    do=((T, E), BF),
    dom=((2, T, E), BF),
    probs=((2, 2560, B), F32),
    mt=((E, T), BF),
    mixed=((T, E), BF),
    dqt=((E, T), F32),
    dk=((T, E), F32),
    dv=((T, E), F32),
    qkvg=((T, 3 * E), BF),
    op=((T, D), BF),
    ng=((T, D), BF),
    ctab=((T, E), F32),
    stab=((T, E), F32),
    ssend=((8, B), F32),
    srecv=((8, B), F32),
    g1=((F + E, D), BF),
    g2=((F, D), BF),
    g3=((3 * E, D), BF),
    vec=((8, D), F32),
    vr=((10, 8, D), F32),
    vs=((4, 8, D), F32),
)
SCATTER = dict(
    ta=((YR, D // 2), BF),
    tb=((YR, D // 2), BF),
    inl=((YR, D), BF),
    inr=((YR, D), BF),
    ry=((4, ZR, D // 2), BF),
    ta2=((ZR, D // 4), BF),
    tb2=((ZR, D // 4), BF),
    inl2=((ZR, D // 2), BF),
    inr2=((ZR, D // 2), BF),
    ysend=((2, YR, D // 2), BF),
    yrecv=((YR, D // 2), BF),
)


def reduce_scratch(n):
    return dict(
        rc=((n // 2, D), BF),
        ta=((n // 8, D // 2), BF),
        tb=((n // 8, D // 2), BF),
        inl=((n // 8, D), BF),
        inr=((n // 8, D), BF),
        sy=((2, n // 8, D // 2), BF),
        ry=((3, n // 8, D // 2), BF),
    )


ROWS = (F + E, F, 3 * E)
for name in "on":
    SCRATCH.update({name + "_" + key: spec for key, spec in SCATTER.items()})
for k, n in enumerate(ROWS):
    SCRATCH.update({f"r{k}_{key}": spec for key, spec in reduce_scratch(n).items()})


def under(s, prefix, **more):
    picked = {k[len(prefix) :]: v for k, v in vars(s).items() if k.startswith(prefix)}
    return SimpleNamespace(**picked, **more)


def body(
    tok, cot, wqkv, wout, wup, wdown, bqkv, bup, bout, bdown, gain, bias, seg, ctab_h, stab_h,
    out, tgrad, f0, f1, f2, vout, *scratch,
):
    s = SimpleNamespace(**dict(zip(SCRATCH, scratch)))
    send, recv = scratch[len(SCRATCH) :]
    net = Net(send, recv)
    dp, row, col = lax.axis_index("dp"), lax.axis_index("row"), lax.axis_index("col")
    core, x, yh = lax.rem(dp, 2), lax.rem(dp // 2, 4), dp // 8
    half = D // 2

    def dev(core=core, x=x, yh=yh, row=row, col=col):
        return (yh * 8 + x * 2 + core, row, col)

    at = {"core": dev(core=1 - core)}
    for k in (1, 2, 3):
        at[f"x{k}"] = dev(x=lax.rem(x + k, 4))
        at[f"z{k}"] = dev(col=lax.rem(col + k, 4))
    at["y1"] = dev(row=1 - row)
    at["y2"] = dev(yh=1 - yh)
    at["y3"] = dev(yh=1 - yh, row=1 - row)
    y1 = at["y1"]

    s.nbs[...] = jnp.concatenate(
        [gain[...].astype(F32), bias[...].astype(F32), jnp.zeros((4, half), F32)]
    )
    barrier = pltpu.get_barrier_semaphore()
    for device in at.values():
        pl.semaphore_signal(barrier, inc=1, device_id=device, device_id_type=MESH)
    pl.semaphore_wait(barrier, len(at))

    gx = gather_tokens(net, tok, s.xall, at, half, col, row)
    gg = gather_tokens(net, cot, s.gall, at, half, col, row)
    gw = gather_weights(net, wqkv, wup, wout, wdown, s, at, core, row)
    nbc = net.go(s.nbs, s.nb.at[row], y1)
    step(gx)
    step(gw)
    tabs = [net.local(ctab_h, s.ctab), net.local(stab_h, s.stab)]
    s.nb[row] = s.nbs[...]
    s.vec[...] = jnp.zeros_like(s.vec)
    s.dk[...] = jnp.zeros_like(s.dk)
    s.dv[...] = jnp.zeros_like(s.dv)

    def flat(values):
        values = values.astype(F32)
        return jnp.concatenate([values[k : k + 1, :] for k in range(values.shape[0])], axis=1)

    segr = flat(seg[...])
    s.segc[...] = jnp.broadcast_to(segr, (8, T)).T
    bq_all = bqkv[...].astype(F32)
    mine = row == 0
    bq = jnp.concatenate(
        [jnp.where(mine, bq_all[k : k + 1, :E], bq_all[k : k + 1, E:]) for k in range(3)], axis=1
    )
    bu_all = flat(bup[...])
    bu = jnp.where(mine, bu_all[:, :F], bu_all[:, F:])
    fcols = pl.ds(pl.multiple_of(row * F, F), F)
    gcols = pl.ds(pl.multiple_of(row * half, half), half)

    nbc.wait_recv()

    def wide(k):
        return jnp.concatenate([s.nb[0, k : k + 1, :], s.nb[1, k : k + 1, :]], axis=1)

    gain0, gain1, bias0, bias1 = wide(0), wide(1), wide(2), wide(3)

    def norm(c):
        @pl.loop(0, 2)
        def _(b):
            r = rows(c * 2 + b, 128)
            xv = s.xall[r, :].astype(F32)
            mean = jnp.sum(xv, axis=1, keepdims=True) * (1.0 / D)
            square = jnp.sum(xv * xv, axis=1, keepdims=True) * (1.0 / D)
            inv = lax.rsqrt(square - mean * mean + EPSILON)
            normed = (xv - mean) * inv
            s.mean[r, :] = mean
            s.inv[r, :] = inv
            s.ain[r, :] = (normed * gain0 + bias0).astype(BF)
            s.mim[r, :] = (normed * gain1 + bias1).astype(BF)

    def project(c):
        r = rows(c)
        pre = nn(s.ain[r, :], s.wq[...]) + bq
        cos, sin = s.ctab[r, :], s.stab[r, :]
        query = (turn(pre[:, :E], cos, sin)).astype(BF).astype(F32) * (1.0 / math.sqrt(HD))
        key = turn(pre[:, E : 2 * E], cos, sin).astype(BF).astype(F32)
        value = pre[:, 2 * E :].astype(BF).astype(F32)
        s.qs[r, :] = query.astype(BF)
        split_heads(s.qsm, r, query)
        split_heads(s.km, r, key)
        split_heads(s.vm, r, value)
        s.kt[:, r] = key.T.astype(BF)
        s.vt[:, r] = value.T.astype(BF)

    def expand(c):
        r = rows(c)
        pre = nn(s.mim[r, :], s.wu[...]) + bu
        cdf = 0.5 * (1.0 + lax.erf(pre * math.sqrt(0.5)))
        s.hid[r, :] = (pre * cdf).astype(BF)
        s.slope[r, :] = cdf + pre * jnp.exp(-0.5 * pre * pre) * (1.0 / math.sqrt(2.0 * math.pi))

    def contract(c):
        r = rows(c)
        back = (nt(s.gall[r, :], s.wd[...]) * s.slope[r, :]).astype(BF)
        s.hpg[r, :] = back
        s.vec[6:7, fcols] += jnp.sum(back.astype(F32), axis=0, keepdims=True)
        s.vec[4:5, gcols] += jnp.sum(s.gall[r, gcols].astype(F32), axis=0, keepdims=True)
        dout = nt(s.gall[r, :], s.wo[...]).astype(BF).astype(F32)
        s.do[r, :] = dout.astype(BF)
        split_heads(s.dom, r, dout)

    rb, lb, fb = lax.rem(col + 1, 4), lax.rem(col + 3, 4), lax.rem(col + 2, 4)
    step(gx)
    norm(col)
    step(gx)
    step(gw)
    step(gx)
    step(gx)
    step(gg)
    norm(lb)
    norm(rb)
    for copy in tabs:
        copy.wait()
    step(gw)
    step(gw)
    project(col)
    project(lb)
    step(gx)
    project(rb)
    step(gw)
    expand(col)
    step(gg)
    expand(lb)
    expand(rb)
    step(gw)
    finish(gx)
    norm(fb)
    project(fb)
    expand(fb)

    first = [0, 256, 768, 1536]
    for i in range(4):
        n = (i + 1) * B
        q = pl.ds(i * B, B)

        @pl.loop(0, 2)
        def _(h):
            scores = nt(s.km[h, pl.ds(0, n), :], s.qs[q, :])
            kid = lax.broadcasted_iota(jnp.int32, (n, B), 0)
            qid = lax.broadcasted_iota(jnp.int32, (n, B), 1) + i * B
            allowed = (kid <= qid) & (s.segc[pl.ds(0, n), 0:1] == segr[:, i * B : (i + 1) * B])
            scores = jnp.where(allowed, scores, -1e30)
            top = jnp.max(scores, axis=0, keepdims=True)
            expo = jnp.exp(scores - top)
            probs = expo * (1.0 / jnp.sum(expo, axis=0, keepdims=True))
            s.probs[h, pl.ds(first[i], n), :] = probs
            hrows = rows(h, HD)
            s.mt[hrows, q] = nn(s.vt[hrows, pl.ds(0, n)], probs.astype(BF)).astype(BF)

        s.mixed[q, :] = s.mt[:, q].astype(F32).T.astype(BF)
        step(gg) if i in (1, 3) else None

    finish(gw)
    step(gg)

    @pl.loop(0, 4)
    def _(b):
        r = rows(b)
        s.op[r, :] = (nn(s.mixed[r, :], s.wo[...]) + nn(s.hid[r, :], s.wd[...])).astype(BF)

    step(gg)
    contract(col)
    contract(lb)
    contract(rb)
    finish(gg)
    contract(fb)
    so, sn = under(s, "o_"), under(s, "n_")
    ro = scatter(net, s.op, so, at, col, row)
    step(ro)

    where = dict(core=core, x=x, row=row)
    r0 = reduce_weights(net, s.g1, under(s, "r0_", fin=f0), at, where, ROWS[0])
    r1 = reduce_weights(net, s.g2, under(s, "r1_", fin=f1), at, where, ROWS[1])
    r2 = reduce_weights(net, s.g3, under(s, "r2_", fin=f2), at, where, ROWS[2])

    @pl.loop(0, 4)
    def _(b):
        r = rows(b, 128)
        s.g1[r, :] = tn(s.hid[:, r], s.gall[...]).astype(BF)

    s.g1[F:, :] = nn(s.mt[...], s.gall[...]).astype(BF)
    step(r0)

    @pl.loop(0, 4)
    def _(b):
        r = rows(b, 128)
        s.g2[r, :] = tn(s.hpg[:, r], s.mim[...]).astype(BF)

    step(r1)
    step(r0)

    for i in range(4):
        n = (i + 1) * B
        q = pl.ds(i * B, B)

        @pl.loop(0, 2)
        def _(h):
            probs = s.probs[h, pl.ds(first[i], n), :]
            dprob = nt(s.vm[h, pl.ds(0, n), :], s.do[q, :])
            inner = jnp.sum(probs * dprob, axis=0, keepdims=True)
            dscore = (probs * (dprob - inner)).astype(BF)
            s.dv[pl.ds(0, n), :] += nn(probs.astype(BF), s.dom[h, q, :])
            s.dk[pl.ds(0, n), :] += nn(dscore, s.qsm[h, q, :])
            hrows = rows(h, HD)
            s.dqt[hrows, q] = nn(s.kt[hrows, pl.ds(0, n)], dscore) * (1.0 / math.sqrt(HD))

        if i == 0:
            step(r1)
        if i == 2:
            step(ro)
        if i == 3:
            step(r0)
            step(ro)

    @pl.loop(0, 4)
    def _(b):
        r = rows(b)
        cos, sin = s.ctab[r, :], -s.stab[r, :]
        dq = turn(s.dqt[:, r].T, cos, sin).astype(BF)
        dk = turn(s.dk[r, :], cos, sin).astype(BF)
        dv = s.dv[r, :].astype(BF)
        both = jnp.concatenate([dq, dk, dv], axis=1)
        s.qkvg[r, :] = both
        ecols3 = pl.ds(pl.multiple_of(row * 3 * E, 3 * E), 3 * E)
        s.vec[5:6, ecols3] += jnp.sum(both.astype(F32), axis=0, keepdims=True)

    step(r1)
    step(ro)

    @pl.loop(0, 3)
    def _(b):
        r = rows(b, E)
        s.g3[r, :] = tn(s.qkvg[:, r], s.ain[...]).astype(BF)

    step(r2)

    @pl.loop(0, 4)
    def _(b):
        r = rows(b)
        attn = nt(s.qkvg[r, :], s.wq[...])
        mlp = nt(s.hpg[r, :], s.wu[...])
        normed = (s.xall[r, :].astype(F32) - s.mean[r, :]) * s.inv[r, :]
        s.ng[r, :] = (attn * gain0 + mlp * gain1).astype(BF)
        s.vec[0:1, :] += jnp.sum(attn * normed, axis=0, keepdims=True)
        s.vec[1:2, :] += jnp.sum(mlp * normed, axis=0, keepdims=True)
        s.vec[2:3, :] += jnp.sum(attn, axis=0, keepdims=True)
        s.vec[3:4, :] += jnp.sum(mlp, axis=0, keepdims=True)

    r = rows(col)
    mean, inv = s.mean[r, :], s.inv[r, :]
    sums = []

    def look(h, total):
        xv = s.xall[pl.ds(pl.multiple_of(col * B, B), YR), pl.ds(h * half, half)].astype(F32)
        normed = (xv - mean[:YR]) * inv[:YR]
        sums.append(jnp.sum(total, axis=1, keepdims=True))
        sums.append(jnp.sum(total * normed, axis=1, keepdims=True))

    rn = scatter(net, s.ng, sn, at, col, row, look)
    step(rn)
    rv = reduce_vectors(net, s, at)
    step(rv)
    step(r2)
    step(r0)
    step(ro)
    step(r1)
    finish(ro)
    bias_out = flat(bout[...]) + flat(bdown[...])
    xv = s.xall[r, gcols].astype(F32) + bias_out
    out[...] = (xv + jnp.concatenate([total_y(so, row), total_z(s.op, so, col, row)])).astype(BF)
    step(rv)
    step(r0)
    step(rn)
    step(r2)
    step(r1)
    step(rv)
    step(rn)
    step(r0)
    step(r2)
    step(r1)
    step(rv)
    step(rn)
    step(r2)
    step(r0)
    step(rn)
    step(r1)
    finish(rn)
    normed = (s.xall[r, gcols].astype(F32) - mean) * inv
    zsum = total_z(s.ng, sn, col, row)
    first_sum = jnp.concatenate([sums[0] + sums[2], jnp.sum(zsum, axis=1, keepdims=True)])
    second = jnp.sum(zsum * normed[YR:], axis=1, keepdims=True)
    second_sum = jnp.concatenate([sums[1] + sums[3], second])
    lane = lax.broadcasted_iota(jnp.int32, (B, 128), 1)
    s.ssend[...] = jnp.where(lane < 4, first_sum, second_sum).T[:8, :]
    ys = net.go(s.ssend, s.srecv, y1)
    interleave(r0, r2, r1, rv)
    vout[0] = s.vs[2]
    vout[1] = s.vs[3]
    ys.wait_recv()
    both = (s.ssend[...] + s.srecv[...]) * (1.0 / D)
    both = jnp.concatenate([both] * 16).T
    total = jnp.concatenate([total_y(sn, row), zsum])
    tgrad[...] = (
        s.gall[r, gcols].astype(F32) + inv * (total - both[:, 0:1] - normed * both[:, 4:5])
    ).astype(BF)
    for copy in net.sent:
        copy.wait_send()


def tables():
    freq = np.arange(ROT // 2, dtype=np.float32)
    inverse = np.float32(10000.0) ** (np.float32(-2.0) * freq / np.float32(ROT))
    angle = np.arange(T, dtype=np.float32)[:, None] * inverse[None, :].astype(np.float32)
    cos, sin = np.cos(angle), np.sin(angle)
    ones, zeros = np.ones((T, HD - ROT), np.float32), np.zeros((T, HD - ROT), np.float32)
    ctab = np.concatenate([cos, cos, ones] * 2, axis=1)
    stab = np.concatenate([-sin, sin, zeros] * 2, axis=1)
    return ctab.astype(np.float32), stab.astype(np.float32)


def last(
    f0_h, f1_h, f2_h, vec_h, out_h, tgrad_h,
    out_o, tgrad_o, wq_o, bq_o, wo_o, bo_o, wu_o, bu_o, wd_o, bd_o, gain_o, bias_o,
    f0, f1, f2, vec, out, tgrad, wq, wo, wu, wd, sems,
):
    row = lax.axis_index("row")
    copies = []

    def write(src, dst):
        copy = pltpu.make_async_copy(src, dst, sems.at[len(copies)])
        copy.start()
        copies.append(copy)
        return copy

    pairs = ((f0_h, f0), (f1_h, f1), (f2_h, f2), (vec_h, vec), (out_h, out), (tgrad_h, tgrad))
    reads = [write(a, b) for a, b in pairs]
    reads[0].wait()
    for r in range(2):
        for k in range(8):
            piece = f0[k // 4, k % 4, r].astype(F32)
            n = piece.shape[0]
            inside = max(0, min(n, F - k * n))
            if inside:
                wd[pl.ds(r * F + k * n, inside), :] = piece[:inside]
            if inside < n:
                wo[pl.ds(r * E + k * n + inside - F, n - inside), :] = piece[inside:]
        write(wd.at[pl.ds(r * F, F)], wd_o.at[pl.ds(r * F, F)])
    write(wo, wo_o)
    reads[1].wait()
    for r in range(2):
        for k in range(4):
            pair = [f1[(2 * k + h) // 4, (2 * k + h) % 4, r].astype(F32) for h in range(2)]
            wu[:, pl.ds(r * F + k * E, E)] = jnp.concatenate(pair).T
        write(wu.at[:, pl.ds(r * F, F)], wu_o.at[:, pl.ds(r * F, F)])
    reads[2].wait()
    for r in range(2):
        whole = jnp.concatenate([f2[k // 4, k % 4, r].astype(F32) for k in range(8)])
        for k in range(3):
            wq[k, :, pl.ds(r * E, E)] = whole[k * E : (k + 1) * E].T
    write(wq, wq_o)
    for copy in reads[3:]:
        copy.wait()
    write(out, out_o)
    write(tgrad, tgrad_o)
    half = D // 2
    left = row == 0

    def cut(values):
        return jnp.where(left, values[:, :half], values[:, half:])

    bo_o[...] = cut(vec[0, 4:5, :])
    bd_o[...] = cut(vec[0, 4:5, :])
    for k in range(3):
        bq_o[k : k + 1, :E] = vec[0, 5:6, k * E : (k + 1) * E]
        bq_o[k : k + 1, E:] = vec[0, 5:6, (k + 3) * E : (k + 4) * E]
    bu_o[...] = vec[0, 6:7, :]
    gain_o[...] = cut(vec[1, 0:2, :])
    bias_o[...] = cut(vec[1, 2:4, :])
    for copy in copies[len(reads) :]:
        copy.wait()


def on_device(
    tokens, segment_ids, w_qkv, b_qkv, w_out, b_out, w_up, b_up, w_down, b_down, norm_gain, norm_bias, cotangent
):
    ctab, stab = tables()
    vmem = pl.BlockSpec(memory_space=pltpu.VMEM)
    hbm = pl.BlockSpec(memory_space=pl.ANY)
    shape = jax.ShapeDtypeStruct
    early = [
        shape((2, 4, 2, ROWS[0] // 8, D // 2), BF),
        shape((2, 4, 2, ROWS[1] // 8, D // 2), BF),
        shape((2, 4, 2, ROWS[2] // 8, D // 2), BF),
        shape((2, 8, D), F32),
    ]
    out, tgrad, f0, f1, f2, vec = pl.pallas_call(
        body,
        out_shape=[
            shape((B, D // 2), BF),
            shape((B, D // 2), BF),
            *early,
        ],
        in_specs=[hbm] * 6 + [vmem] * 7 + [hbm] * 2,
        out_specs=[vmem] * 6,
        scratch_shapes=[pltpu.VMEM(*spec) for spec in SCRATCH.values()]
        + [pltpu.SemaphoreType.DMA((NSEM,)), pltpu.SemaphoreType.DMA((NSEM,))],
        compiler_params=pltpu.CompilerParams(
            collective_id=0, has_side_effects=True, vmem_limit_bytes=60 * 1024 * 1024
        ),
        name="block",
    )(
        tokens, cotangent, w_qkv, w_out, w_up, w_down, b_qkv, b_up.reshape(8, 128),
        b_out.reshape(4, 128), b_down.reshape(4, 128), norm_gain, norm_bias,
        segment_ids.reshape(8, 128), jnp.asarray(ctab), jnp.asarray(stab),
    )
    big = [
        ((3, D // 2, 2 * E), F32),
        ((2 * E, D // 2), F32),
        ((D // 2, 2 * F), F32),
        ((2 * F, D // 2), F32),
    ]
    results = pl.pallas_call(
        last,
        out_shape=[
            shape((B, D // 2), BF),
            shape((B, D // 2), BF),
            shape(*big[0]),
            shape((3, 2 * E), F32),
            shape(*big[1]),
            shape((1, D // 2), F32),
            shape(*big[2]),
            shape((1, 2 * F), F32),
            shape(*big[3]),
            shape((1, D // 2), F32),
            shape((2, D // 2), F32),
            shape((2, D // 2), F32),
        ],
        in_specs=[hbm] * 6,
        out_specs=[hbm, hbm, hbm, vmem, hbm, vmem, hbm, vmem, hbm, vmem, vmem, vmem],
        scratch_shapes=[pltpu.VMEM(e.shape, e.dtype) for e in early]
        + [pltpu.VMEM((B, D // 2), BF)] * 2
        + [pltpu.VMEM(*spec) for spec in big]
        + [pltpu.SemaphoreType.DMA((16,))],
        compiler_params=pltpu.CompilerParams(vmem_limit_bytes=60 * 1024 * 1024),
        name="last",
    )(f0, f1, f2, vec, out, tgrad)
    out, tgrad, wq, bq, wo, bo, wu, bu, wd, bd, gain, bias = results
    bo, bu, bd = bo.reshape(-1), bu.reshape(-1), bd.reshape(-1)
    return (out, tgrad, wq, bq, wo, bo, wu, bu, wd, bd, gain, bias)


def solution(mesh):
    in_specs = (
        P(("dp", "col"), "row"),
        P("dp"),
        P(None, "row", "col"),
        P(None, "col"),
        P("col", "row"),
        P("row"),
        P("row", "col"),
        P("col"),
        P("col", "row"),
        P("row"),
        P(None, "row"),
        P(None, "row"),
        P(("dp", "col"), "row"),
    )
    out_specs = (
        P(("dp", "col"), "row"),
        P(("dp", "col"), "row"),
        P(None, "row", "col"),
        P(None, "col"),
        P("col", "row"),
        P("row"),
        P("row", "col"),
        P("col"),
        P("col", "row"),
        P("row"),
        P(None, "row"),
        P(None, "row"),
    )
    return jax.shard_map(
        on_device, mesh=mesh, in_specs=in_specs, out_specs=out_specs, check_vma=False
    )
```

```python
from types import SimpleNamespace
import math

import numpy as np
import jax
import jax.numpy as jnp
from jax import lax
from jax.experimental import pallas as pl
from jax.experimental.pallas import tpu as pltpu
from jax.sharding import PartitionSpec as P

MESH = pl.DeviceIdType.MESH
BF = jnp.bfloat16
F32 = jnp.float32
T = 1024
D = 1024
HD = 64
ROT = 16
E = 128
F = 512
B = 256
EPSILON = 1e-05
NSEM = 200
YROWS = dict(x=144, g=144, o=176, n=240)


ORDER = (
    0, 1, 2, 3, 4, 7, 8, 42, 2, 10, 3, 6, 11, 7, 4, 12, 8, 1, 5, 9, 15, 126, 38, 6, 14, 40, 40, 38,
    127, 5, 13, 10, 11, 17, 130, 131, 12, 9, 16, 19, 20, 21, 22, 23, 26, 27, 128, 129, 14, 13, 18,
    132, 133, 134, 39, 41, 135, 136, 21, 26, 29, 39, 137, 20, 22, 23, 24, 25, 27, 28, 30, 31, 34,
    41, 138, 139, 140, 141, 29, 142, 143, 144, 30, 145, 25, 33, 146, 24, 32, 36, 148, 28, 35, 147,
    31, 33, 32, 37, 77, 43, 47, 78, 44, 48, 50, 79, 45, 49, 51, 80, 46, 149, 150, 81, 151, 95, 152,
    153, 81, 82, 83, 84, 85, 86, 154, 43, 53, 95, 44, 45, 46, 51, 50, 52, 54, 55, 56, 57, 96, 97,
    98, 99, 100, 155, 56, 57, 58, 85, 86, 87, 156, 157, 158, 159, 99, 100, 101, 160, 60, 64, 161,
    58, 61, 65, 67, 162, 52, 62, 66, 68, 87, 88, 59, 163, 60, 63, 70, 101, 102, 61, 71, 73, 165,
    123, 164, 62, 72, 74, 109, 123, 74, 73, 63, 75, 75, 109, 110, 111, 112, 113, 114, 123, 68, 114,
    113, 115, 67, 69, 88, 89, 90, 102, 103, 104, 123, 59, 166, 115, 116, 123, 124, 116, 117, 118,
    104, 106, 69, 76, 103, 105, 107, 90, 92, 92, 106, 89, 91, 93, 91, 105, 117, 119, 119, 118, 120,
    121, 120, 107, 108, 93, 94, 76, 125, 121, 122, 108, 94, 125, 122,
)


def nn(a, b):
    return jnp.dot(a, b, preferred_element_type=F32)


def nt(a, b):
    return lax.dot_general(a, b, (((1,), (1,)), ((), ())), preferred_element_type=F32)


def tn(a, b):
    return lax.dot_general(a, b, (((0,), (0,)), ((), ())), preferred_element_type=F32)


def rows(block, size=B):
    return pl.ds(pl.multiple_of(block * size, size), size)


class Net:
    def __init__(self, send, recv):
        self.send, self.recv, self.count, self.sent = send, recv, 0, []

    def go(self, src, dst, device):
        k = self.count
        self.count += 1
        assert k < NSEM
        copy = pltpu.make_async_remote_copy(
            src_ref=src,
            dst_ref=dst,
            send_sem=self.send.at[k],
            recv_sem=self.recv.at[k],
            device_id=device,
            device_id_type=MESH,
        )
        copy.start()
        self.sent.append(copy)
        return copy

    def local(self, src, dst):
        k = self.count
        self.count += 1
        assert k < NSEM
        copy = pltpu.make_async_copy(src, dst, self.send.at[k])
        copy.start()
        return copy


def later(deps, cost, work):
    yield deps, cost
    work()


def gather_tokens(net, add, done, name, begin, own, full, at, half, col, row, yr):
    right, left, peer = at["z1"], at["z3"], at["y1"]
    zr = B - yr
    part = zr // 32 * 16
    cut = yr + part
    c = {}

    def place(b, h, start=0, size=B):
        r = pl.ds(pl.multiple_of(b * B + start, 16), size)
        return full.at[r, pl.ds(pl.multiple_of(h * half, half), half)]

    def move(key, device, *where):
        c[key] = net.go(place(*where), place(*where), device)
        done.add(name + key)

    def send(key, device, start, size):
        c[key] = net.go(own.at[pl.ds(start, size)], place(col, row, start, size), device)
        done.add(name + key)

    lcol, rcol, fcol = lax.rem(col + 3, 4), lax.rem(col + 1, 4), lax.rem(col + 2, 4)

    def begin_work():
        yield begin, 0.1
        c["keep"] = net.local(own, place(col, row))
        send("p0", peer, 0, yr)
        send("r1", right, yr, zr)
        send("l1", left, yr, zr)
        send("r0", right, 0, yr)
        send("l0", left, 0, yr)
        send("p1", peer, yr, zr)
        c["keep"].wait()

    def hop(keys, *work):
        yield tuple(name + k for k in keys), 0.0
        yield tuple(c[k] for k in keys), 0.05
        for k in keys:
            c[k].wait_recv()
        for w in work:
            move(*w)
        done.update(name + k + "!" for k in keys)

    def whole(flag, keys):
        yield tuple(name + k + "!" for k in keys), 0.0
        done.add(name + flag)

    add(begin_work())
    add(hop(["p0"], ("r2", right, col, 1 - row, 0, yr), ("l2", left, col, 1 - row, 0, yr)))
    add(hop(["r1"], ("r3", right, lcol, row, yr, part), ("p2", peer, lcol, row, yr, zr)))
    add(hop(["l1"], ("l3", left, rcol, row, cut, B - cut), ("p3", peer, rcol, row, yr, zr)))
    add(hop(["r0"], ("r4", right, lcol, row, 0, yr)))
    add(hop(["l2"], ("l4", left, rcol, 1 - row, 0, yr)))
    add(hop(["r3", "l3"], ("p4", peer, fcol, row, yr, zr)))
    add(hop(["p1"]))
    add(hop(["l0"]))
    add(hop(["r2"]))
    add(hop(["p2"]))
    add(hop(["p3"]))
    add(hop(["r4"]))
    add(hop(["l4"]))
    add(hop(["p4"]))
    add(whole("own", ["p0", "p1"]))
    add(whole("left", ["r0", "r1", "r2", "p2"]))
    add(whole("right", ["l0", "l1", "l2", "p3"]))
    add(whole("far", ["r3", "r4", "l3", "l4", "p4"]))


def gather_weights(net, add, done, wqkv, wup, wout, wdown, s, at, core, row):
    half, part = D // 2, D // 4
    mine, theirs = row, 1 - row
    drows, ocols = rows(row, half), rows(1 - row, half)

    def cut(which, size):
        return pl.ds(pl.multiple_of(which * size, size), size)

    local = {}
    for k in range(3):
        kcols = pl.ds(k * E, E)
        local[k] = net.local(wqkv.at[k, :, cut(mine, E)], s.wq.at[drows, kcols])
    local["u"] = net.local(wup.at[:, cut(mine, F)], s.wu.at[drows])
    local["o"] = net.local(wout.at[cut(mine, E)], s.wo.at[:, drows])
    local["d"] = net.local(wdown.at[cut(mine, F)], s.wd.at[:, drows])
    src, dst, got = cut(core, part), cut(row * 2 + core, part), cut((1 - row) * 2 + core, part)
    far, near = at["y3"], at["core"]
    q = [
        net.go(wqkv.at[k, src, cut(theirs, E)], s.wq.at[dst, pl.ds(k * E, E)], far)
        for k in range(3)
    ]
    u = net.go(wup.at[src, cut(theirs, F)], s.wu.at[dst], far)
    o = net.go(wout.at[cut(theirs * 2 + core, E // 2)], s.wo.at[cut(core, E // 2), drows], far)
    d = net.go(wdown.at[cut(theirs * 2 + core, F // 2)], s.wd.at[cut(core, F // 2), drows], far)

    def share(flag, copies, view, locals_):
        yield tuple(copies), 0.05
        for copy in copies:
            copy.wait_recv()
        second = net.go(view, view, near)
        yield (second,), 0.0
        second.wait_recv()
        for k in locals_:
            local[k].wait()
        done.add(flag)

    add(share("wq", q, s.wq.at[got], range(3)))
    add(share("wu", [u], s.wu.at[got], "u"))
    add(share("wo", [o], s.wo.at[cut(core, E // 2), ocols], "o"))
    add(share("wd", [d], s.wd.at[cut(core, F // 2), ocols], "d"))


def ring_scatter(net, add, done, name, part, bufs, me, right, left, width, ready):
    ta, tb, inl, inr = bufs
    lo, hi = pl.ds(0, width), pl.ds(width, width)
    far, rb, lb = lax.rem(me + 2, 4), lax.rem(me + 1, 4), lax.rem(me + 3, 4)
    c = {}

    def send(deps, *sends):
        yield deps, 0.05
        for key, src, dst, device in sends:
            c[key] = net.go(src, dst, device)
            done.add(name + key)

    def through(came, flag, buf, view, key, dst, device):
        yield (name + came, flag), 0.0
        yield (c[came],), 0.15
        c[came].wait_recv()
        view[...] = (view[...].astype(F32) + buf[...].astype(F32)).astype(BF)
        c[key] = net.go(view, dst, device)
        done.add(name + key)

    def finish():
        yield tuple(name + k for k in "cdef") + (ready[3],), 0.0
        yield tuple(c[k] for k in "cdef"), 0.0
        for k in "cdef":
            c[k].wait_recv()
        done.add(name + "sum")

    add(send((ready[0],), ("a", part(far, lo), ta, right), ("b", part(far, hi), tb, left)))
    add(send((ready[1],), ("c", part(rb, hi), inl.at[:, hi], right)))
    add(send((ready[2],), ("d", part(lb, lo), inr.at[:, lo], left)))
    add(through("a", ready[1], ta, part(rb, lo), "e", inl.at[:, lo], right))
    add(through("b", ready[2], tb, part(lb, hi), "f", inr.at[:, hi], left))
    add(finish())


def reduce_weights(net, add, done, name, begin, grad, s, at, me, n):
    core, x, row = me["core"], me["x"], me["row"]
    half, size = n // 2, n // 8
    base, away = core * half, (1 - core) * half
    x1, x3, near = at["x1"], at["x3"], at["core"]
    lx, rx, fx = lax.rem(x + 3, 4), lax.rem(x + 1, 4), lax.rem(x + 2, 4)
    c = {}

    def start():
        yield (begin,), 0.05
        copy = net.go(grad.at[pl.ds(pl.multiple_of(away, half), half)], s.rc, near)
        yield (copy,), 0.4 * n / 640
        copy.wait_recv()
        own = grad.at[pl.ds(pl.multiple_of(base, half), half)]
        own[...] = (own[...].astype(F32) + s.rc[...].astype(F32)).astype(BF)
        done.add(name + "core")

    def part(block, cols):
        return grad.at[pl.ds(pl.multiple_of(base + block * size, size), size), cols]

    def across():
        yield (name + "sum",), 0.2
        for h in range(2):
            cols = pl.ds(h * (D // 2), D // 2)
            total = part(x, cols)[...].astype(F32) + s.inl[:, cols].astype(F32)
            s.sy[h] = (total + s.inr[:, cols].astype(F32)).astype(BF)
        g0 = net.go(s.sy.at[row], s.ry.at[0], at["y2"])
        g1 = net.go(s.sy.at[1 - row], s.ry.at[1], at["y1"])
        g2 = net.go(s.sy.at[1 - row], s.ry.at[2], at["y3"])
        yield (g0, g1, g2), 0.15
        for copy in (g0, g1, g2):
            copy.wait_recv()
        s.fin[core, x, row] = (s.sy[row].astype(F32) + s.ry[0].astype(F32)).astype(BF)
        s.fin[core, x, 1 - row] = (s.ry[1].astype(F32) + s.ry[2].astype(F32)).astype(BF)
        for key, h, device in (("a", 0, x1), ("b", 1, x3), ("c", 1, x1), ("d", 0, x3)):
            view = s.fin.at[core, x, h]
            c[key] = net.go(view, view, device)
        view = s.fin.at[core, x]
        c["k"] = net.go(view, view, near)
        done.add(name + "sent")

    def hop(keys, flag, view, device, key, need=()):
        yield (name + flag,) + tuple(name + k + "!" for k in need), 0.0
        yield tuple(c[k] for k in keys), 0.05
        for k in keys:
            c[k].wait_recv()
        c[key] = net.go(view, view, device)
        done.update(name + k + "!" for k in keys)
        done.add(name + key)

    def end():
        yield tuple(name + k for k in ("l", "m", "n")), 0.0
        yield tuple(c[k] for k in "klmn"), 0.0
        for k in "klmn":
            c[k].wait_recv()
        done.add(name + "end")

    ready = (name + "core",) * 4
    add(start())
    ring_scatter(
        net, add, done, name, part, (s.ta, s.tb, s.inl, s.inr), x, x1, x3, D // 2, ready
    )
    add(across())
    add(hop("a", "sent", s.fin.at[core, lx, 0], x1, "p"))
    add(hop("b", "sent", s.fin.at[core, rx, 1], x3, "q"))
    add(hop("c", "sent", s.fin.at[core, lx], near, "l", "a"))
    add(hop("d", "sent", s.fin.at[core, rx], near, "m", "b"))
    add(hop("pq", "p", s.fin.at[core, fx], near, "n", "b"))
    add(end())


def reduce_vectors(net, done, s, at):
    yield ("vec",), 0.0
    c = net.go(s.vec, s.vr.at[0], at["core"])
    yield (c,), 0.05
    c.wait_recv()
    s.vs[0] = s.vec[...] + s.vr[0]
    for n, axis in enumerate("xyz"):
        copies = [net.go(s.vs.at[n], s.vr.at[3 * n + k], at[axis + str(k)]) for k in (1, 2, 3)]
        yield tuple(copies), 0.05
        for copy in copies:
            copy.wait_recv()
        s.vs[n + 1] = (s.vs[n] + s.vr[3 * n + 1]) + (s.vr[3 * n + 2] + s.vr[3 * n + 3])
    done.add("vsum")


def scatter(net, add, done, name, ready, p, s, at, col, row, yr, look=None):
    half, zr = D // 2, B - yr
    far, rb, lb = lax.rem(col + 2, 4), lax.rem(col + 1, 4), lax.rem(col + 3, 4)
    mcols, ocols = rows(row, half), rows(1 - row, half)
    right, left, peer = at["z1"], at["z3"], at["y1"]

    def yrows(b):
        return pl.ds(pl.multiple_of(b * B, B), yr)

    def zrows(b):
        return pl.ds(pl.multiple_of(b * B + yr, 16), zr)

    def zpart(b, cols):
        return p.at[zrows(b), pl.ds(pl.multiple_of(row * half + cols.start, 256), cols.size)]

    def pair(k, b):
        yield (ready[k],), 0.05
        copy = net.go(p.at[zrows(b), ocols], s.ry.at[k], peer)
        yield (copy,), 0.15
        copy.wait_recv()
        view = p.at[zrows(b), mcols]
        view[...] = (view[...].astype(F32) + s.ry[k].astype(F32)).astype(BF)
        done.add(name + "z" + str(k))

    def last():
        yield (name + "y.sum",), 0.3
        for h in range(2):
            cols = pl.ds(h * half, half)
            total = p[yrows(col), cols].astype(F32) + s.inl[:, cols].astype(F32)
            total += s.inr[:, cols].astype(F32)
            s.ysend[h] = total.astype(BF)
            if look is not None:
                look(h, total)
        copy = net.go(s.ysend.at[1 - row], s.yrecv, peer)
        yield (copy,), 0.0
        copy.wait_recv()
        done.add(name + "y.end")

    for k, b in enumerate((far, rb, lb, col)):
        add(pair(k, b))
    ring_scatter(
        net, add, done, name + "y.", lambda b, cols: p.at[yrows(b), cols],
        (s.ta, s.tb, s.inl, s.inr), col, right, left, half, ready,
    )
    ring_scatter(
        net, add, done, name + "z.", zpart,
        (s.ta2, s.tb2, s.inl2, s.inr2), col, right, left, half // 2,
        tuple(name + "z" + str(k) for k in range(4)),
    )
    add(last())


def total_y(s, row):
    return s.ysend[row].astype(F32) + s.yrecv[...].astype(F32)


def total_z(p, s, col, row, yr):
    own = p[pl.ds(pl.multiple_of(col * B + yr, 16), B - yr), rows(row, D // 2)]
    return own.astype(F32) + s.inl2[...].astype(F32) + s.inr2[...].astype(F32)


def run(tasks, done):
    asked = [next(task)[0] for task in tasks]
    for k in ORDER:
        for need in asked[k]:
            assert not isinstance(need, str) or need in done, "order"
        asked[k] = next(tasks[k], ((),))[0]
    assert all(next(task, None) is None for task in tasks), "unfinished"


def turn(values, cos, sin):
    lane = lax.broadcasted_iota(jnp.int32, values.shape, 1)
    other = jnp.where(lane % HD < ROT // 2, pltpu.roll(values, E - ROT // 2, 1), pltpu.roll(values, ROT // 2, 1))
    return values * cos + other * sin


def split_heads(ref, at_rows, values):
    lane = lax.broadcasted_iota(jnp.int32, values.shape, 1)
    zero = jnp.zeros_like(values)
    ref[0, at_rows, :] = jnp.where(lane < HD, values, zero).astype(BF)
    ref[1, at_rows, :] = jnp.where(lane < HD, zero, values).astype(BF)


SCRATCH = dict(
    xall=((T, D), BF),
    gall=((T, D), BF),
    ain=((T, D), BF),
    mim=((T, D), BF),
    wq=((D, 3 * E), BF),
    wo=((E, D), BF),
    wu=((D, F), BF),
    wd=((F, D), BF),
    nb=((2, 8, D // 2), F32),
    mean=((T, 1), F32),
    inv=((T, 1), F32),
    hid=((T, F), BF),
    slope=((T, F), F32),
    segc=((T, 8), F32),
    nbs=((8, D // 2), F32),
    hpg=((T, F), BF),
    qs=((T, E), BF),
    qsm=((2, T, E), BF),
    km=((2, T, E), BF),
    vm=((2, T, E), BF),
    kt=((E, T), BF),
    vt=((E, T), BF),
    do=((T, E), BF),
    dom=((2, T, E), BF),
    probs=((2, 2560, B), F32),
    mt=((E, T), BF),
    mixed=((T, E), BF),
    dqt=((E, T), F32),
    dk=((T, E), F32),
    dv=((T, E), F32),
    qkvg=((T, 3 * E), BF),
    op=((T, D), BF),
    ng=((T, D), BF),
    ctab=((T, E), F32),
    stab=((T, E), F32),
    ssend=((8, B), F32),
    srecv=((8, B), F32),
    g1=((F + E, D), BF),
    g2=((F, D), BF),
    g3=((3 * E, D), BF),
    vec=((8, D), F32),
    vr=((10, 8, D), F32),
    vs=((4, 8, D), F32),
)
def scatter_scratch(yr):
    zr = B - yr
    return dict(
        ta=((yr, D // 2), BF),
        tb=((yr, D // 2), BF),
        inl=((yr, D), BF),
        inr=((yr, D), BF),
        ry=((4, zr, D // 2), BF),
        ta2=((zr, D // 4), BF),
        tb2=((zr, D // 4), BF),
        inl2=((zr, D // 2), BF),
        inr2=((zr, D // 2), BF),
        ysend=((2, yr, D // 2), BF),
        yrecv=((yr, D // 2), BF),
    )


def reduce_scratch(n):
    return dict(
        rc=((n // 2, D), BF),
        ta=((n // 8, D // 2), BF),
        tb=((n // 8, D // 2), BF),
        inl=((n // 8, D), BF),
        inr=((n // 8, D), BF),
        sy=((2, n // 8, D // 2), BF),
        ry=((3, n // 8, D // 2), BF),
    )


ROWS = (F + E, F, 3 * E)
for name in "on":
    SCRATCH.update({name + "_" + key: v for key, v in scatter_scratch(YROWS[name]).items()})
for k, n in enumerate(ROWS):
    SCRATCH.update({f"r{k}_{key}": spec for key, spec in reduce_scratch(n).items()})


def under(s, prefix, **more):
    picked = {k[len(prefix) :]: v for k, v in vars(s).items() if k.startswith(prefix)}
    return SimpleNamespace(**picked, **more)


def body(
    tok, cot, wqkv, wout, wup, wdown, bqkv, bup, bout, bdown, gain, bias, seg, ctab_h, stab_h,
    out, tgrad, f0, f1, f2, vout, *scratch,
):
    s = SimpleNamespace(**dict(zip(SCRATCH, scratch)))
    send, recv = scratch[len(SCRATCH) :]
    net = Net(send, recv)
    dp, row, col = lax.axis_index("dp"), lax.axis_index("row"), lax.axis_index("col")
    core, x, yh = lax.rem(dp, 2), lax.rem(dp // 2, 4), dp // 8
    half = D // 2

    def dev(core=core, x=x, yh=yh, row=row, col=col):
        return (yh * 8 + x * 2 + core, row, col)

    at = {"core": dev(core=1 - core)}
    for k in (1, 2, 3):
        at[f"x{k}"] = dev(x=lax.rem(x + k, 4))
        at[f"z{k}"] = dev(col=lax.rem(col + k, 4))
    at["y1"] = dev(row=1 - row)
    at["y2"] = dev(yh=1 - yh)
    at["y3"] = dev(yh=1 - yh, row=1 - row)
    y1 = at["y1"]

    s.nbs[...] = jnp.concatenate(
        [gain[...].astype(F32), bias[...].astype(F32), jnp.zeros((4, half), F32)]
    )
    barrier = pltpu.get_barrier_semaphore()
    for device in at.values():
        pl.semaphore_signal(barrier, inc=1, device_id=device, device_id_type=MESH)
    pl.semaphore_wait(barrier, len(at))

    tasks, done = [], set()
    add = tasks.append
    gather_tokens(net, add, done, "x.", (), tok, s.xall, at, half, col, row, YROWS["x"])
    gather_tokens(net, add, done, "g.", ("x.r2!", "x.l2!"), cot, s.gall, at, half, col, row, YROWS["g"])
    nbc = net.go(s.nbs, s.nb.at[row], y1)
    gather_weights(net, add, done, wqkv, wup, wout, wdown, s, at, core, row)
    tabs = [net.local(ctab_h, s.ctab), net.local(stab_h, s.stab)]
    s.nb[row] = s.nbs[...]
    s.vec[...] = jnp.zeros_like(s.vec)
    s.dk[...] = jnp.zeros_like(s.dk)
    s.dv[...] = jnp.zeros_like(s.dv)

    def flat(values):
        values = values.astype(F32)
        return jnp.concatenate([values[k : k + 1, :] for k in range(values.shape[0])], axis=1)

    segr = flat(seg[...])
    s.segc[...] = jnp.broadcast_to(segr, (8, T)).T
    bq_all = bqkv[...].astype(F32)
    mine = row == 0
    bq = jnp.concatenate(
        [jnp.where(mine, bq_all[k : k + 1, :E], bq_all[k : k + 1, E:]) for k in range(3)], axis=1
    )
    bu_all = flat(bup[...])
    bu = jnp.where(mine, bu_all[:, :F], bu_all[:, F:])
    fcols = pl.ds(pl.multiple_of(row * F, F), F)
    gcols = pl.ds(pl.multiple_of(row * half, half), half)

    def wide(k):
        return jnp.concatenate([s.nb[0, k : k + 1, :], s.nb[1, k : k + 1, :]], axis=1)

    def params():
        yield (nbc,), 0.0
        nbc.wait_recv()
        for copy in tabs:
            copy.wait()
        done.add("nb")

    add(params())

    def norm(c):
        gain0, gain1, bias0, bias1 = wide(0), wide(1), wide(2), wide(3)

        @pl.loop(0, 2)
        def _(b):
            r = rows(c * 2 + b, 128)
            xv = s.xall[r, :].astype(F32)
            mean = jnp.sum(xv, axis=1, keepdims=True) * (1.0 / D)
            square = jnp.sum(xv * xv, axis=1, keepdims=True) * (1.0 / D)
            inv = lax.rsqrt(square - mean * mean + EPSILON)
            normed = (xv - mean) * inv
            s.mean[r, :] = mean
            s.inv[r, :] = inv
            s.ain[r, :] = (normed * gain0 + bias0).astype(BF)
            s.mim[r, :] = (normed * gain1 + bias1).astype(BF)

    def project(c):
        r = rows(c)
        pre = nn(s.ain[r, :], s.wq[...]) + bq
        cos, sin = s.ctab[r, :], s.stab[r, :]
        query = (turn(pre[:, :E], cos, sin)).astype(BF).astype(F32) * (1.0 / math.sqrt(HD))
        key = turn(pre[:, E : 2 * E], cos, sin).astype(BF).astype(F32)
        value = pre[:, 2 * E :].astype(BF).astype(F32)
        s.qs[r, :] = query.astype(BF)
        split_heads(s.qsm, r, query)
        split_heads(s.km, r, key)
        split_heads(s.vm, r, value)
        s.kt[:, r] = key.T.astype(BF)
        s.vt[:, r] = value.T.astype(BF)

    def expand(c):
        r = rows(c)
        pre = nn(s.mim[r, :], s.wu[...]) + bu
        cdf = 0.5 * (1.0 + lax.erf(pre * math.sqrt(0.5)))
        s.hid[r, :] = (pre * cdf).astype(BF)
        s.slope[r, :] = cdf + pre * jnp.exp(-0.5 * pre * pre) * (1.0 / math.sqrt(2.0 * math.pi))

    def contract(c):
        r = rows(c)
        back = (nt(s.gall[r, :], s.wd[...]) * s.slope[r, :]).astype(BF)
        s.hpg[r, :] = back
        s.vec[6:7, fcols] += jnp.sum(back.astype(F32), axis=0, keepdims=True)
        s.vec[4:5, gcols] += jnp.sum(s.gall[r, gcols].astype(F32), axis=0, keepdims=True)
        dout = nt(s.gall[r, :], s.wo[...]).astype(BF).astype(F32)
        s.do[r, :] = dout.astype(BF)
        split_heads(s.dom, r, dout)

    rb, lb, fb = lax.rem(col + 1, 4), lax.rem(col + 3, 4), lax.rem(col + 2, 4)
    blocks = {"own": col, "left": lb, "right": rb, "far": fb}
    outward = ("far", "right", "left", "own")

    def mark(flag, work, *args):
        def both():
            work(*args)
            done.add(flag)

        return both

    first = [0, 256, 768, 1536]

    def attend(i):
        n = (i + 1) * B
        q = pl.ds(i * B, B)

        @pl.loop(0, 2)
        def _(h):
            scores = nt(s.km[h, pl.ds(0, n), :], s.qs[q, :])
            kid = lax.broadcasted_iota(jnp.int32, (n, B), 0)
            qid = lax.broadcasted_iota(jnp.int32, (n, B), 1) + i * B
            allowed = (kid <= qid) & (s.segc[pl.ds(0, n), 0:1] == segr[:, i * B : (i + 1) * B])
            scores = jnp.where(allowed, scores, -1e30)
            top = jnp.max(scores, axis=0, keepdims=True)
            expo = jnp.exp(scores - top)
            probs = expo * (1.0 / jnp.sum(expo, axis=0, keepdims=True))
            s.probs[h, pl.ds(first[i], n), :] = probs
            hrows = rows(h, HD)
            s.mt[hrows, q] = nn(s.vt[hrows, pl.ds(0, n)], probs.astype(BF)).astype(BF)

        s.mixed[q, :] = s.mt[:, q].astype(F32).T.astype(BF)

    def attend_back(i):
        n = (i + 1) * B
        q = pl.ds(i * B, B)

        @pl.loop(0, 2)
        def _(h):
            probs = s.probs[h, pl.ds(first[i], n), :]
            dprob = nt(s.vm[h, pl.ds(0, n), :], s.do[q, :])
            inner = jnp.sum(probs * dprob, axis=0, keepdims=True)
            dscore = (probs * (dprob - inner)).astype(BF)
            s.dv[pl.ds(0, n), :] += nn(probs.astype(BF), s.dom[h, q, :])
            s.dk[pl.ds(0, n), :] += nn(dscore, s.qsm[h, q, :])
            hrows = rows(h, HD)
            s.dqt[hrows, q] = nn(s.kt[hrows, pl.ds(0, n)], dscore) * (1.0 / math.sqrt(HD))

    def branch(b):
        r = rows(b)
        s.op[r, :] = (nn(s.mixed[r, :], s.wo[...]) + nn(s.hid[r, :], s.wd[...])).astype(BF)

    def down_grad():
        @pl.loop(0, 4)
        def _(b):
            r = rows(b, 128)
            s.g1[r, :] = tn(s.hid[:, r], s.gall[...]).astype(BF)

        s.g1[F:, :] = nn(s.mt[...], s.gall[...]).astype(BF)

    def up_grad():
        @pl.loop(0, 4)
        def _(b):
            r = rows(b, 128)
            s.g2[r, :] = tn(s.hpg[:, r], s.mim[...]).astype(BF)

    def qkv_grad(b):
        r = rows(b)
        cos, sin = s.ctab[r, :], -s.stab[r, :]
        dq = turn(s.dqt[:, r].T, cos, sin).astype(BF)
        dk = turn(s.dk[r, :], cos, sin).astype(BF)
        dv = s.dv[r, :].astype(BF)
        both = jnp.concatenate([dq, dk, dv], axis=1)
        s.qkvg[r, :] = both
        ecols3 = pl.ds(pl.multiple_of(row * 3 * E, 3 * E), 3 * E)
        s.vec[5:6, ecols3] += jnp.sum(both.astype(F32), axis=0, keepdims=True)

    def qkv_weight_grad():
        @pl.loop(0, 3)
        def _(b):
            r = rows(b, E)
            s.g3[r, :] = tn(s.qkvg[:, r], s.ain[...]).astype(BF)

    def input_grad(b):
        r = rows(b)
        gain0, gain1 = wide(0), wide(1)
        attn = nt(s.qkvg[r, :], s.wq[...])
        mlp = nt(s.hpg[r, :], s.wu[...])
        normed = (s.xall[r, :].astype(F32) - s.mean[r, :]) * s.inv[r, :]
        s.ng[r, :] = (attn * gain0 + mlp * gain1).astype(BF)
        s.vec[0:1, :] += jnp.sum(attn * normed, axis=0, keepdims=True)
        s.vec[1:2, :] += jnp.sum(mlp * normed, axis=0, keepdims=True)
        s.vec[2:3, :] += jnp.sum(attn, axis=0, keepdims=True)
        s.vec[3:4, :] += jnp.sum(mlp, axis=0, keepdims=True)

    so, sn = under(s, "o_"), under(s, "n_")
    where = dict(core=core, x=x, row=row)
    sums = []
    ny = YROWS["n"]
    own = rows(col)

    def look(h, total):
        mean, inv = s.mean[own, :], s.inv[own, :]
        xv = s.xall[pl.ds(pl.multiple_of(col * B, B), ny), pl.ds(h * half, half)].astype(F32)
        normed = (xv - mean[:ny]) * inv[:ny]
        sums.append(jnp.sum(total, axis=1, keepdims=True))
        sums.append(jnp.sum(total * normed, axis=1, keepdims=True))

    def write_out():
        xv = s.xall[own, gcols].astype(F32) + (flat(bout[...]) + flat(bdown[...]))
        total = jnp.concatenate([total_y(so, row), total_z(s.op, so, col, row, YROWS["o"])])
        out[...] = (xv + total).astype(BF)

    def write_grad():
        yield ("n.y.sum", "n.y.end", "n.z.sum"), 0.4
        mean, inv = s.mean[own, :], s.inv[own, :]
        normed = (s.xall[own, gcols].astype(F32) - mean) * inv
        zsum = total_z(s.ng, sn, col, row, ny)
        first_sum = jnp.concatenate([sums[0] + sums[2], jnp.sum(zsum, axis=1, keepdims=True)])
        second = jnp.sum(zsum * normed[ny:], axis=1, keepdims=True)
        second_sum = jnp.concatenate([sums[1] + sums[3], second])
        lane = lax.broadcasted_iota(jnp.int32, (B, 128), 1)
        s.ssend[...] = jnp.where(lane < 4, first_sum, second_sum).T[:8, :]
        ys = net.go(s.ssend, s.srecv, y1)
        yield (ys,), 0.5
        ys.wait_recv()
        both = (s.ssend[...] + s.srecv[...]) * (1.0 / D)
        both = jnp.concatenate([both] * 16).T
        total = jnp.concatenate([total_y(sn, row), zsum])
        tgrad[...] = (
            s.gall[own, gcols].astype(F32) + inv * (total - both[:, 0:1] - normed * both[:, 4:5])
        ).astype(BF)

    def write_vectors():
        vout[0] = s.vs[2]
        vout[1] = s.vs[3]

    scatter(net, add, done, "o.", tuple("send." + b for b in outward), s.op, so, at, col, row, YROWS["o"])
    scatter(net, add, done, "n.", tuple("ng." + b for b in outward), s.ng, sn, at, col, row, ny, look)
    for b in outward:
        add(later(("op." + b, "g.far"), 0.0, mark("send." + b, lambda: None)))
    reduce_weights(net, add, done, "a.", "g1", s.g1, under(s, "r0_", fin=f0), at, where, ROWS[0])
    reduce_weights(net, add, done, "b.", "g2", s.g2, under(s, "r1_", fin=f1), at, where, ROWS[1])
    reduce_weights(net, add, done, "c.", "g3", s.g3, under(s, "r2_", fin=f2), at, where, ROWS[2])
    add(reduce_vectors(net, done, s, at))
    add(later(("vsum",), 0.05, write_vectors))
    add(write_grad())
    for name, b in blocks.items():
        add(later(("nb", "x." + name), 0.28, mark("norm." + name, norm, b)))
        add(later(("wq", "norm." + name), 0.63, mark("proj." + name, project, b)))
    needs = tuple("proj." + name for name in blocks)
    for i in range(4):
        add(later(needs, 0.58 * (i + 1), mark(f"attf{i}", attend, i)))
        needs = (f"attf{i}",)
    for name, b in blocks.items():
        add(later(("wu", "norm." + name), 0.55, mark("exp." + name, expand, b)))
    for name in outward:
        needs = ("wo", "wd", "attf3", "exp." + name)
        add(later(needs, 0.7, mark("op." + name, branch, blocks[name])))
    for name, b in blocks.items():
        needs = ("wo", "wd", "g." + name, "exp." + name)
        add(later(needs, 0.4, mark("con." + name, contract, b)))
    allg = tuple("g." + name for name in blocks) + tuple("exp." + name for name in blocks)
    add(later(allg + ("attf3",), 1.85, mark("g1", down_grad)))
    allc = tuple("con." + name for name in blocks)
    add(later(allc, 1.65, mark("g2", up_grad)))
    needs = allc + ("attf3",)
    for i in range(4):
        add(later(needs, 0.6 * (i + 1), mark(f"attb{i}", attend_back, i)))
        needs = (f"attb{i}",)
    for name in outward:
        add(later(("attb3",), 0.46, mark("qg." + name, qkv_grad, blocks[name])))
    for name in outward:
        add(later(("qg." + name,), 0.65, mark("ng." + name, input_grad, blocks[name])))
    add(later(tuple("qg." + name for name in blocks), 1.75, mark("g3", qkv_weight_grad)))
    add(later(tuple("ng." + name for name in blocks), 0.0, mark("vec", lambda: None)))
    add(later(("o.y.end", "o.z.sum"), 0.3, mark("out", write_out)))
    run(tasks, done)
    for copy in net.sent:
        copy.wait_send()


def tables():
    freq = np.arange(ROT // 2, dtype=np.float32)
    inverse = np.float32(10000.0) ** (np.float32(-2.0) * freq / np.float32(ROT))
    angle = np.arange(T, dtype=np.float32)[:, None] * inverse[None, :].astype(np.float32)
    cos, sin = np.cos(angle), np.sin(angle)
    ones, zeros = np.ones((T, HD - ROT), np.float32), np.zeros((T, HD - ROT), np.float32)
    ctab = np.concatenate([cos, cos, ones] * 2, axis=1)
    stab = np.concatenate([-sin, sin, zeros] * 2, axis=1)
    return ctab.astype(np.float32), stab.astype(np.float32)


def last(
    f0_h, f1_h, f2_h, vec_h, out_h, tgrad_h,
    out_o, tgrad_o, wq_o, bq_o, wo_o, bo_o, wu_o, bu_o, wd_o, bd_o, gain_o, bias_o,
    f0, f1, f2, vec, out, tgrad, wq, wo, wu, wd, sems,
):
    row = lax.axis_index("row")
    copies = []

    def write(src, dst):
        copy = pltpu.make_async_copy(src, dst, sems.at[len(copies)])
        copy.start()
        copies.append(copy)
        return copy

    pairs = ((f0_h, f0), (f1_h, f1), (f2_h, f2), (vec_h, vec), (out_h, out), (tgrad_h, tgrad))
    reads = [write(a, b) for a, b in pairs]
    reads[0].wait()
    for r in range(2):
        for k in range(8):
            piece = f0[k // 4, k % 4, r].astype(F32)
            n = piece.shape[0]
            inside = max(0, min(n, F - k * n))
            if inside:
                wd[pl.ds(r * F + k * n, inside), :] = piece[:inside]
            if inside < n:
                wo[pl.ds(r * E + k * n + inside - F, n - inside), :] = piece[inside:]
        write(wd.at[pl.ds(r * F, F)], wd_o.at[pl.ds(r * F, F)])
    write(wo, wo_o)
    reads[1].wait()
    for r in range(2):
        for k in range(4):
            pair = [f1[(2 * k + h) // 4, (2 * k + h) % 4, r].astype(F32) for h in range(2)]
            wu[:, pl.ds(r * F + k * E, E)] = jnp.concatenate(pair).T
        write(wu.at[:, pl.ds(r * F, F)], wu_o.at[:, pl.ds(r * F, F)])
    reads[2].wait()
    for r in range(2):
        whole = jnp.concatenate([f2[k // 4, k % 4, r].astype(F32) for k in range(8)])
        for k in range(3):
            wq[k, :, pl.ds(r * E, E)] = whole[k * E : (k + 1) * E].T
    write(wq, wq_o)
    for copy in reads[3:]:
        copy.wait()
    write(out, out_o)
    write(tgrad, tgrad_o)
    half = D // 2
    left = row == 0

    def cut(values):
        return jnp.where(left, values[:, :half], values[:, half:])

    bo_o[...] = cut(vec[0, 4:5, :])
    bd_o[...] = cut(vec[0, 4:5, :])
    for k in range(3):
        bq_o[k : k + 1, :E] = vec[0, 5:6, k * E : (k + 1) * E]
        bq_o[k : k + 1, E:] = vec[0, 5:6, (k + 3) * E : (k + 4) * E]
    bu_o[...] = vec[0, 6:7, :]
    gain_o[...] = cut(vec[1, 0:2, :])
    bias_o[...] = cut(vec[1, 2:4, :])
    for copy in copies[len(reads) :]:
        copy.wait()


def on_device(
    tokens, segment_ids, w_qkv, b_qkv, w_out, b_out, w_up, b_up, w_down, b_down, norm_gain, norm_bias, cotangent
):
    ctab, stab = tables()
    vmem = pl.BlockSpec(memory_space=pltpu.VMEM)
    hbm = pl.BlockSpec(memory_space=pl.ANY)
    shape = jax.ShapeDtypeStruct
    early = [
        shape((2, 4, 2, ROWS[0] // 8, D // 2), BF),
        shape((2, 4, 2, ROWS[1] // 8, D // 2), BF),
        shape((2, 4, 2, ROWS[2] // 8, D // 2), BF),
        shape((2, 8, D), F32),
    ]
    out, tgrad, f0, f1, f2, vec = pl.pallas_call(
        body,
        out_shape=[
            shape((B, D // 2), BF),
            shape((B, D // 2), BF),
            *early,
        ],
        in_specs=[hbm] * 6 + [vmem] * 7 + [hbm] * 2,
        out_specs=[vmem] * 6,
        scratch_shapes=[pltpu.VMEM(*spec) for spec in SCRATCH.values()]
        + [pltpu.SemaphoreType.DMA((NSEM,)), pltpu.SemaphoreType.DMA((NSEM,))],
        compiler_params=pltpu.CompilerParams(
            collective_id=0, has_side_effects=True, vmem_limit_bytes=60 * 1024 * 1024
        ),
        name="block",
    )(
        tokens, cotangent, w_qkv, w_out, w_up, w_down, b_qkv, b_up.reshape(8, 128),
        b_out.reshape(4, 128), b_down.reshape(4, 128), norm_gain, norm_bias,
        segment_ids.reshape(8, 128), jnp.asarray(ctab), jnp.asarray(stab),
    )
    big = [
        ((3, D // 2, 2 * E), F32),
        ((2 * E, D // 2), F32),
        ((D // 2, 2 * F), F32),
        ((2 * F, D // 2), F32),
    ]
    results = pl.pallas_call(
        last,
        out_shape=[
            shape((B, D // 2), BF),
            shape((B, D // 2), BF),
            shape(*big[0]),
            shape((3, 2 * E), F32),
            shape(*big[1]),
            shape((1, D // 2), F32),
            shape(*big[2]),
            shape((1, 2 * F), F32),
            shape(*big[3]),
            shape((1, D // 2), F32),
            shape((2, D // 2), F32),
            shape((2, D // 2), F32),
        ],
        in_specs=[hbm] * 6,
        out_specs=[hbm, hbm, hbm, vmem, hbm, vmem, hbm, vmem, hbm, vmem, vmem, vmem],
        scratch_shapes=[pltpu.VMEM(e.shape, e.dtype) for e in early]
        + [pltpu.VMEM((B, D // 2), BF)] * 2
        + [pltpu.VMEM(*spec) for spec in big]
        + [pltpu.SemaphoreType.DMA((16,))],
        compiler_params=pltpu.CompilerParams(vmem_limit_bytes=60 * 1024 * 1024),
        name="last",
    )(f0, f1, f2, vec, out, tgrad)
    out, tgrad, wq, bq, wo, bo, wu, bu, wd, bd, gain, bias = results
    bo, bu, bd = bo.reshape(-1), bu.reshape(-1), bd.reshape(-1)
    return (out, tgrad, wq, bq, wo, bo, wu, bu, wd, bd, gain, bias)


def solution(mesh):
    in_specs = (
        P(("dp", "col"), "row"),
        P("dp"),
        P(None, "row", "col"),
        P(None, "col"),
        P("col", "row"),
        P("row"),
        P("row", "col"),
        P("col"),
        P("col", "row"),
        P("row"),
        P(None, "row"),
        P(None, "row"),
        P(("dp", "col"), "row"),
    )
    out_specs = (
        P(("dp", "col"), "row"),
        P(("dp", "col"), "row"),
        P(None, "row", "col"),
        P(None, "col"),
        P("col", "row"),
        P("row"),
        P("row", "col"),
        P("col"),
        P("col", "row"),
        P("row"),
        P(None, "row"),
        P(None, "row"),
    )
    return jax.shard_map(
        on_device, mesh=mesh, in_specs=in_specs, out_specs=out_specs, check_vma=False
    )
```

```python
from types import SimpleNamespace
import math

import numpy as np
import jax
import jax.numpy as jnp
from jax import lax
from jax.experimental import pallas as pl
from jax.experimental.pallas import tpu as pltpu
from jax.sharding import PartitionSpec as P

MESH = pl.DeviceIdType.MESH
BF = jnp.bfloat16
F32 = jnp.float32
T = 1024
D = 1024
HD = 64
ROT = 16
E = 128
F = 512
B = 256
EPSILON = 1e-05
NSEM = 200
YROWS = dict(x=112, g=144, o=160, n=208)


ORDER = (
    0, 1, 2, 3, 4, 5, 8, 9, 44, 2, 6, 10, 3, 4, 7, 11, 12, 40, 5, 9, 13, 8, 16, 128, 40, 129, 6, 14,
    10, 21, 25, 24, 29, 23, 11, 17, 130, 131, 41, 7, 20, 22, 28, 15, 42, 13, 12, 18, 132, 14, 41,
    141, 42, 140, 142, 133, 24, 32, 23, 27, 31, 15, 19, 134, 135, 143, 43, 136, 137, 22, 25, 26, 33,
    30, 29, 138, 43, 27, 35, 139, 28, 36, 144, 26, 32, 34, 38, 30, 79, 45, 49, 150, 145, 80, 50, 46,
    52, 146, 81, 47, 51, 53, 31, 37, 147, 33, 82, 48, 148, 149, 35, 34, 39, 152, 45, 55, 52, 83,
    151, 153, 46, 53, 54, 56, 97, 58, 154, 155, 47, 57, 58, 59, 83, 84, 85, 86, 87, 88, 156, 48, 59,
    60, 97, 99, 100, 98, 101, 102, 157, 54, 87, 88, 89, 61, 158, 159, 60, 160, 161, 162, 111, 101,
    102, 103, 163, 66, 89, 90, 62, 165, 61, 64, 70, 68, 166, 65, 111, 112, 116, 114, 115, 113, 168,
    103, 104, 164, 67, 69, 63, 167, 125, 116, 115, 117, 125, 90, 91, 92, 69, 70, 71, 62, 72, 64, 74,
    76, 117, 118, 65, 125, 91, 93, 104, 105, 106, 92, 94, 95, 63, 75, 73, 93, 94, 118, 119, 120,
    106, 108, 71, 78, 105, 107, 109, 76, 75, 77, 108, 125, 107, 95, 96, 119, 121, 77, 120, 123, 122,
    121, 96, 122, 125, 126, 109, 110, 78, 127, 123, 124, 110, 127, 124,
)


def nn(a, b):
    return jnp.dot(a, b, preferred_element_type=F32)


def nt(a, b):
    return lax.dot_general(a, b, (((1,), (1,)), ((), ())), preferred_element_type=F32)


def tn(a, b):
    return lax.dot_general(a, b, (((0,), (0,)), ((), ())), preferred_element_type=F32)


def rows(block, size=B):
    return pl.ds(pl.multiple_of(block * size, size), size)


class Net:
    def __init__(self, send, recv):
        self.send, self.recv, self.count, self.sent = send, recv, 0, []

    def go(self, src, dst, device):
        k = self.count
        self.count += 1
        assert k < NSEM
        copy = pltpu.make_async_remote_copy(
            src_ref=src,
            dst_ref=dst,
            send_sem=self.send.at[k],
            recv_sem=self.recv.at[k],
            device_id=device,
            device_id_type=MESH,
        )
        copy.start()
        self.sent.append(copy)
        return copy

    def local(self, src, dst):
        k = self.count
        self.count += 1
        assert k < NSEM
        copy = pltpu.make_async_copy(src, dst, self.send.at[k])
        copy.start()
        return copy


def later(deps, cost, work):
    yield deps, cost
    work()


def gather_tokens(net, add, done, name, begin, own, full, at, half, col, row, yr):
    right, left, peer = at["z1"], at["z3"], at["y1"]
    zr = B - yr
    part = zr // 32 * 16
    cut = yr + part
    c = {}

    def place(b, h, start=0, size=B):
        r = pl.ds(pl.multiple_of(b * B + start, 16), size)
        return full.at[r, pl.ds(pl.multiple_of(h * half, half), half)]

    def move(key, device, *where):
        c[key] = net.go(place(*where), place(*where), device)
        done.add(name + key)

    def send(key, device, start, size):
        c[key] = net.go(own.at[pl.ds(start, size)], place(col, row, start, size), device)
        done.add(name + key)

    lcol, rcol, fcol = lax.rem(col + 3, 4), lax.rem(col + 1, 4), lax.rem(col + 2, 4)

    def begin_y():
        yield begin[0], 0.1
        c["keep"] = net.local(own, place(col, row))
        send("p0", peer, 0, yr)
        send("p1", peer, yr, zr)
        c["keep"].wait()
        done.add(name + "keep")

    def begin_z():
        yield begin[1], 0.1
        send("r1", right, yr, zr)
        send("l1", left, yr, zr)
        send("r0", right, 0, yr)
        send("l0", left, 0, yr)

    def hop(keys, *work):
        yield tuple(name + k for k in keys), 0.0
        yield tuple(c[k] for k in keys), 0.05
        for k in keys:
            c[k].wait_recv()
        for w in work:
            move(*w)
        done.update(name + k + "!" for k in keys)

    def whole(flag, keys):
        yield tuple(name + k + ("" if k == "keep" else "!") for k in keys), 0.0
        done.add(name + flag)

    add(begin_y())
    add(begin_z())
    add(hop(["p0"], ("r2", right, col, 1 - row, 0, yr), ("l2", left, col, 1 - row, 0, yr)))
    add(hop(["r1"], ("r3", right, lcol, row, yr, part), ("p2", peer, lcol, row, yr, zr)))
    add(hop(["l1"], ("l3", left, rcol, row, cut, B - cut), ("p3", peer, rcol, row, yr, zr)))
    add(hop(["r0"], ("r4", right, lcol, row, 0, yr)))
    add(hop(["l2"], ("l4", left, rcol, 1 - row, 0, yr)))
    add(hop(["r3", "l3"], ("p4", peer, fcol, row, yr, zr)))
    add(hop(["p1"]))
    add(hop(["l0"]))
    add(hop(["r2"]))
    add(hop(["p2"]))
    add(hop(["p3"]))
    add(hop(["r4"]))
    add(hop(["l4"]))
    add(hop(["p4"]))
    add(whole("own", ["p0", "p1", "keep"]))
    add(whole("left", ["r0", "r1", "r2", "p2"]))
    add(whole("right", ["l0", "l1", "l2", "p3"]))
    add(whole("far", ["r3", "r4", "l3", "l4", "p4"]))


def gather_weights(net, add, done, wqkv, wup, wout, wdown, s, at, core, row):
    half, part = D // 2, D // 4
    mine, theirs = row, 1 - row
    drows, ocols = rows(row, half), rows(1 - row, half)

    def cut(which, size):
        return pl.ds(pl.multiple_of(which * size, size), size)

    local = {}
    for k in range(3):
        kcols = pl.ds(k * E, E)
        local[k] = net.local(wqkv.at[k, :, cut(mine, E)], s.wq.at[drows, kcols])
    local["u"] = net.local(wup.at[:, cut(mine, F)], s.wu.at[drows])
    local["o"] = net.local(wout.at[cut(mine, E)], s.wo.at[:, drows])
    local["d"] = net.local(wdown.at[cut(mine, F)], s.wd.at[:, drows])
    src, dst, got = cut(core, part), cut(row * 2 + core, part), cut((1 - row) * 2 + core, part)
    far, near = at["y3"], at["core"]
    q = [
        net.go(wqkv.at[k, src, cut(theirs, E)], s.wq.at[dst, pl.ds(k * E, E)], far)
        for k in range(3)
    ]
    u = net.go(wup.at[src, cut(theirs, F)], s.wu.at[dst], far)
    o = net.go(wout.at[cut(theirs * 2 + core, E // 2)], s.wo.at[cut(core, E // 2), drows], far)
    d = net.go(wdown.at[cut(theirs * 2 + core, F // 2)], s.wd.at[cut(core, F // 2), drows], far)

    def share(flag, copies, view, locals_):
        yield tuple(copies), 0.05
        for copy in copies:
            copy.wait_recv()
        second = net.go(view, view, near)
        yield (second,), 0.0
        second.wait_recv()
        for k in locals_:
            local[k].wait()
        done.add(flag)

    add(share("wq", q, s.wq.at[got], range(3)))
    add(share("wu", [u], s.wu.at[got], "u"))
    add(share("wo", [o], s.wo.at[cut(core, E // 2), ocols], "o"))
    add(share("wd", [d], s.wd.at[cut(core, F // 2), ocols], "d"))


def ring_scatter(net, add, done, name, part, bufs, me, right, left, width, ready):
    ta, tb, inl, inr = bufs
    lo, hi = pl.ds(0, width), pl.ds(width, width)
    far, rb, lb = lax.rem(me + 2, 4), lax.rem(me + 1, 4), lax.rem(me + 3, 4)
    c = {}

    def send(deps, *sends):
        yield deps, 0.05
        for key, src, dst, device in sends:
            c[key] = net.go(src, dst, device)
            done.add(name + key)

    def through(came, flag, buf, view, key, dst, device):
        yield (name + came, flag), 0.0
        yield (c[came],), 0.15
        c[came].wait_recv()
        view[...] = (view[...].astype(F32) + buf[...].astype(F32)).astype(BF)
        c[key] = net.go(view, dst, device)
        done.add(name + key)

    def finish():
        yield tuple(name + k for k in "cdef") + (ready[3],), 0.0
        yield tuple(c[k] for k in "cdef"), 0.0
        for k in "cdef":
            c[k].wait_recv()
        done.add(name + "sum")

    add(send((ready[0],), ("a", part(far, lo), ta, right), ("b", part(far, hi), tb, left)))
    add(send((ready[1],), ("c", part(rb, hi), inl.at[:, hi], right)))
    add(send((ready[2],), ("d", part(lb, lo), inr.at[:, lo], left)))
    add(through("a", ready[1], ta, part(rb, lo), "e", inl.at[:, lo], right))
    add(through("b", ready[2], tb, part(lb, hi), "f", inr.at[:, hi], left))
    add(finish())


def reduce_weights(net, add, done, name, begin, grad, s, at, me, n):
    core, x, row = me["core"], me["x"], me["row"]
    half, size = n // 2, n // 8
    base, away = core * half, (1 - core) * half
    x1, x3, near = at["x1"], at["x3"], at["core"]
    lx, rx, fx = lax.rem(x + 3, 4), lax.rem(x + 1, 4), lax.rem(x + 2, 4)
    c = {}

    def start():
        yield (begin,), 0.05
        copy = net.go(grad.at[pl.ds(pl.multiple_of(away, half), half)], s.rc, near)
        yield (copy,), 0.4 * n / 640
        copy.wait_recv()
        own = grad.at[pl.ds(pl.multiple_of(base, half), half)]
        own[...] = (own[...].astype(F32) + s.rc[...].astype(F32)).astype(BF)
        done.add(name + "core")

    def part(block, cols):
        return grad.at[pl.ds(pl.multiple_of(base + block * size, size), size), cols]

    def across():
        yield (name + "sum",), 0.2
        for h in range(2):
            cols = pl.ds(h * (D // 2), D // 2)
            total = part(x, cols)[...].astype(F32) + s.inl[:, cols].astype(F32)
            s.sy[h] = (total + s.inr[:, cols].astype(F32)).astype(BF)
        g0 = net.go(s.sy.at[row], s.ry.at[0], at["y2"])
        g1 = net.go(s.sy.at[1 - row], s.ry.at[1], at["y1"])
        g2 = net.go(s.sy.at[1 - row], s.ry.at[2], at["y3"])
        yield (g0, g1, g2), 0.15
        for copy in (g0, g1, g2):
            copy.wait_recv()
        s.fin[core, x, row] = (s.sy[row].astype(F32) + s.ry[0].astype(F32)).astype(BF)
        s.fin[core, x, 1 - row] = (s.ry[1].astype(F32) + s.ry[2].astype(F32)).astype(BF)
        for key, h, device in (("a", 0, x1), ("b", 1, x3), ("c", 1, x1), ("d", 0, x3)):
            view = s.fin.at[core, x, h]
            c[key] = net.go(view, view, device)
        view = s.fin.at[core, x]
        c["k"] = net.go(view, view, near)
        done.add(name + "sent")

    def hop(keys, flag, view, device, key, need=()):
        yield (name + flag,) + tuple(name + k + "!" for k in need), 0.0
        yield tuple(c[k] for k in keys), 0.05
        for k in keys:
            c[k].wait_recv()
        c[key] = net.go(view, view, device)
        done.update(name + k + "!" for k in keys)
        done.add(name + key)

    def end():
        yield tuple(name + k for k in ("l", "m", "n")), 0.0
        yield tuple(c[k] for k in "klmn"), 0.0
        for k in "klmn":
            c[k].wait_recv()
        done.add(name + "end")

    ready = (name + "core",) * 4
    add(start())
    ring_scatter(
        net, add, done, name, part, (s.ta, s.tb, s.inl, s.inr), x, x1, x3, D // 2, ready
    )
    add(across())
    add(hop("a", "sent", s.fin.at[core, lx, 0], x1, "p"))
    add(hop("b", "sent", s.fin.at[core, rx, 1], x3, "q"))
    add(hop("c", "sent", s.fin.at[core, lx], near, "l", "a"))
    add(hop("d", "sent", s.fin.at[core, rx], near, "m", "b"))
    add(hop("pq", "p", s.fin.at[core, fx], near, "n", "b"))
    add(end())


def reduce_vectors(net, done, s, at):
    yield ("vec",), 0.0
    c = net.go(s.vec, s.vr.at[0], at["core"])
    yield (c,), 0.05
    c.wait_recv()
    s.vs[0] = s.vec[...] + s.vr[0]
    for n, axis in enumerate("xyz"):
        copies = [net.go(s.vs.at[n], s.vr.at[3 * n + k], at[axis + str(k)]) for k in (1, 2, 3)]
        yield tuple(copies), 0.05
        for copy in copies:
            copy.wait_recv()
        s.vs[n + 1] = (s.vs[n] + s.vr[3 * n + 1]) + (s.vr[3 * n + 2] + s.vr[3 * n + 3])
    done.add("vsum")


def scatter(net, add, done, name, ready, p, s, at, col, row, yr, look=None):
    half, zr = D // 2, B - yr
    far, rb, lb = lax.rem(col + 2, 4), lax.rem(col + 1, 4), lax.rem(col + 3, 4)
    mcols, ocols = rows(row, half), rows(1 - row, half)
    right, left, peer = at["z1"], at["z3"], at["y1"]

    def yrows(b):
        return pl.ds(pl.multiple_of(b * B, B), yr)

    def zrows(b):
        return pl.ds(pl.multiple_of(b * B + yr, 16), zr)

    def zpart(b, cols):
        return p.at[zrows(b), pl.ds(pl.multiple_of(row * half + cols.start, 256), cols.size)]

    def pair(k, b):
        yield (ready[k],), 0.05
        copy = net.go(p.at[zrows(b), ocols], s.ry.at[k], peer)
        yield (copy,), 0.15
        copy.wait_recv()
        view = p.at[zrows(b), mcols]
        view[...] = (view[...].astype(F32) + s.ry[k].astype(F32)).astype(BF)
        done.add(name + "z" + str(k))

    def last():
        yield (name + "y.sum",), 0.3
        for h in range(2):
            cols = pl.ds(h * half, half)
            total = p[yrows(col), cols].astype(F32) + s.inl[:, cols].astype(F32)
            total += s.inr[:, cols].astype(F32)
            s.ysend[h] = total.astype(BF)
            if look is not None:
                look(h, total)
        copy = net.go(s.ysend.at[1 - row], s.yrecv, peer)
        yield (copy,), 0.0
        copy.wait_recv()
        done.add(name + "y.end")

    for k, b in enumerate((far, rb, lb, col)):
        add(pair(k, b))
    ring_scatter(
        net, add, done, name + "y.", lambda b, cols: p.at[yrows(b), cols],
        (s.ta, s.tb, s.inl, s.inr), col, right, left, half, ready,
    )
    ring_scatter(
        net, add, done, name + "z.", zpart,
        (s.ta2, s.tb2, s.inl2, s.inr2), col, right, left, half // 2,
        tuple(name + "z" + str(k) for k in range(4)),
    )
    add(last())


def total_y(s, row):
    return s.ysend[row].astype(F32) + s.yrecv[...].astype(F32)


def total_z(p, s, col, row, yr):
    own = p[pl.ds(pl.multiple_of(col * B + yr, 16), B - yr), rows(row, D // 2)]
    return own.astype(F32) + s.inl2[...].astype(F32) + s.inr2[...].astype(F32)


def run(tasks, done):
    asked = [next(task)[0] for task in tasks]
    for k in ORDER:
        for need in asked[k]:
            assert not isinstance(need, str) or need in done, "order"
        asked[k] = next(tasks[k], ((),))[0]
    assert all(next(task, None) is None for task in tasks), "unfinished"


def turn(values, cos, sin):
    lane = lax.broadcasted_iota(jnp.int32, values.shape, 1)
    other = jnp.where(lane % HD < ROT // 2, pltpu.roll(values, E - ROT // 2, 1), pltpu.roll(values, ROT // 2, 1))
    return values * cos + other * sin


def split_heads(ref, at_rows, values):
    lane = lax.broadcasted_iota(jnp.int32, values.shape, 1)
    zero = jnp.zeros_like(values)
    ref[0, at_rows, :] = jnp.where(lane < HD, values, zero).astype(BF)
    ref[1, at_rows, :] = jnp.where(lane < HD, zero, values).astype(BF)


SCRATCH = dict(
    xall=((T, D), BF),
    gall=((T, D), BF),
    ain=((T, D), BF),
    mim=((T, D), BF),
    wq=((D, 3 * E), BF),
    wo=((E, D), BF),
    wu=((D, F), BF),
    wd=((F, D), BF),
    nb=((2, 8, D // 2), F32),
    mean=((T, 1), F32),
    inv=((T, 1), F32),
    hid=((T, F), BF),
    slope=((T, F), F32),
    segc=((T, 8), F32),
    nbs=((8, D // 2), F32),
    hpg=((T, F), BF),
    qs=((T, E), BF),
    qsm=((2, T, E), BF),
    km=((2, T, E), BF),
    vm=((2, T, E), BF),
    kt=((E, T), BF),
    vt=((E, T), BF),
    do=((T, E), BF),
    dom=((2, T, E), BF),
    probs=((2, 2560, B), F32),
    mt=((E, T), BF),
    mixed=((T, E), BF),
    dqt=((E, T), F32),
    dk=((T, E), F32),
    dv=((T, E), F32),
    qkvg=((T, 3 * E), BF),
    op=((T, D), BF),
    ng=((T, D), BF),
    ctab=((T, E), F32),
    stab=((T, E), F32),
    ssend=((8, B), F32),
    srecv=((8, B), F32),
    g1=((F + E, D), BF),
    g2=((F, D), BF),
    g3=((3 * E, D), BF),
    vec=((8, D), F32),
    vr=((10, 8, D), F32),
    vs=((4, 8, D), F32),
)
def scatter_scratch(yr):
    zr = B - yr
    return dict(
        ta=((yr, D // 2), BF),
        tb=((yr, D // 2), BF),
        inl=((yr, D), BF),
        inr=((yr, D), BF),
        ry=((4, zr, D // 2), BF),
        ta2=((zr, D // 4), BF),
        tb2=((zr, D // 4), BF),
        inl2=((zr, D // 2), BF),
        inr2=((zr, D // 2), BF),
        ysend=((2, yr, D // 2), BF),
        yrecv=((yr, D // 2), BF),
    )


def reduce_scratch(n):
    return dict(
        rc=((n // 2, D), BF),
        ta=((n // 8, D // 2), BF),
        tb=((n // 8, D // 2), BF),
        inl=((n // 8, D), BF),
        inr=((n // 8, D), BF),
        sy=((2, n // 8, D // 2), BF),
        ry=((3, n // 8, D // 2), BF),
    )


ROWS = (F + E, F, 3 * E)
for name in "on":
    SCRATCH.update({name + "_" + key: v for key, v in scatter_scratch(YROWS[name]).items()})
for k, n in enumerate(ROWS):
    SCRATCH.update({f"r{k}_{key}": spec for key, spec in reduce_scratch(n).items()})


def under(s, prefix, **more):
    picked = {k[len(prefix) :]: v for k, v in vars(s).items() if k.startswith(prefix)}
    return SimpleNamespace(**picked, **more)


def body(
    tok, cot, wqkv, wout, wup, wdown, bqkv, bup, bout, bdown, gain, bias, seg, ctab_h, stab_h,
    out, tgrad, f0, f1, f2, vout, *scratch,
):
    s = SimpleNamespace(**dict(zip(SCRATCH, scratch)))
    send, recv = scratch[len(SCRATCH) :]
    net = Net(send, recv)
    dp, row, col = lax.axis_index("dp"), lax.axis_index("row"), lax.axis_index("col")
    core, x, yh = lax.rem(dp, 2), lax.rem(dp // 2, 4), dp // 8
    half = D // 2

    def dev(core=core, x=x, yh=yh, row=row, col=col):
        return (yh * 8 + x * 2 + core, row, col)

    at = {"core": dev(core=1 - core)}
    for k in (1, 2, 3):
        at[f"x{k}"] = dev(x=lax.rem(x + k, 4))
        at[f"z{k}"] = dev(col=lax.rem(col + k, 4))
    at["y1"] = dev(row=1 - row)
    at["y2"] = dev(yh=1 - yh)
    at["y3"] = dev(yh=1 - yh, row=1 - row)
    y1 = at["y1"]

    s.nbs[...] = jnp.concatenate(
        [gain[...].astype(F32), bias[...].astype(F32), jnp.zeros((4, half), F32)]
    )
    barrier = pltpu.get_barrier_semaphore()
    for device in at.values():
        pl.semaphore_signal(barrier, inc=1, device_id=device, device_id_type=MESH)
    pl.semaphore_wait(barrier, len(at))

    tasks, done = [], set()
    add = tasks.append
    gather_tokens(net, add, done, "x.", ((), ()), tok, s.xall, at, half, col, row, YROWS["x"])
    gather_tokens(net, add, done, "g.", (("x.p4",), ("x.r3", "x.r4", "x.l3", "x.l4")), cot, s.gall, at, half, col, row, YROWS["g"])
    nbc = net.go(s.nbs, s.nb.at[row], y1)
    gather_weights(net, add, done, wqkv, wup, wout, wdown, s, at, core, row)
    tabs = [net.local(ctab_h, s.ctab), net.local(stab_h, s.stab)]
    s.nb[row] = s.nbs[...]
    s.vec[...] = jnp.zeros_like(s.vec)
    s.dk[...] = jnp.zeros_like(s.dk)
    s.dv[...] = jnp.zeros_like(s.dv)

    def flat(values):
        values = values.astype(F32)
        return jnp.concatenate([values[k : k + 1, :] for k in range(values.shape[0])], axis=1)

    segr = flat(seg[...])
    s.segc[...] = jnp.broadcast_to(segr, (8, T)).T
    bq_all = bqkv[...].astype(F32)
    mine = row == 0
    bq = jnp.concatenate(
        [jnp.where(mine, bq_all[k : k + 1, :E], bq_all[k : k + 1, E:]) for k in range(3)], axis=1
    )
    bu_all = flat(bup[...])
    bu = jnp.where(mine, bu_all[:, :F], bu_all[:, F:])
    fcols = pl.ds(pl.multiple_of(row * F, F), F)
    gcols = pl.ds(pl.multiple_of(row * half, half), half)

    def wide(k):
        return jnp.concatenate([s.nb[0, k : k + 1, :], s.nb[1, k : k + 1, :]], axis=1)

    def params():
        yield (nbc,), 0.0
        nbc.wait_recv()
        for copy in tabs:
            copy.wait()
        done.add("nb")

    add(params())

    def norm(c):
        gain0, gain1, bias0, bias1 = wide(0), wide(1), wide(2), wide(3)

        @pl.loop(0, 2)
        def _(b):
            r = rows(c * 2 + b, 128)
            xv = s.xall[r, :].astype(F32)
            mean = jnp.sum(xv, axis=1, keepdims=True) * (1.0 / D)
            square = jnp.sum(xv * xv, axis=1, keepdims=True) * (1.0 / D)
            inv = lax.rsqrt(square - mean * mean + EPSILON)
            normed = (xv - mean) * inv
            s.mean[r, :] = mean
            s.inv[r, :] = inv
            s.ain[r, :] = (normed * gain0 + bias0).astype(BF)
            s.mim[r, :] = (normed * gain1 + bias1).astype(BF)

    def project(c):
        r = rows(c)
        pre = nn(s.ain[r, :], s.wq[...]) + bq
        cos, sin = s.ctab[r, :], s.stab[r, :]
        query = (turn(pre[:, :E], cos, sin)).astype(BF).astype(F32) * (1.0 / math.sqrt(HD))
        key = turn(pre[:, E : 2 * E], cos, sin).astype(BF).astype(F32)
        value = pre[:, 2 * E :].astype(BF).astype(F32)
        s.qs[r, :] = query.astype(BF)
        split_heads(s.qsm, r, query)
        split_heads(s.km, r, key)
        split_heads(s.vm, r, value)
        s.kt[:, r] = key.T.astype(BF)
        s.vt[:, r] = value.T.astype(BF)

    def expand(c):
        r = rows(c)
        pre = nn(s.mim[r, :], s.wu[...]) + bu
        cdf = 0.5 * (1.0 + lax.erf(pre * math.sqrt(0.5)))
        s.hid[r, :] = (pre * cdf).astype(BF)
        s.slope[r, :] = cdf + pre * jnp.exp(-0.5 * pre * pre) * (1.0 / math.sqrt(2.0 * math.pi))

    def contract(c):
        r = rows(c)
        back = (nt(s.gall[r, :], s.wd[...]) * s.slope[r, :]).astype(BF)
        s.hpg[r, :] = back
        s.vec[6:7, fcols] += jnp.sum(back.astype(F32), axis=0, keepdims=True)
        s.vec[4:5, gcols] += jnp.sum(s.gall[r, gcols].astype(F32), axis=0, keepdims=True)
        dout = nt(s.gall[r, :], s.wo[...]).astype(BF).astype(F32)
        s.do[r, :] = dout.astype(BF)
        split_heads(s.dom, r, dout)

    rb, lb, fb = lax.rem(col + 1, 4), lax.rem(col + 3, 4), lax.rem(col + 2, 4)
    blocks = {"own": col, "left": lb, "right": rb, "far": fb}
    outward = ("far", "right", "left", "own")

    def mark(flag, work, *args):
        def both():
            work(*args)
            done.add(flag)

        return both

    first = [0, 256, 768, 1536]

    def attend(i):
        n = (i + 1) * B
        q = pl.ds(i * B, B)

        @pl.loop(0, 2)
        def _(h):
            scores = nt(s.km[h, pl.ds(0, n), :], s.qs[q, :])
            kid = lax.broadcasted_iota(jnp.int32, (n, B), 0)
            qid = lax.broadcasted_iota(jnp.int32, (n, B), 1) + i * B
            allowed = (kid <= qid) & (s.segc[pl.ds(0, n), 0:1] == segr[:, i * B : (i + 1) * B])
            scores = jnp.where(allowed, scores, -1e30)
            top = jnp.max(scores, axis=0, keepdims=True)
            expo = jnp.exp(scores - top)
            probs = expo * (1.0 / jnp.sum(expo, axis=0, keepdims=True))
            s.probs[h, pl.ds(first[i], n), :] = probs
            hrows = rows(h, HD)
            s.mt[hrows, q] = nn(s.vt[hrows, pl.ds(0, n)], probs.astype(BF)).astype(BF)

        s.mixed[q, :] = s.mt[:, q].astype(F32).T.astype(BF)

    def attend_back(i):
        n = (i + 1) * B
        q = pl.ds(i * B, B)

        @pl.loop(0, 2)
        def _(h):
            probs = s.probs[h, pl.ds(first[i], n), :]
            dprob = nt(s.vm[h, pl.ds(0, n), :], s.do[q, :])
            inner = jnp.sum(probs * dprob, axis=0, keepdims=True)
            dscore = (probs * (dprob - inner)).astype(BF)
            s.dv[pl.ds(0, n), :] += nn(probs.astype(BF), s.dom[h, q, :])
            s.dk[pl.ds(0, n), :] += nn(dscore, s.qsm[h, q, :])
            hrows = rows(h, HD)
            s.dqt[hrows, q] = nn(s.kt[hrows, pl.ds(0, n)], dscore) * (1.0 / math.sqrt(HD))

    def branch(b):
        r = rows(b)
        s.op[r, :] = (nn(s.mixed[r, :], s.wo[...]) + nn(s.hid[r, :], s.wd[...])).astype(BF)

    def down_grad():
        @pl.loop(0, 4)
        def _(b):
            r = rows(b, 128)
            s.g1[r, :] = tn(s.hid[:, r], s.gall[...]).astype(BF)

        s.g1[F:, :] = nn(s.mt[...], s.gall[...]).astype(BF)

    def up_grad():
        @pl.loop(0, 4)
        def _(b):
            r = rows(b, 128)
            s.g2[r, :] = tn(s.hpg[:, r], s.mim[...]).astype(BF)

    def qkv_grad(b):
        r = rows(b)
        cos, sin = s.ctab[r, :], -s.stab[r, :]
        dq = turn(s.dqt[:, r].T, cos, sin).astype(BF)
        dk = turn(s.dk[r, :], cos, sin).astype(BF)
        dv = s.dv[r, :].astype(BF)
        both = jnp.concatenate([dq, dk, dv], axis=1)
        s.qkvg[r, :] = both
        ecols3 = pl.ds(pl.multiple_of(row * 3 * E, 3 * E), 3 * E)
        s.vec[5:6, ecols3] += jnp.sum(both.astype(F32), axis=0, keepdims=True)

    def qkv_weight_grad():
        @pl.loop(0, 3)
        def _(b):
            r = rows(b, E)
            s.g3[r, :] = tn(s.qkvg[:, r], s.ain[...]).astype(BF)

    def input_grad(b):
        r = rows(b)
        gain0, gain1 = wide(0), wide(1)
        attn = nt(s.qkvg[r, :], s.wq[...])
        mlp = nt(s.hpg[r, :], s.wu[...])
        normed = (s.xall[r, :].astype(F32) - s.mean[r, :]) * s.inv[r, :]
        s.ng[r, :] = (attn * gain0 + mlp * gain1).astype(BF)
        s.vec[0:1, :] += jnp.sum(attn * normed, axis=0, keepdims=True)
        s.vec[1:2, :] += jnp.sum(mlp * normed, axis=0, keepdims=True)
        s.vec[2:3, :] += jnp.sum(attn, axis=0, keepdims=True)
        s.vec[3:4, :] += jnp.sum(mlp, axis=0, keepdims=True)

    so, sn = under(s, "o_"), under(s, "n_")
    where = dict(core=core, x=x, row=row)
    sums = []
    ny = YROWS["n"]
    own = rows(col)

    def look(h, total):
        mean, inv = s.mean[own, :], s.inv[own, :]
        xv = s.xall[pl.ds(pl.multiple_of(col * B, B), ny), pl.ds(h * half, half)].astype(F32)
        normed = (xv - mean[:ny]) * inv[:ny]
        sums.append(jnp.sum(total, axis=1, keepdims=True))
        sums.append(jnp.sum(total * normed, axis=1, keepdims=True))

    def write_out():
        xv = s.xall[own, gcols].astype(F32) + (flat(bout[...]) + flat(bdown[...]))
        total = jnp.concatenate([total_y(so, row), total_z(s.op, so, col, row, YROWS["o"])])
        out[...] = (xv + total).astype(BF)

    def write_grad():
        yield ("n.y.sum", "n.y.end", "n.z.sum"), 0.4
        mean, inv = s.mean[own, :], s.inv[own, :]
        normed = (s.xall[own, gcols].astype(F32) - mean) * inv
        zsum = total_z(s.ng, sn, col, row, ny)
        first_sum = jnp.concatenate([sums[0] + sums[2], jnp.sum(zsum, axis=1, keepdims=True)])
        second = jnp.sum(zsum * normed[ny:], axis=1, keepdims=True)
        second_sum = jnp.concatenate([sums[1] + sums[3], second])
        lane = lax.broadcasted_iota(jnp.int32, (B, 128), 1)
        s.ssend[...] = jnp.where(lane < 4, first_sum, second_sum).T[:8, :]
        ys = net.go(s.ssend, s.srecv, y1)
        yield (ys,), 0.5
        ys.wait_recv()
        both = (s.ssend[...] + s.srecv[...]) * (1.0 / D)
        both = jnp.concatenate([both] * 16).T
        total = jnp.concatenate([total_y(sn, row), zsum])
        tgrad[...] = (
            s.gall[own, gcols].astype(F32) + inv * (total - both[:, 0:1] - normed * both[:, 4:5])
        ).astype(BF)

    def write_vectors():
        vout[0] = s.vs[2]
        vout[1] = s.vs[3]

    scatter(net, add, done, "o.", tuple("send." + b for b in outward), s.op, so, at, col, row, YROWS["o"])
    scatter(net, add, done, "n.", tuple("ng." + b for b in outward), s.ng, sn, at, col, row, ny, look)
    gate = ("g.r3", "g.r4", "g.l3", "g.l4")
    for b in outward:
        add(later(("op." + b,) + gate, 0.0, mark("send." + b, lambda: None)))
    reduce_weights(net, add, done, "a.", "g1", s.g1, under(s, "r0_", fin=f0), at, where, ROWS[0])
    reduce_weights(net, add, done, "b.", "g2", s.g2, under(s, "r1_", fin=f1), at, where, ROWS[1])
    reduce_weights(net, add, done, "c.", "g3", s.g3, under(s, "r2_", fin=f2), at, where, ROWS[2])
    add(reduce_vectors(net, done, s, at))
    add(later(("vsum",), 0.05, write_vectors))
    add(write_grad())
    for name, b in blocks.items():
        add(later(("nb", "x." + name), 0.28, mark("norm." + name, norm, b)))
        add(later(("wq", "norm." + name), 0.63, mark("proj." + name, project, b)))
    needs = tuple("proj." + name for name in blocks)
    for i in range(4):
        add(later(needs, 0.58 * (i + 1), mark(f"attf{i}", attend, i)))
        needs = (f"attf{i}",)
    for name, b in blocks.items():
        add(later(("wu", "norm." + name), 0.55, mark("exp." + name, expand, b)))
    for name in outward:
        needs = ("wo", "wd", "attf3", "exp." + name)
        add(later(needs, 0.7, mark("op." + name, branch, blocks[name])))
    for name, b in blocks.items():
        needs = ("wo", "wd", "g." + name, "exp." + name)
        add(later(needs, 0.4, mark("con." + name, contract, b)))
    allg = tuple("g." + name for name in blocks) + tuple("exp." + name for name in blocks)
    add(later(allg + ("attf3",), 1.85, mark("g1", down_grad)))
    allc = tuple("con." + name for name in blocks)
    add(later(allc, 1.65, mark("g2", up_grad)))
    needs = allc + ("attf3",)
    for i in range(4):
        add(later(needs, 0.6 * (i + 1), mark(f"attb{i}", attend_back, i)))
        needs = (f"attb{i}",)
    for name in outward:
        add(later(("attb3",), 0.46, mark("qg." + name, qkv_grad, blocks[name])))
    add(later(tuple("qg." + name for name in blocks), 1.75, mark("g3", qkv_weight_grad)))
    for name in outward:
        add(later(("qg." + name,), 0.65, mark("ng." + name, input_grad, blocks[name])))
    add(later(tuple("ng." + name for name in blocks), 0.0, mark("vec", lambda: None)))
    add(later(("o.y.end", "o.z.sum"), 0.3, mark("out", write_out)))
    run(tasks, done)
    for copy in net.sent:
        copy.wait_send()


def tables():
    freq = np.arange(ROT // 2, dtype=np.float32)
    inverse = np.float32(10000.0) ** (np.float32(-2.0) * freq / np.float32(ROT))
    angle = np.arange(T, dtype=np.float32)[:, None] * inverse[None, :].astype(np.float32)
    cos, sin = np.cos(angle), np.sin(angle)
    ones, zeros = np.ones((T, HD - ROT), np.float32), np.zeros((T, HD - ROT), np.float32)
    ctab = np.concatenate([cos, cos, ones] * 2, axis=1)
    stab = np.concatenate([-sin, sin, zeros] * 2, axis=1)
    return ctab.astype(np.float32), stab.astype(np.float32)


def last(
    f0_h, f1_h, f2_h, vec_h, out_h, tgrad_h,
    out_o, tgrad_o, wq_o, bq_o, wo_o, bo_o, wu_o, bu_o, wd_o, bd_o, gain_o, bias_o,
    f0, f1, f2, vec, out, tgrad, wq, wo, wu, wd, sems,
):
    row = lax.axis_index("row")
    copies = []

    def write(src, dst):
        copy = pltpu.make_async_copy(src, dst, sems.at[len(copies)])
        copy.start()
        copies.append(copy)
        return copy

    pairs = ((f0_h, f0), (f1_h, f1), (f2_h, f2), (vec_h, vec), (out_h, out), (tgrad_h, tgrad))
    reads = [write(a, b) for a, b in pairs]
    reads[0].wait()
    for r in range(2):
        for k in range(8):
            piece = f0[k // 4, k % 4, r].astype(F32)
            n = piece.shape[0]
            inside = max(0, min(n, F - k * n))
            if inside:
                wd[pl.ds(r * F + k * n, inside), :] = piece[:inside]
            if inside < n:
                wo[pl.ds(r * E + k * n + inside - F, n - inside), :] = piece[inside:]
        write(wd.at[pl.ds(r * F, F)], wd_o.at[pl.ds(r * F, F)])
    write(wo, wo_o)
    reads[1].wait()
    for r in range(2):
        for k in range(4):
            pair = [f1[(2 * k + h) // 4, (2 * k + h) % 4, r].astype(F32) for h in range(2)]
            wu[:, pl.ds(r * F + k * E, E)] = jnp.concatenate(pair).T
        write(wu.at[:, pl.ds(r * F, F)], wu_o.at[:, pl.ds(r * F, F)])
    reads[2].wait()
    for r in range(2):
        whole = jnp.concatenate([f2[k // 4, k % 4, r].astype(F32) for k in range(8)])
        for k in range(3):
            wq[k, :, pl.ds(r * E, E)] = whole[k * E : (k + 1) * E].T
    write(wq, wq_o)
    for copy in reads[3:]:
        copy.wait()
    write(out, out_o)
    write(tgrad, tgrad_o)
    half = D // 2
    left = row == 0

    def cut(values):
        return jnp.where(left, values[:, :half], values[:, half:])

    bo_o[...] = cut(vec[0, 4:5, :])
    bd_o[...] = cut(vec[0, 4:5, :])
    for k in range(3):
        bq_o[k : k + 1, :E] = vec[0, 5:6, k * E : (k + 1) * E]
        bq_o[k : k + 1, E:] = vec[0, 5:6, (k + 3) * E : (k + 4) * E]
    bu_o[...] = vec[0, 6:7, :]
    gain_o[...] = cut(vec[1, 0:2, :])
    bias_o[...] = cut(vec[1, 2:4, :])
    for copy in copies[len(reads) :]:
        copy.wait()


def on_device(
    tokens, segment_ids, w_qkv, b_qkv, w_out, b_out, w_up, b_up, w_down, b_down, norm_gain, norm_bias, cotangent
):
    ctab, stab = tables()
    vmem = pl.BlockSpec(memory_space=pltpu.VMEM)
    hbm = pl.BlockSpec(memory_space=pl.ANY)
    shape = jax.ShapeDtypeStruct
    early = [
        shape((2, 4, 2, ROWS[0] // 8, D // 2), BF),
        shape((2, 4, 2, ROWS[1] // 8, D // 2), BF),
        shape((2, 4, 2, ROWS[2] // 8, D // 2), BF),
        shape((2, 8, D), F32),
    ]
    out, tgrad, f0, f1, f2, vec = pl.pallas_call(
        body,
        out_shape=[
            shape((B, D // 2), BF),
            shape((B, D // 2), BF),
            *early,
        ],
        in_specs=[hbm] * 6 + [vmem] * 7 + [hbm] * 2,
        out_specs=[vmem] * 6,
        scratch_shapes=[pltpu.VMEM(*spec) for spec in SCRATCH.values()]
        + [pltpu.SemaphoreType.DMA((NSEM,)), pltpu.SemaphoreType.DMA((NSEM,))],
        compiler_params=pltpu.CompilerParams(
            collective_id=0, has_side_effects=True, vmem_limit_bytes=60 * 1024 * 1024
        ),
        name="block",
    )(
        tokens, cotangent, w_qkv, w_out, w_up, w_down, b_qkv, b_up.reshape(8, 128),
        b_out.reshape(4, 128), b_down.reshape(4, 128), norm_gain, norm_bias,
        segment_ids.reshape(8, 128), jnp.asarray(ctab), jnp.asarray(stab),
    )
    big = [
        ((3, D // 2, 2 * E), F32),
        ((2 * E, D // 2), F32),
        ((D // 2, 2 * F), F32),
        ((2 * F, D // 2), F32),
    ]
    results = pl.pallas_call(
        last,
        out_shape=[
            shape((B, D // 2), BF),
            shape((B, D // 2), BF),
            shape(*big[0]),
            shape((3, 2 * E), F32),
            shape(*big[1]),
            shape((1, D // 2), F32),
            shape(*big[2]),
            shape((1, 2 * F), F32),
            shape(*big[3]),
            shape((1, D // 2), F32),
            shape((2, D // 2), F32),
            shape((2, D // 2), F32),
        ],
        in_specs=[hbm] * 6,
        out_specs=[hbm, hbm, hbm, vmem, hbm, vmem, hbm, vmem, hbm, vmem, vmem, vmem],
        scratch_shapes=[pltpu.VMEM(e.shape, e.dtype) for e in early]
        + [pltpu.VMEM((B, D // 2), BF)] * 2
        + [pltpu.VMEM(*spec) for spec in big]
        + [pltpu.SemaphoreType.DMA((16,))],
        compiler_params=pltpu.CompilerParams(vmem_limit_bytes=60 * 1024 * 1024),
        name="last",
    )(f0, f1, f2, vec, out, tgrad)
    out, tgrad, wq, bq, wo, bo, wu, bu, wd, bd, gain, bias = results
    bo, bu, bd = bo.reshape(-1), bu.reshape(-1), bd.reshape(-1)
    return (out, tgrad, wq, bq, wo, bo, wu, bu, wd, bd, gain, bias)


def solution(mesh):
    in_specs = (
        P(("dp", "col"), "row"),
        P("dp"),
        P(None, "row", "col"),
        P(None, "col"),
        P("col", "row"),
        P("row"),
        P("row", "col"),
        P("col"),
        P("col", "row"),
        P("row"),
        P(None, "row"),
        P(None, "row"),
        P(("dp", "col"), "row"),
    )
    out_specs = (
        P(("dp", "col"), "row"),
        P(("dp", "col"), "row"),
        P(None, "row", "col"),
        P(None, "col"),
        P("col", "row"),
        P("row"),
        P("row", "col"),
        P("col"),
        P("col", "row"),
        P("row"),
        P(None, "row"),
        P(None, "row"),
    )
    return jax.shard_map(
        on_device, mesh=mesh, in_specs=in_specs, out_specs=out_specs, check_vma=False
    )
```

```python
from types import SimpleNamespace
import math

import numpy as np
import jax
import jax.numpy as jnp
from jax import lax
from jax.experimental import pallas as pl
from jax.experimental.pallas import tpu as pltpu
from jax.sharding import PartitionSpec as P

MESH = pl.DeviceIdType.MESH
BF = jnp.bfloat16
F32 = jnp.float32
T = 1024
D = 1024
HD = 64
ROT = 16
E = 128
F = 512
B = 256
EPSILON = 1e-05
NSEM = 200
YROWS = dict(x=112, g=144, o=128, n=208)


ORDER = (
    1, 5, 0, 2, 8, 3, 4, 9, 44, 2, 6, 10, 3, 11, 4, 12, 7, 40, 5, 13, 9, 8, 16, 128, 40, 129, 6, 14,
    21, 23, 25, 24, 29, 10, 11, 17, 130, 131, 41, 7, 15, 20, 28, 22, 42, 13, 12, 18, 132, 14, 41,
    142, 133, 42, 140, 141, 23, 31, 24, 27, 32, 15, 19, 134, 135, 136, 143, 43, 137, 25, 33, 138,
    22, 26, 30, 29, 139, 27, 35, 43, 145, 147, 28, 36, 148, 144, 146, 33, 31, 26, 34, 79, 45, 49,
    82, 48, 81, 53, 47, 51, 80, 52, 50, 46, 30, 37, 149, 32, 38, 150, 35, 52, 34, 39, 152, 83, 151,
    53, 54, 45, 55, 153, 97, 48, 154, 83, 86, 84, 87, 88, 85, 155, 156, 54, 47, 57, 59, 157, 87, 46,
    58, 58, 56, 59, 60, 160, 97, 98, 88, 100, 102, 89, 101, 99, 61, 158, 163, 66, 62, 159, 161, 162,
    111, 102, 164, 67, 63, 101, 103, 69, 60, 165, 61, 64, 68, 70, 89, 90, 166, 65, 111, 113, 114,
    167, 125, 112, 116, 115, 62, 72, 168, 63, 75, 73, 103, 104, 70, 69, 71, 64, 74, 76, 125, 115,
    116, 117, 90, 91, 92, 125, 65, 76, 75, 77, 117, 118, 91, 93, 92, 95, 94, 104, 105, 106, 93, 94,
    125, 71, 78, 95, 96, 77, 118, 119, 120, 105, 107, 106, 109, 108, 96, 107, 108, 125, 126, 119,
    121, 120, 123, 122, 121, 122, 78, 127, 109, 110, 123, 124, 127, 110, 124,
)


def nn(a, b):
    return jnp.dot(a, b, preferred_element_type=F32)


def nt(a, b):
    return lax.dot_general(a, b, (((1,), (1,)), ((), ())), preferred_element_type=F32)


def tn(a, b):
    return lax.dot_general(a, b, (((0,), (0,)), ((), ())), preferred_element_type=F32)


def rows(block, size=B):
    return pl.ds(pl.multiple_of(block * size, size), size)


class Net:
    def __init__(self, send, recv):
        self.send, self.recv, self.count, self.sent = send, recv, 0, []

    def go(self, src, dst, device):
        k = self.count
        self.count += 1
        assert k < NSEM
        copy = pltpu.make_async_remote_copy(
            src_ref=src,
            dst_ref=dst,
            send_sem=self.send.at[k],
            recv_sem=self.recv.at[k],
            device_id=device,
            device_id_type=MESH,
        )
        copy.start()
        self.sent.append(copy)
        return copy

    def local(self, src, dst):
        k = self.count
        self.count += 1
        assert k < NSEM
        copy = pltpu.make_async_copy(src, dst, self.send.at[k])
        copy.start()
        return copy


def later(deps, cost, work):
    yield deps, cost
    work()


def gather_tokens(net, add, done, name, begin, own, full, at, half, col, row, yr):
    right, left, peer = at["z1"], at["z3"], at["y1"]
    zr = B - yr
    part = zr // 32 * 16
    cut = yr + part
    c = {}

    def place(b, h, start=0, size=B):
        r = pl.ds(pl.multiple_of(b * B + start, 16), size)
        return full.at[r, pl.ds(pl.multiple_of(h * half, half), half)]

    def move(key, device, *where):
        c[key] = net.go(place(*where), place(*where), device)
        done.add(name + key)

    def send(key, device, start, size):
        c[key] = net.go(own.at[pl.ds(start, size)], place(col, row, start, size), device)
        done.add(name + key)

    lcol, rcol, fcol = lax.rem(col + 3, 4), lax.rem(col + 1, 4), lax.rem(col + 2, 4)

    def begin_y():
        yield begin[0], 0.1
        c["keep"] = net.local(own, place(col, row))
        send("p0", peer, 0, yr)
        send("p1", peer, yr, zr)
        c["keep"].wait()
        done.add(name + "keep")

    def begin_z():
        yield begin[1], 0.1
        send("r1", right, yr, zr)
        send("l1", left, yr, zr)
        send("r0", right, 0, yr)
        send("l0", left, 0, yr)

    def hop(keys, *work):
        yield tuple(name + k for k in keys), 0.0
        yield tuple(c[k] for k in keys), 0.05
        for k in keys:
            c[k].wait_recv()
        for w in work:
            move(*w)
        done.update(name + k + "!" for k in keys)

    def whole(flag, keys):
        yield tuple(name + k + ("" if k == "keep" else "!") for k in keys), 0.0
        done.add(name + flag)

    add(begin_y())
    add(begin_z())
    add(hop(["p0"], ("r2", right, col, 1 - row, 0, yr), ("l2", left, col, 1 - row, 0, yr)))
    add(hop(["r1"], ("r3", right, lcol, row, yr, part), ("p2", peer, lcol, row, yr, zr)))
    add(hop(["l1"], ("l3", left, rcol, row, cut, B - cut), ("p3", peer, rcol, row, yr, zr)))
    add(hop(["r0"], ("r4", right, lcol, row, 0, yr)))
    add(hop(["l2"], ("l4", left, rcol, 1 - row, 0, yr)))
    add(hop(["r3", "l3"], ("p4", peer, fcol, row, yr, zr)))
    add(hop(["p1"]))
    add(hop(["l0"]))
    add(hop(["r2"]))
    add(hop(["p2"]))
    add(hop(["p3"]))
    add(hop(["r4"]))
    add(hop(["l4"]))
    add(hop(["p4"]))
    add(whole("own", ["p0", "p1", "keep"]))
    add(whole("left", ["r0", "r1", "r2", "p2"]))
    add(whole("right", ["l0", "l1", "l2", "p3"]))
    add(whole("far", ["r3", "r4", "l3", "l4", "p4"]))


def gather_weights(net, add, done, wqkv, wup, wout, wdown, s, at, core, row):
    half, part = D // 2, D // 4
    mine, theirs = row, 1 - row
    drows, ocols = rows(row, half), rows(1 - row, half)

    def cut(which, size):
        return pl.ds(pl.multiple_of(which * size, size), size)

    local = {}
    for k in range(3):
        kcols = pl.ds(k * E, E)
        local[k] = net.local(wqkv.at[k, :, cut(mine, E)], s.wq.at[drows, kcols])
    local["u"] = net.local(wup.at[:, cut(mine, F)], s.wu.at[drows])
    local["o"] = net.local(wout.at[cut(mine, E)], s.wo.at[:, drows])
    local["d"] = net.local(wdown.at[cut(mine, F)], s.wd.at[:, drows])
    src, dst, got = cut(core, part), cut(row * 2 + core, part), cut((1 - row) * 2 + core, part)
    far, near = at["y3"], at["core"]
    q = [
        net.go(wqkv.at[k, src, cut(theirs, E)], s.wq.at[dst, pl.ds(k * E, E)], far)
        for k in range(3)
    ]
    u = net.go(wup.at[src, cut(theirs, F)], s.wu.at[dst], far)
    o = net.go(wout.at[cut(theirs * 2 + core, E // 2)], s.wo.at[cut(core, E // 2), drows], far)
    d = net.go(wdown.at[cut(theirs * 2 + core, F // 2)], s.wd.at[cut(core, F // 2), drows], far)

    def share(flag, copies, view, locals_):
        yield tuple(copies), 0.05
        for copy in copies:
            copy.wait_recv()
        second = net.go(view, view, near)
        yield (second,), 0.0
        second.wait_recv()
        for k in locals_:
            local[k].wait()
        done.add(flag)

    add(share("wq", q, s.wq.at[got], range(3)))
    add(share("wu", [u], s.wu.at[got], "u"))
    add(share("wo", [o], s.wo.at[cut(core, E // 2), ocols], "o"))
    add(share("wd", [d], s.wd.at[cut(core, F // 2), ocols], "d"))


def ring_scatter(net, add, done, name, part, bufs, me, right, left, width, ready):
    ta, tb, inl, inr = bufs
    lo, hi = pl.ds(0, width), pl.ds(width, width)
    far, rb, lb = lax.rem(me + 2, 4), lax.rem(me + 1, 4), lax.rem(me + 3, 4)
    c = {}

    def send(deps, *sends):
        yield deps, 0.05
        for key, src, dst, device in sends:
            c[key] = net.go(src, dst, device)
            done.add(name + key)

    def through(came, flag, buf, view, key, dst, device):
        yield (name + came, flag), 0.0
        yield (c[came],), 0.15
        c[came].wait_recv()
        view[...] = (view[...].astype(F32) + buf[...].astype(F32)).astype(BF)
        c[key] = net.go(view, dst, device)
        done.add(name + key)

    def finish():
        yield tuple(name + k for k in "cdef") + (ready[3],), 0.0
        yield tuple(c[k] for k in "cdef"), 0.0
        for k in "cdef":
            c[k].wait_recv()
        done.add(name + "sum")

    add(send((ready[0],), ("a", part(far, lo), ta, right), ("b", part(far, hi), tb, left)))
    add(send((ready[1],), ("c", part(rb, hi), inl.at[:, hi], right)))
    add(send((ready[2],), ("d", part(lb, lo), inr.at[:, lo], left)))
    add(through("a", ready[1], ta, part(rb, lo), "e", inl.at[:, lo], right))
    add(through("b", ready[2], tb, part(lb, hi), "f", inr.at[:, hi], left))
    add(finish())


def reduce_weights(net, add, done, name, begin, grad, s, at, me, n):
    core, x, row = me["core"], me["x"], me["row"]
    half, size = n // 2, n // 8
    base, away = core * half, (1 - core) * half
    x1, x3, near = at["x1"], at["x3"], at["core"]
    lx, rx, fx = lax.rem(x + 3, 4), lax.rem(x + 1, 4), lax.rem(x + 2, 4)
    c = {}

    def start():
        yield (begin,), 0.05
        copy = net.go(grad.at[pl.ds(pl.multiple_of(away, half), half)], s.rc, near)
        yield (copy,), 0.4 * n / 640
        copy.wait_recv()
        own = grad.at[pl.ds(pl.multiple_of(base, half), half)]
        own[...] = (own[...].astype(F32) + s.rc[...].astype(F32)).astype(BF)
        done.add(name + "core")

    def part(block, cols):
        return grad.at[pl.ds(pl.multiple_of(base + block * size, size), size), cols]

    def across():
        yield (name + "sum",), 0.2
        for h in range(2):
            cols = pl.ds(h * (D // 2), D // 2)
            total = part(x, cols)[...].astype(F32) + s.inl[:, cols].astype(F32)
            s.sy[h] = (total + s.inr[:, cols].astype(F32)).astype(BF)
        g0 = net.go(s.sy.at[row], s.ry.at[0], at["y2"])
        g1 = net.go(s.sy.at[1 - row], s.ry.at[1], at["y1"])
        g2 = net.go(s.sy.at[1 - row], s.ry.at[2], at["y3"])
        yield (g0, g1, g2), 0.15
        for copy in (g0, g1, g2):
            copy.wait_recv()
        s.fin[core, x, row] = (s.sy[row].astype(F32) + s.ry[0].astype(F32)).astype(BF)
        s.fin[core, x, 1 - row] = (s.ry[1].astype(F32) + s.ry[2].astype(F32)).astype(BF)
        for key, h, device in (("a", 0, x1), ("b", 1, x3), ("c", 1, x1), ("d", 0, x3)):
            view = s.fin.at[core, x, h]
            c[key] = net.go(view, view, device)
        view = s.fin.at[core, x]
        c["k"] = net.go(view, view, near)
        done.add(name + "sent")

    def hop(keys, flag, view, device, key, need=()):
        yield (name + flag,) + tuple(name + k + "!" for k in need), 0.0
        yield tuple(c[k] for k in keys), 0.05
        for k in keys:
            c[k].wait_recv()
        c[key] = net.go(view, view, device)
        done.update(name + k + "!" for k in keys)
        done.add(name + key)

    def end():
        yield tuple(name + k for k in ("l", "m", "n")), 0.0
        yield tuple(c[k] for k in "klmn"), 0.0
        for k in "klmn":
            c[k].wait_recv()
        done.add(name + "end")

    ready = (name + "core",) * 4
    add(start())
    ring_scatter(
        net, add, done, name, part, (s.ta, s.tb, s.inl, s.inr), x, x1, x3, D // 2, ready
    )
    add(across())
    add(hop("a", "sent", s.fin.at[core, lx, 0], x1, "p"))
    add(hop("b", "sent", s.fin.at[core, rx, 1], x3, "q"))
    add(hop("c", "sent", s.fin.at[core, lx], near, "l", "a"))
    add(hop("d", "sent", s.fin.at[core, rx], near, "m", "b"))
    add(hop("pq", "p", s.fin.at[core, fx], near, "n", "b"))
    add(end())


def reduce_vectors(net, done, s, at):
    yield ("vec",), 0.0
    c = net.go(s.vec, s.vr.at[0], at["core"])
    yield (c,), 0.05
    c.wait_recv()
    s.vs[0] = s.vec[...] + s.vr[0]
    for n, axis in enumerate("xyz"):
        copies = [net.go(s.vs.at[n], s.vr.at[3 * n + k], at[axis + str(k)]) for k in (1, 2, 3)]
        yield tuple(copies), 0.05
        for copy in copies:
            copy.wait_recv()
        s.vs[n + 1] = (s.vs[n] + s.vr[3 * n + 1]) + (s.vr[3 * n + 2] + s.vr[3 * n + 3])
    done.add("vsum")


def scatter(net, add, done, name, ready, p, s, at, col, row, yr, look=None):
    half, zr = D // 2, B - yr
    far, rb, lb = lax.rem(col + 2, 4), lax.rem(col + 1, 4), lax.rem(col + 3, 4)
    mcols, ocols = rows(row, half), rows(1 - row, half)
    right, left, peer = at["z1"], at["z3"], at["y1"]

    def yrows(b):
        return pl.ds(pl.multiple_of(b * B, B), yr)

    def zrows(b):
        return pl.ds(pl.multiple_of(b * B + yr, 16), zr)

    def zpart(b, cols):
        return p.at[zrows(b), pl.ds(pl.multiple_of(row * half + cols.start, 256), cols.size)]

    def pair(k, b):
        yield (ready[k],), 0.05
        copy = net.go(p.at[zrows(b), ocols], s.ry.at[k], peer)
        yield (copy,), 0.15
        copy.wait_recv()
        view = p.at[zrows(b), mcols]
        view[...] = (view[...].astype(F32) + s.ry[k].astype(F32)).astype(BF)
        done.add(name + "z" + str(k))

    def last():
        yield (name + "y.sum",), 0.3
        for h in range(2):
            cols = pl.ds(h * half, half)
            total = p[yrows(col), cols].astype(F32) + s.inl[:, cols].astype(F32)
            total += s.inr[:, cols].astype(F32)
            s.ysend[h] = total.astype(BF)
            if look is not None:
                look(h, total)
        copy = net.go(s.ysend.at[1 - row], s.yrecv, peer)
        yield (copy,), 0.0
        copy.wait_recv()
        done.add(name + "y.end")

    for k, b in enumerate((far, rb, lb, col)):
        add(pair(k, b))
    ring_scatter(
        net, add, done, name + "y.", lambda b, cols: p.at[yrows(b), cols],
        (s.ta, s.tb, s.inl, s.inr), col, right, left, half, ready,
    )
    ring_scatter(
        net, add, done, name + "z.", zpart,
        (s.ta2, s.tb2, s.inl2, s.inr2), col, right, left, half // 2,
        tuple(name + "z" + str(k) for k in range(4)),
    )
    add(last())


def total_y(s, row):
    return s.ysend[row].astype(F32) + s.yrecv[...].astype(F32)


def total_z(p, s, col, row, yr):
    own = p[pl.ds(pl.multiple_of(col * B + yr, 16), B - yr), rows(row, D // 2)]
    return own.astype(F32) + s.inl2[...].astype(F32) + s.inr2[...].astype(F32)


def run(tasks, done):
    asked = [next(task)[0] for task in tasks]
    for k in ORDER:
        for need in asked[k]:
            assert not isinstance(need, str) or need in done, "order"
        asked[k] = next(tasks[k], ((),))[0]
    assert all(next(task, None) is None for task in tasks), "unfinished"


def turn(values, cos, sin):
    lane = lax.broadcasted_iota(jnp.int32, values.shape, 1)
    other = jnp.where(lane % HD < ROT // 2, pltpu.roll(values, E - ROT // 2, 1), pltpu.roll(values, ROT // 2, 1))
    return values * cos + other * sin


def split_heads(ref, at_rows, values):
    lane = lax.broadcasted_iota(jnp.int32, values.shape, 1)
    zero = jnp.zeros_like(values)
    ref[0, at_rows, :] = jnp.where(lane < HD, values, zero).astype(BF)
    ref[1, at_rows, :] = jnp.where(lane < HD, zero, values).astype(BF)


SCRATCH = dict(
    xall=((T, D), BF),
    gall=((T, D), BF),
    ain=((T, D), BF),
    mim=((T, D), BF),
    wq=((D, 3 * E), BF),
    wo=((E, D), BF),
    wu=((D, F), BF),
    wd=((F, D), BF),
    nb=((2, 8, D // 2), F32),
    mean=((T, 1), F32),
    inv=((T, 1), F32),
    hid=((T, F), BF),
    slope=((T, F), F32),
    segc=((T, 8), F32),
    nbs=((8, D // 2), F32),
    hpg=((T, F), BF),
    qs=((T, E), BF),
    qsm=((2, T, E), BF),
    km=((2, T, E), BF),
    vm=((2, T, E), BF),
    kt=((E, T), BF),
    vt=((E, T), BF),
    do=((T, E), BF),
    dom=((2, T, E), BF),
    probs=((2, 2560, B), F32),
    mt=((E, T), BF),
    mixed=((T, E), BF),
    dqt=((E, T), F32),
    cap=((T, B), F32),
    dk=((T, E), F32),
    dv=((T, E), F32),
    qkvg=((T, 3 * E), BF),
    op=((T, D), BF),
    ng=((T, D), BF),
    ctab=((T, E), F32),
    stab=((T, E), F32),
    ssend=((8, B), F32),
    srecv=((8, B), F32),
    g1=((F + E, D), BF),
    g2=((F, D), BF),
    g3=((3 * E, D), BF),
    vec=((8, D), F32),
    vr=((10, 8, D), F32),
    vs=((4, 8, D), F32),
)
def scatter_scratch(yr):
    zr = B - yr
    return dict(
        ta=((yr, D // 2), BF),
        tb=((yr, D // 2), BF),
        inl=((yr, D), BF),
        inr=((yr, D), BF),
        ry=((4, zr, D // 2), BF),
        ta2=((zr, D // 4), BF),
        tb2=((zr, D // 4), BF),
        inl2=((zr, D // 2), BF),
        inr2=((zr, D // 2), BF),
        ysend=((2, yr, D // 2), BF),
        yrecv=((yr, D // 2), BF),
    )


def reduce_scratch(n):
    return dict(
        rc=((n // 2, D), BF),
        ta=((n // 8, D // 2), BF),
        tb=((n // 8, D // 2), BF),
        inl=((n // 8, D), BF),
        inr=((n // 8, D), BF),
        sy=((2, n // 8, D // 2), BF),
        ry=((3, n // 8, D // 2), BF),
    )


ROWS = (F + E, F, 3 * E)
for name in "on":
    SCRATCH.update({name + "_" + key: v for key, v in scatter_scratch(YROWS[name]).items()})
for k, n in enumerate(ROWS):
    SCRATCH.update({f"r{k}_{key}": spec for key, spec in reduce_scratch(n).items()})


def under(s, prefix, **more):
    picked = {k[len(prefix) :]: v for k, v in vars(s).items() if k.startswith(prefix)}
    return SimpleNamespace(**picked, **more)


def body(
    tok, cot, wqkv, wout, wup, wdown, bqkv, bup, bout, bdown, gain, bias, seg, ctab_h, stab_h,
    out, tgrad, f0, f1, f2, vout, *scratch,
):
    s = SimpleNamespace(**dict(zip(SCRATCH, scratch)))
    send, recv = scratch[len(SCRATCH) :]
    net = Net(send, recv)
    dp, row, col = lax.axis_index("dp"), lax.axis_index("row"), lax.axis_index("col")
    core, x, yh = lax.rem(dp, 2), lax.rem(dp // 2, 4), dp // 8
    half = D // 2

    def dev(core=core, x=x, yh=yh, row=row, col=col):
        return (yh * 8 + x * 2 + core, row, col)

    at = {"core": dev(core=1 - core)}
    for k in (1, 2, 3):
        at[f"x{k}"] = dev(x=lax.rem(x + k, 4))
        at[f"z{k}"] = dev(col=lax.rem(col + k, 4))
    at["y1"] = dev(row=1 - row)
    at["y2"] = dev(yh=1 - yh)
    at["y3"] = dev(yh=1 - yh, row=1 - row)
    y1 = at["y1"]

    s.nbs[...] = jnp.concatenate(
        [gain[...].astype(F32), bias[...].astype(F32), jnp.zeros((4, half), F32)]
    )
    barrier = pltpu.get_barrier_semaphore()
    for device in at.values():
        pl.semaphore_signal(barrier, inc=1, device_id=device, device_id_type=MESH)
    pl.semaphore_wait(barrier, len(at))

    tasks, done = [], set()
    add = tasks.append
    gather_tokens(net, add, done, "x.", ((), ()), tok, s.xall, at, half, col, row, YROWS["x"])
    gather_tokens(net, add, done, "g.", (("x.p4",), ("x.r3", "x.r4", "x.l3", "x.l4")), cot, s.gall, at, half, col, row, YROWS["g"])
    nbc = net.go(s.nbs, s.nb.at[row], y1)
    gather_weights(net, add, done, wqkv, wup, wout, wdown, s, at, core, row)
    tabs = [net.local(ctab_h, s.ctab), net.local(stab_h, s.stab)]
    s.nb[row] = s.nbs[...]
    s.vec[...] = jnp.zeros_like(s.vec)
    s.dk[...] = jnp.zeros_like(s.dk)
    s.dv[...] = jnp.zeros_like(s.dv)

    def flat(values):
        values = values.astype(F32)
        return jnp.concatenate([values[k : k + 1, :] for k in range(values.shape[0])], axis=1)

    segr = flat(seg[...])
    s.segc[...] = jnp.broadcast_to(segr, (8, T)).T
    bq_all = bqkv[...].astype(F32)
    mine = row == 0
    bq = jnp.concatenate(
        [jnp.where(mine, bq_all[k : k + 1, :E], bq_all[k : k + 1, E:]) for k in range(3)], axis=1
    )
    bu_all = flat(bup[...])
    bu = jnp.where(mine, bu_all[:, :F], bu_all[:, F:])
    fcols = pl.ds(pl.multiple_of(row * F, F), F)
    gcols = pl.ds(pl.multiple_of(row * half, half), half)

    def wide(k):
        return jnp.concatenate([s.nb[0, k : k + 1, :], s.nb[1, k : k + 1, :]], axis=1)

    def params():
        yield (nbc,), 0.0
        nbc.wait_recv()
        for copy in tabs:
            copy.wait()
        done.add("nb")

    add(params())

    def norm(c):
        gain0, gain1, bias0, bias1 = wide(0), wide(1), wide(2), wide(3)

        @pl.loop(0, 2)
        def _(b):
            r = rows(c * 2 + b, 128)
            xv = s.xall[r, :].astype(F32)
            mean = jnp.sum(xv, axis=1, keepdims=True) * (1.0 / D)
            square = jnp.sum(xv * xv, axis=1, keepdims=True) * (1.0 / D)
            inv = lax.rsqrt(square - mean * mean + EPSILON)
            normed = (xv - mean) * inv
            s.mean[r, :] = mean
            s.inv[r, :] = inv
            s.ain[r, :] = (normed * gain0 + bias0).astype(BF)
            s.mim[r, :] = (normed * gain1 + bias1).astype(BF)

    def project(c):
        r = rows(c)
        pre = nn(s.ain[r, :], s.wq[...]) + bq
        cos, sin = s.ctab[r, :], s.stab[r, :]
        query = (turn(pre[:, :E], cos, sin)).astype(BF).astype(F32) * (1.0 / math.sqrt(HD))
        key = turn(pre[:, E : 2 * E], cos, sin).astype(BF).astype(F32)
        value = pre[:, 2 * E :].astype(BF).astype(F32)
        s.qs[r, :] = query.astype(BF)
        split_heads(s.qsm, r, query)
        split_heads(s.km, r, key)
        split_heads(s.vm, r, value)
        s.kt[:, r] = key.T.astype(BF)
        s.vt[:, r] = value.T.astype(BF)

    def expand(c):
        r = rows(c)
        pre = nn(s.mim[r, :], s.wu[...]) + bu
        cdf = 0.5 * (1.0 + lax.erf(pre * math.sqrt(0.5)))
        s.hid[r, :] = (pre * cdf).astype(BF)
        s.slope[r, :] = cdf + pre * jnp.exp(-0.5 * pre * pre) * (1.0 / math.sqrt(2.0 * math.pi))

    def contract(c):
        r = rows(c)
        back = (nt(s.gall[r, :], s.wd[...]) * s.slope[r, :]).astype(BF)
        s.hpg[r, :] = back
        s.vec[6:7, fcols] += jnp.sum(back.astype(F32), axis=0, keepdims=True)
        s.vec[4:5, gcols] += jnp.sum(s.gall[r, gcols].astype(F32), axis=0, keepdims=True)
        dout = nt(s.gall[r, :], s.wo[...]).astype(BF).astype(F32)
        s.do[r, :] = dout.astype(BF)
        split_heads(s.dom, r, dout)

    rb, lb, fb = lax.rem(col + 1, 4), lax.rem(col + 3, 4), lax.rem(col + 2, 4)
    blocks = {"own": col, "left": lb, "right": rb, "far": fb}
    outward = ("far", "right", "left", "own")

    def mark(flag, work, *args):
        def both():
            work(*args)
            done.add(flag)

        return both

    first = [0, 256, 768, 1536]

    def fold(values, how):
        return how(values.reshape(-1, 8, B), axis=0)

    def attend(i):
        q = pl.ds(i * B, B)
        for c in range(i + 1):
            kid = lax.broadcasted_iota(jnp.int32, (B, B), 0)
            qid = lax.broadcasted_iota(jnp.int32, (B, B), 1)
            allowed = s.segc[pl.ds(c * B, B), 0:1] == segr[:, i * B : (i + 1) * B]
            allowed = allowed & (kid <= qid) if c == i else allowed
            s.cap[pl.ds(c * B, B), :] = jnp.where(allowed, 3e38, -1e30)

        for h in range(2):
            top = jnp.full((8, B), -1e30, F32)
            for c in range(i + 1):
                k, at_c = pl.ds(c * B, B), pl.ds(first[i] + c * B, B)
                scores = jnp.minimum(nt(s.km[h, k, :], s.qs[q, :]), s.cap[k, :])
                s.probs[h, at_c, :] = scores
                top = jnp.maximum(top, fold(scores, jnp.max))
            top = jnp.max(top, axis=0, keepdims=True)
            total = jnp.zeros((8, B), F32)
            for c in range(i + 1):
                at_c = pl.ds(first[i] + c * B, B)
                expo = jnp.exp(s.probs[h, at_c, :] - top)
                s.probs[h, at_c, :] = expo
                total = total + fold(expo, jnp.sum)
            inverse = 1.0 / jnp.sum(total, axis=0, keepdims=True)
            hrows = pl.ds(h * HD, HD)
            mix = jnp.zeros((HD, B), F32)
            for c in range(i + 1):
                at_c = pl.ds(first[i] + c * B, B)
                probs = s.probs[h, at_c, :] * inverse
                s.probs[h, at_c, :] = probs
                mix = mix + nn(s.vt[hrows, pl.ds(c * B, B)], probs.astype(BF))
            s.mt[hrows, q] = mix.astype(BF)

        s.mixed[q, :] = s.mt[:, q].astype(F32).T.astype(BF)

    def attend_back(i):
        q = pl.ds(i * B, B)

        for h in range(2):
            inner = jnp.zeros((8, B), F32)
            for c in range(i + 1):
                k, at_c = pl.ds(c * B, B), pl.ds(first[i] + c * B, B)
                probs = s.probs[h, at_c, :]
                dprob = nt(s.vm[h, k, :], s.do[q, :])
                s.cap[k, :] = dprob
                inner = inner + fold(probs * dprob, jnp.sum)
                s.dv[k, :] += nn(probs.astype(BF), s.dom[h, q, :])
            inner = jnp.sum(inner, axis=0, keepdims=True)
            hrows = pl.ds(h * HD, HD)
            dquery = jnp.zeros((HD, B), F32)
            for c in range(i + 1):
                k, at_c = pl.ds(c * B, B), pl.ds(first[i] + c * B, B)
                dscore = (s.probs[h, at_c, :] * (s.cap[k, :] - inner)).astype(BF)
                s.dk[k, :] += nn(dscore, s.qsm[h, q, :])
                dquery = dquery + nn(s.kt[hrows, k], dscore)
            s.dqt[hrows, q] = dquery * (1.0 / math.sqrt(HD))

    def branch(b):
        r = rows(b)
        s.op[r, :] = (nn(s.mixed[r, :], s.wo[...]) + nn(s.hid[r, :], s.wd[...])).astype(BF)

    def down_grad():
        @pl.loop(0, 4)
        def _(b):
            r = rows(b, 128)
            s.g1[r, :] = tn(s.hid[:, r], s.gall[...]).astype(BF)

        s.g1[F:, :] = nn(s.mt[...], s.gall[...]).astype(BF)

    def up_grad():
        @pl.loop(0, 4)
        def _(b):
            r = rows(b, 128)
            s.g2[r, :] = tn(s.hpg[:, r], s.mim[...]).astype(BF)

    def qkv_grad(b):
        r = rows(b)
        cos, sin = s.ctab[r, :], -s.stab[r, :]
        dq = turn(s.dqt[:, r].T, cos, sin).astype(BF)
        dk = turn(s.dk[r, :], cos, sin).astype(BF)
        dv = s.dv[r, :].astype(BF)
        both = jnp.concatenate([dq, dk, dv], axis=1)
        s.qkvg[r, :] = both
        ecols3 = pl.ds(pl.multiple_of(row * 3 * E, 3 * E), 3 * E)
        s.vec[5:6, ecols3] += jnp.sum(both.astype(F32), axis=0, keepdims=True)

    def qkv_weight_grad():
        @pl.loop(0, 3)
        def _(b):
            r = rows(b, E)
            s.g3[r, :] = tn(s.qkvg[:, r], s.ain[...]).astype(BF)

    def input_grad(b):
        r = rows(b)
        gain0, gain1 = wide(0), wide(1)
        attn = nt(s.qkvg[r, :], s.wq[...])
        mlp = nt(s.hpg[r, :], s.wu[...])
        normed = (s.xall[r, :].astype(F32) - s.mean[r, :]) * s.inv[r, :]
        s.ng[r, :] = (attn * gain0 + mlp * gain1).astype(BF)
        s.vec[0:1, :] += jnp.sum(attn * normed, axis=0, keepdims=True)
        s.vec[1:2, :] += jnp.sum(mlp * normed, axis=0, keepdims=True)
        s.vec[2:3, :] += jnp.sum(attn, axis=0, keepdims=True)
        s.vec[3:4, :] += jnp.sum(mlp, axis=0, keepdims=True)

    so, sn = under(s, "o_"), under(s, "n_")
    where = dict(core=core, x=x, row=row)
    sums = []
    ny = YROWS["n"]
    own = rows(col)

    def look(h, total):
        mean, inv = s.mean[own, :], s.inv[own, :]
        xv = s.xall[pl.ds(pl.multiple_of(col * B, B), ny), pl.ds(h * half, half)].astype(F32)
        normed = (xv - mean[:ny]) * inv[:ny]
        sums.append(jnp.sum(total, axis=1, keepdims=True))
        sums.append(jnp.sum(total * normed, axis=1, keepdims=True))

    def write_out():
        xv = s.xall[own, gcols].astype(F32) + (flat(bout[...]) + flat(bdown[...]))
        total = jnp.concatenate([total_y(so, row), total_z(s.op, so, col, row, YROWS["o"])])
        out[...] = (xv + total).astype(BF)

    def write_grad():
        yield ("n.y.sum", "n.y.end", "n.z.sum"), 0.4
        mean, inv = s.mean[own, :], s.inv[own, :]
        normed = (s.xall[own, gcols].astype(F32) - mean) * inv
        zsum = total_z(s.ng, sn, col, row, ny)
        first_sum = jnp.concatenate([sums[0] + sums[2], jnp.sum(zsum, axis=1, keepdims=True)])
        second = jnp.sum(zsum * normed[ny:], axis=1, keepdims=True)
        second_sum = jnp.concatenate([sums[1] + sums[3], second])
        lane = lax.broadcasted_iota(jnp.int32, (B, 128), 1)
        s.ssend[...] = jnp.where(lane < 4, first_sum, second_sum).T[:8, :]
        ys = net.go(s.ssend, s.srecv, y1)
        yield (ys,), 0.5
        ys.wait_recv()
        both = (s.ssend[...] + s.srecv[...]) * (1.0 / D)
        both = jnp.concatenate([both] * 16).T
        total = jnp.concatenate([total_y(sn, row), zsum])
        tgrad[...] = (
            s.gall[own, gcols].astype(F32) + inv * (total - both[:, 0:1] - normed * both[:, 4:5])
        ).astype(BF)

    def write_vectors():
        vout[0] = s.vs[2]
        vout[1] = s.vs[3]

    scatter(net, add, done, "o.", tuple("send." + b for b in outward), s.op, so, at, col, row, YROWS["o"])
    scatter(net, add, done, "n.", tuple("ng." + b for b in outward), s.ng, sn, at, col, row, ny, look)
    gate = ("g.r3", "g.r4", "g.l3", "g.l4")
    for b in outward:
        add(later(("op." + b,) + gate, 0.0, mark("send." + b, lambda: None)))
    reduce_weights(net, add, done, "a.", "g1", s.g1, under(s, "r0_", fin=f0), at, where, ROWS[0])
    reduce_weights(net, add, done, "b.", "g2", s.g2, under(s, "r1_", fin=f1), at, where, ROWS[1])
    reduce_weights(net, add, done, "c.", "g3", s.g3, under(s, "r2_", fin=f2), at, where, ROWS[2])
    add(reduce_vectors(net, done, s, at))
    add(later(("vsum",), 0.05, write_vectors))
    add(write_grad())
    for name, b in blocks.items():
        add(later(("nb", "x." + name), 0.5, mark("norm." + name, norm, b)))
        add(later(("wq", "norm." + name), 0.45, mark("proj." + name, project, b)))
    needs = tuple("proj." + name for name in blocks)
    for i in range(4):
        add(later(needs, 0.37 * (i + 1), mark(f"attf{i}", attend, i)))
        needs = (f"attf{i}",)
    for name, b in blocks.items():
        add(later(("wu", "norm." + name), 0.36, mark("exp." + name, expand, b)))
    for name in outward:
        needs = ("wo", "wd", "attf3", "exp." + name)
        add(later(needs, 0.55, mark("op." + name, branch, blocks[name])))
    for name, b in blocks.items():
        needs = ("wo", "wd", "g." + name, "exp." + name)
        add(later(needs, 0.43, mark("con." + name, contract, b)))
    allg = tuple("g." + name for name in blocks) + tuple("exp." + name for name in blocks)
    add(later(allg + ("attf3",), 2.5, mark("g1", down_grad)))
    allc = tuple("con." + name for name in blocks)
    add(later(allc, 2.2, mark("g2", up_grad)))
    needs = allc + ("attf3",)
    for i in range(4):
        add(later(needs, 0.43 * (i + 1), mark(f"attb{i}", attend_back, i)))
        needs = (f"attb{i}",)
    for name in outward:
        add(later(("attb3",), 0.26, mark("qg." + name, qkv_grad, blocks[name])))
    add(later(tuple("qg." + name for name in blocks), 1.4, mark("g3", qkv_weight_grad)))
    for name in outward:
        add(later(("qg." + name,), 0.68, mark("ng." + name, input_grad, blocks[name])))
    add(later(tuple("ng." + name for name in blocks), 0.0, mark("vec", lambda: None)))
    add(later(("o.y.end", "o.z.sum"), 0.3, mark("out", write_out)))
    run(tasks, done)
    for copy in net.sent:
        copy.wait_send()


def tables():
    freq = np.arange(ROT // 2, dtype=np.float32)
    inverse = np.float32(10000.0) ** (np.float32(-2.0) * freq / np.float32(ROT))
    angle = np.arange(T, dtype=np.float32)[:, None] * inverse[None, :].astype(np.float32)
    cos, sin = np.cos(angle), np.sin(angle)
    ones, zeros = np.ones((T, HD - ROT), np.float32), np.zeros((T, HD - ROT), np.float32)
    ctab = np.concatenate([cos, cos, ones] * 2, axis=1)
    stab = np.concatenate([-sin, sin, zeros] * 2, axis=1)
    return ctab.astype(np.float32), stab.astype(np.float32)


def last(
    f0_h, f1_h, f2_h, vec_h, out_h, tgrad_h,
    out_o, tgrad_o, wq_o, bq_o, wo_o, bo_o, wu_o, bu_o, wd_o, bd_o, gain_o, bias_o,
    f0, f1, f2, vec, out, tgrad, wq, wo, wu, wd, sems,
):
    row = lax.axis_index("row")
    copies = []

    def write(src, dst):
        copy = pltpu.make_async_copy(src, dst, sems.at[len(copies)])
        copy.start()
        copies.append(copy)
        return copy

    pairs = ((f0_h, f0), (f1_h, f1), (f2_h, f2), (vec_h, vec), (out_h, out), (tgrad_h, tgrad))
    reads = [write(a, b) for a, b in pairs]
    reads[0].wait()
    for r in range(2):
        for k in range(8):
            piece = f0[k // 4, k % 4, r].astype(F32)
            n = piece.shape[0]
            inside = max(0, min(n, F - k * n))
            if inside:
                wd[pl.ds(r * F + k * n, inside), :] = piece[:inside]
            if inside < n:
                wo[pl.ds(r * E + k * n + inside - F, n - inside), :] = piece[inside:]
        write(wd.at[pl.ds(r * F, F)], wd_o.at[pl.ds(r * F, F)])
    write(wo, wo_o)
    reads[1].wait()
    for r in range(2):
        for k in range(4):
            pair = [f1[(2 * k + h) // 4, (2 * k + h) % 4, r].astype(F32) for h in range(2)]
            wu[:, pl.ds(r * F + k * E, E)] = jnp.concatenate(pair).T
        write(wu.at[:, pl.ds(r * F, F)], wu_o.at[:, pl.ds(r * F, F)])
    reads[2].wait()
    for r in range(2):
        whole = jnp.concatenate([f2[k // 4, k % 4, r].astype(F32) for k in range(8)])
        for k in range(3):
            wq[k, :, pl.ds(r * E, E)] = whole[k * E : (k + 1) * E].T
    write(wq, wq_o)
    for copy in reads[3:]:
        copy.wait()
    write(out, out_o)
    write(tgrad, tgrad_o)
    half = D // 2
    left = row == 0

    def cut(values):
        return jnp.where(left, values[:, :half], values[:, half:])

    bo_o[...] = cut(vec[0, 4:5, :])
    bd_o[...] = cut(vec[0, 4:5, :])
    for k in range(3):
        bq_o[k : k + 1, :E] = vec[0, 5:6, k * E : (k + 1) * E]
        bq_o[k : k + 1, E:] = vec[0, 5:6, (k + 3) * E : (k + 4) * E]
    bu_o[...] = vec[0, 6:7, :]
    gain_o[...] = cut(vec[1, 0:2, :])
    bias_o[...] = cut(vec[1, 2:4, :])
    for copy in copies[len(reads) :]:
        copy.wait()


def on_device(
    tokens, segment_ids, w_qkv, b_qkv, w_out, b_out, w_up, b_up, w_down, b_down, norm_gain, norm_bias, cotangent
):
    ctab, stab = tables()
    vmem = pl.BlockSpec(memory_space=pltpu.VMEM)
    hbm = pl.BlockSpec(memory_space=pl.ANY)
    shape = jax.ShapeDtypeStruct
    early = [
        shape((2, 4, 2, ROWS[0] // 8, D // 2), BF),
        shape((2, 4, 2, ROWS[1] // 8, D // 2), BF),
        shape((2, 4, 2, ROWS[2] // 8, D // 2), BF),
        shape((2, 8, D), F32),
    ]
    out, tgrad, f0, f1, f2, vec = pl.pallas_call(
        body,
        out_shape=[
            shape((B, D // 2), BF),
            shape((B, D // 2), BF),
            *early,
        ],
        in_specs=[hbm] * 6 + [vmem] * 7 + [hbm] * 2,
        out_specs=[vmem] * 6,
        scratch_shapes=[pltpu.VMEM(*spec) for spec in SCRATCH.values()]
        + [pltpu.SemaphoreType.DMA((NSEM,)), pltpu.SemaphoreType.DMA((NSEM,))],
        compiler_params=pltpu.CompilerParams(
            collective_id=0, has_side_effects=True, vmem_limit_bytes=60 * 1024 * 1024
        ),
        name="block",
    )(
        tokens, cotangent, w_qkv, w_out, w_up, w_down, b_qkv, b_up.reshape(8, 128),
        b_out.reshape(4, 128), b_down.reshape(4, 128), norm_gain, norm_bias,
        segment_ids.reshape(8, 128), jnp.asarray(ctab), jnp.asarray(stab),
    )
    big = [
        ((3, D // 2, 2 * E), F32),
        ((2 * E, D // 2), F32),
        ((D // 2, 2 * F), F32),
        ((2 * F, D // 2), F32),
    ]
    results = pl.pallas_call(
        last,
        out_shape=[
            shape((B, D // 2), BF),
            shape((B, D // 2), BF),
            shape(*big[0]),
            shape((3, 2 * E), F32),
            shape(*big[1]),
            shape((1, D // 2), F32),
            shape(*big[2]),
            shape((1, 2 * F), F32),
            shape(*big[3]),
            shape((1, D // 2), F32),
            shape((2, D // 2), F32),
            shape((2, D // 2), F32),
        ],
        in_specs=[hbm] * 6,
        out_specs=[hbm, hbm, hbm, vmem, hbm, vmem, hbm, vmem, hbm, vmem, vmem, vmem],
        scratch_shapes=[pltpu.VMEM(e.shape, e.dtype) for e in early]
        + [pltpu.VMEM((B, D // 2), BF)] * 2
        + [pltpu.VMEM(*spec) for spec in big]
        + [pltpu.SemaphoreType.DMA((16,))],
        compiler_params=pltpu.CompilerParams(vmem_limit_bytes=60 * 1024 * 1024),
        name="last",
    )(f0, f1, f2, vec, out, tgrad)
    out, tgrad, wq, bq, wo, bo, wu, bu, wd, bd, gain, bias = results
    bo, bu, bd = bo.reshape(-1), bu.reshape(-1), bd.reshape(-1)
    return (out, tgrad, wq, bq, wo, bo, wu, bu, wd, bd, gain, bias)


def solution(mesh):
    in_specs = (
        P(("dp", "col"), "row"),
        P("dp"),
        P(None, "row", "col"),
        P(None, "col"),
        P("col", "row"),
        P("row"),
        P("row", "col"),
        P("col"),
        P("col", "row"),
        P("row"),
        P(None, "row"),
        P(None, "row"),
        P(("dp", "col"), "row"),
    )
    out_specs = (
        P(("dp", "col"), "row"),
        P(("dp", "col"), "row"),
        P(None, "row", "col"),
        P(None, "col"),
        P("col", "row"),
        P("row"),
        P("row", "col"),
        P("col"),
        P("col", "row"),
        P("row"),
        P(None, "row"),
        P(None, "row"),
    )
    return jax.shard_map(
        on_device, mesh=mesh, in_specs=in_specs, out_specs=out_specs, check_vma=False
    )
```

```python
from functools import partial
from types import SimpleNamespace
import math

import numpy as np
import jax
import jax.numpy as jnp
from jax import lax
from jax.experimental import pallas as pl
from jax.experimental.pallas import tpu as pltpu
from jax.sharding import PartitionSpec as P

MESH = pl.DeviceIdType.MESH
BF = jnp.bfloat16
F32 = jnp.float32
T = 1024
D = 1024
HD = 64
ROT = 16
E = 128
F = 512
B = 256
EPSILON = 1e-05
NSEM = 200
YROWS = dict(x=112, g=144, o=160, n=176)


ORDER = (
    0, 8, 1, 4, 5, 9, 2, 3, 44, 44, 2, 10, 6, 4, 12, 3, 11, 7, 40, 5, 9, 8, 13, 16, 131, 40, 132,
    10, 6, 21, 25, 23, 14, 29, 24, 12, 18, 135, 41, 136, 7, 20, 28, 22, 15, 42, 13, 41, 143, 11, 17,
    14, 133, 42, 144, 134, 145, 23, 31, 24, 27, 32, 15, 19, 137, 138, 146, 43, 139, 140, 25, 22, 29,
    30, 26, 33, 141, 27, 35, 43, 142, 28, 36, 149, 151, 31, 26, 34, 33, 81, 51, 47, 148, 80, 50, 46,
    150, 82, 48, 147, 32, 79, 49, 52, 53, 38, 45, 153, 30, 37, 152, 35, 34, 39, 155, 47, 57, 83,
    154, 46, 56, 156, 52, 53, 97, 48, 54, 83, 84, 86, 45, 55, 59, 58, 88, 87, 85, 157, 158, 159, 88,
    87, 89, 97, 99, 100, 98, 102, 101, 54, 61, 160, 59, 58, 89, 60, 90, 162, 161, 164, 163, 165,
    111, 102, 60, 101, 103, 61, 166, 62, 66, 171, 168, 111, 113, 114, 70, 68, 112, 64, 116, 90, 91,
    103, 104, 92, 115, 167, 69, 67, 63, 62, 72, 169, 65, 170, 128, 64, 69, 70, 71, 74, 116, 76, 115,
    117, 128, 91, 93, 92, 94, 95, 104, 106, 105, 93, 94, 63, 75, 73, 117, 118, 75, 76, 65, 77, 128,
    95, 96, 71, 78, 118, 120, 119, 105, 107, 106, 109, 108, 77, 107, 96, 125, 128, 108, 119, 121,
    120, 122, 123, 121, 122, 78, 130, 109, 110, 128, 129, 123, 124, 130, 110, 126, 124, 127,
)


def nn(a, b):
    return jnp.dot(a, b, preferred_element_type=F32)


def nt(a, b):
    return lax.dot_general(a, b, (((1,), (1,)), ((), ())), preferred_element_type=F32)


def tn(a, b):
    return lax.dot_general(a, b, (((0,), (0,)), ((), ())), preferred_element_type=F32)


def rows(block, size=B):
    return pl.ds(pl.multiple_of(block * size, size), size)


class Net:
    def __init__(self, send, recv):
        self.send, self.recv, self.count, self.sent = send, recv, 0, []

    def go(self, src, dst, device):
        k = self.count
        self.count += 1
        assert k < NSEM
        copy = pltpu.make_async_remote_copy(
            src_ref=src,
            dst_ref=dst,
            send_sem=self.send.at[k],
            recv_sem=self.recv.at[k],
            device_id=device,
            device_id_type=MESH,
        )
        copy.start()
        self.sent.append(copy)
        return copy

    def local(self, src, dst):
        k = self.count
        self.count += 1
        assert k < NSEM
        copy = pltpu.make_async_copy(src, dst, self.send.at[k])
        copy.start()
        return copy


def later(deps, cost, work):
    yield deps, cost
    work()


def gather_tokens(net, add, done, name, begin, own, full, at, half, col, row, yr):
    right, left, peer = at["z1"], at["z3"], at["y1"]
    zr = B - yr
    part = zr // 32 * 16
    cut = yr + part
    c = {}

    def place(b, h, start=0, size=B):
        r = pl.ds(pl.multiple_of(b * B + start, 16), size)
        return full.at[r, pl.ds(pl.multiple_of(h * half, half), half)]

    def move(key, device, *where):
        c[key] = net.go(place(*where), place(*where), device)
        done.add(name + key)

    def send(key, device, start, size):
        c[key] = net.go(own.at[pl.ds(start, size)], place(col, row, start, size), device)
        done.add(name + key)

    lcol, rcol, fcol = lax.rem(col + 3, 4), lax.rem(col + 1, 4), lax.rem(col + 2, 4)

    def begin_y():
        yield begin[0], 0.1
        c["keep"] = net.local(own, place(col, row))
        send("p0", peer, 0, yr)
        send("p1", peer, yr, zr)
        c["keep"].wait()
        done.add(name + "keep")

    def begin_z():
        yield begin[1], 0.1
        send("r1", right, yr, zr)
        send("l1", left, yr, zr)
        send("r0", right, 0, yr)
        send("l0", left, 0, yr)

    def hop(keys, *work):
        yield tuple(name + k for k in keys), 0.0
        yield tuple(c[k] for k in keys), 0.05
        for k in keys:
            c[k].wait_recv()
        for w in work:
            move(*w)
        done.update(name + k + "!" for k in keys)

    def whole(flag, keys):
        yield tuple(name + k + ("" if k == "keep" else "!") for k in keys), 0.0
        done.add(name + flag)

    add(begin_y())
    add(begin_z())
    add(hop(["p0"], ("r2", right, col, 1 - row, 0, yr), ("l2", left, col, 1 - row, 0, yr)))
    add(hop(["r1"], ("r3", right, lcol, row, yr, part), ("p2", peer, lcol, row, yr, zr)))
    add(hop(["l1"], ("l3", left, rcol, row, cut, B - cut), ("p3", peer, rcol, row, yr, zr)))
    add(hop(["r0"], ("r4", right, lcol, row, 0, yr)))
    add(hop(["l2"], ("l4", left, rcol, 1 - row, 0, yr)))
    add(hop(["r3", "l3"], ("p4", peer, fcol, row, yr, zr)))
    add(hop(["p1"]))
    add(hop(["l0"]))
    add(hop(["r2"]))
    add(hop(["p2"]))
    add(hop(["p3"]))
    add(hop(["r4"]))
    add(hop(["l4"]))
    add(hop(["p4"]))
    add(whole("own", ["p0", "p1", "keep"]))
    add(whole("left", ["r0", "r1", "r2", "p2"]))
    add(whole("right", ["l0", "l1", "l2", "p3"]))
    add(whole("far", ["r3", "r4", "l3", "l4", "p4"]))


def gather_weights(net, add, done, wqkv, wup, wout, wdown, s, at, core, row):
    half, part = D // 2, D // 4
    mine, theirs = row, 1 - row
    drows, ocols = rows(row, half), rows(1 - row, half)

    def cut(which, size):
        return pl.ds(pl.multiple_of(which * size, size), size)

    local = {}
    for k in range(3):
        kcols = pl.ds(k * E, E)
        local[k] = net.local(wqkv.at[k, :, cut(mine, E)], s.wq.at[drows, kcols])
    local["u"] = net.local(wup.at[:, cut(mine, F)], s.wu.at[drows])
    local["o"] = net.local(wout.at[cut(mine, E)], s.wo.at[:, drows])
    local["d"] = net.local(wdown.at[cut(mine, F)], s.wd.at[:, drows])
    src, dst, got = cut(core, part), cut(row * 2 + core, part), cut((1 - row) * 2 + core, part)
    far, near = at["y3"], at["core"]
    q = [
        net.go(wqkv.at[k, src, cut(theirs, E)], s.wq.at[dst, pl.ds(k * E, E)], far)
        for k in range(3)
    ]
    u = net.go(wup.at[src, cut(theirs, F)], s.wu.at[dst], far)
    o = net.go(wout.at[cut(theirs * 2 + core, E // 2)], s.wo.at[cut(core, E // 2), drows], far)
    d = net.go(wdown.at[cut(theirs * 2 + core, F // 2)], s.wd.at[cut(core, F // 2), drows], far)

    def share(flag, copies, view, locals_):
        yield tuple(copies), 0.05
        for copy in copies:
            copy.wait_recv()
        second = net.go(view, view, near)
        yield (second,), 0.0
        second.wait_recv()
        for k in locals_:
            local[k].wait()
        done.add(flag)

    add(share("wq", q, s.wq.at[got], range(3)))
    add(share("wu", [u], s.wu.at[got], "u"))
    add(share("wo", [o], s.wo.at[cut(core, E // 2), ocols], "o"))
    add(share("wd", [d], s.wd.at[cut(core, F // 2), ocols], "d"))


def ring_scatter(net, add, done, name, part, bufs, me, right, left, width, ready):
    ta, tb, inl, inr = bufs
    lo, hi = pl.ds(0, width), pl.ds(width, width)
    far, rb, lb = lax.rem(me + 2, 4), lax.rem(me + 1, 4), lax.rem(me + 3, 4)
    c = {}

    def send(deps, *sends):
        yield deps, 0.05
        for key, src, dst, device in sends:
            c[key] = net.go(src, dst, device)
            done.add(name + key)

    def through(came, flag, buf, view, key, dst, device):
        yield (name + came, flag), 0.0
        yield (c[came],), 0.15
        c[came].wait_recv()
        view[...] = (view[...].astype(F32) + buf[...].astype(F32)).astype(BF)
        c[key] = net.go(view, dst, device)
        done.add(name + key)

    def finish():
        yield tuple(name + k for k in "cdef") + (ready[3],), 0.0
        yield tuple(c[k] for k in "cdef"), 0.0
        for k in "cdef":
            c[k].wait_recv()
        done.add(name + "sum")

    add(send((ready[0],), ("a", part(far, lo), ta, right), ("b", part(far, hi), tb, left)))
    add(send((ready[1],), ("c", part(rb, hi), inl.at[:, hi], right)))
    add(send((ready[2],), ("d", part(lb, lo), inr.at[:, lo], left)))
    add(through("a", ready[1], ta, part(rb, lo), "e", inl.at[:, lo], right))
    add(through("b", ready[2], tb, part(lb, hi), "f", inr.at[:, hi], left))
    add(finish())


def reduce_weights(net, add, done, name, begin, grad, s, at, me, n):
    core, x, row = me["core"], me["x"], me["row"]
    half, size = n // 2, n // 8
    base, away = core * half, (1 - core) * half
    x1, x3, near = at["x1"], at["x3"], at["core"]
    lx, rx, fx = lax.rem(x + 3, 4), lax.rem(x + 1, 4), lax.rem(x + 2, 4)
    c = {}

    def start():
        yield (begin,), 0.05
        copy = net.go(grad.at[pl.ds(pl.multiple_of(away, half), half)], s.rc, near)
        yield (copy,), 0.4 * n / 640
        copy.wait_recv()
        own = grad.at[pl.ds(pl.multiple_of(base, half), half)]
        own[...] = (own[...].astype(F32) + s.rc[...].astype(F32)).astype(BF)
        done.add(name + "core")

    def part(block, cols):
        return grad.at[pl.ds(pl.multiple_of(base + block * size, size), size), cols]

    def across():
        yield (name + "sum",), 0.2
        for h in range(2):
            cols = pl.ds(h * (D // 2), D // 2)
            total = part(x, cols)[...].astype(F32) + s.inl[:, cols].astype(F32)
            s.sy[h] = (total + s.inr[:, cols].astype(F32)).astype(BF)
        g0 = net.go(s.sy.at[row], s.ry.at[0], at["y2"])
        g1 = net.go(s.sy.at[1 - row], s.ry.at[1], at["y1"])
        g2 = net.go(s.sy.at[1 - row], s.ry.at[2], at["y3"])
        yield (g0, g1, g2), 0.15
        for copy in (g0, g1, g2):
            copy.wait_recv()
        s.fin[core, x, row] = (s.sy[row].astype(F32) + s.ry[0].astype(F32)).astype(BF)
        s.fin[core, x, 1 - row] = (s.ry[1].astype(F32) + s.ry[2].astype(F32)).astype(BF)
        for key, h, device in (("a", 0, x1), ("b", 1, x3), ("c", 1, x1), ("d", 0, x3)):
            view = s.fin.at[core, x, h]
            c[key] = net.go(view, view, device)
        view = s.fin.at[core, x]
        c["k"] = net.go(view, view, near)
        done.add(name + "sent")

    def hop(keys, flag, view, device, key, need=()):
        yield (name + flag,) + tuple(name + k + "!" for k in need), 0.0
        yield tuple(c[k] for k in keys), 0.05
        for k in keys:
            c[k].wait_recv()
        c[key] = net.go(view, view, device)
        done.update(name + k + "!" for k in keys)
        done.add(name + key)

    def end():
        yield tuple(name + k for k in ("l", "m", "n")), 0.0
        yield tuple(c[k] for k in "klmn"), 0.0
        for k in "klmn":
            c[k].wait_recv()
        done.add(name + "end")

    ready = (name + "core",) * 4
    add(start())
    ring_scatter(
        net, add, done, name, part, (s.ta, s.tb, s.inl, s.inr), x, x1, x3, D // 2, ready
    )
    add(across())
    add(hop("a", "sent", s.fin.at[core, lx, 0], x1, "p"))
    add(hop("b", "sent", s.fin.at[core, rx, 1], x3, "q"))
    add(hop("c", "sent", s.fin.at[core, lx], near, "l", "a"))
    add(hop("d", "sent", s.fin.at[core, rx], near, "m", "b"))
    add(hop("pq", "p", s.fin.at[core, fx], near, "n", "b"))
    add(end())


def reduce_vectors(net, done, s, at):
    yield ("vec",), 0.0
    c = net.go(s.vec, s.vr.at[0], at["core"])
    yield (c,), 0.05
    c.wait_recv()
    s.vs[0] = s.vec[...] + s.vr[0]
    for n, axis in enumerate("xyz"):
        copies = [net.go(s.vs.at[n], s.vr.at[3 * n + k], at[axis + str(k)]) for k in (1, 2, 3)]
        yield tuple(copies), 0.05
        for copy in copies:
            copy.wait_recv()
        s.vs[n + 1] = (s.vs[n] + s.vr[3 * n + 1]) + (s.vr[3 * n + 2] + s.vr[3 * n + 3])
    done.add("vsum")


def scatter(net, add, done, name, ready, p, s, at, col, row, yr, look=None):
    half, zr = D // 2, B - yr
    far, rb, lb = lax.rem(col + 2, 4), lax.rem(col + 1, 4), lax.rem(col + 3, 4)
    mcols, ocols = rows(row, half), rows(1 - row, half)
    right, left, peer = at["z1"], at["z3"], at["y1"]

    def yrows(b):
        return pl.ds(pl.multiple_of(b * B, B), yr)

    def zrows(b):
        return pl.ds(pl.multiple_of(b * B + yr, 16), zr)

    def zpart(b, cols):
        return p.at[zrows(b), pl.ds(pl.multiple_of(row * half + cols.start, 256), cols.size)]

    def pair(k, b):
        yield (ready[k],), 0.05
        copy = net.go(p.at[zrows(b), ocols], s.ry.at[k], peer)
        yield (copy,), 0.15
        copy.wait_recv()
        view = p.at[zrows(b), mcols]
        view[...] = (view[...].astype(F32) + s.ry[k].astype(F32)).astype(BF)
        done.add(name + "z" + str(k))

    def last():
        yield (name + "y.sum",), 0.3
        for h in range(2):
            cols = pl.ds(h * half, half)
            total = p[yrows(col), cols].astype(F32) + s.inl[:, cols].astype(F32)
            total += s.inr[:, cols].astype(F32)
            s.ysend[h] = total.astype(BF)
            if look is not None:
                look(h, total)
        copy = net.go(s.ysend.at[1 - row], s.yrecv, peer)
        yield (copy,), 0.0
        copy.wait_recv()
        done.add(name + "y.end")

    for k, b in enumerate((far, rb, lb, col)):
        add(pair(k, b))
    ring_scatter(
        net, add, done, name + "y.", lambda b, cols: p.at[yrows(b), cols],
        (s.ta, s.tb, s.inl, s.inr), col, right, left, half, ready,
    )
    ring_scatter(
        net, add, done, name + "z.", zpart,
        (s.ta2, s.tb2, s.inl2, s.inr2), col, right, left, half // 2,
        tuple(name + "z" + str(k) for k in range(4)),
    )
    add(last())


def total_y(s, row):
    return s.ysend[row].astype(F32) + s.yrecv[...].astype(F32)


def total_z(p, s, col, row, yr):
    own = p[pl.ds(pl.multiple_of(col * B + yr, 16), B - yr), rows(row, D // 2)]
    return own.astype(F32) + s.inl2[...].astype(F32) + s.inr2[...].astype(F32)


def run(tasks, done):
    asked = [next(task)[0] for task in tasks]
    for k in ORDER:
        for need in asked[k]:
            assert not isinstance(need, str) or need in done, "order"
        asked[k] = next(tasks[k], ((),))[0]
    assert all(next(task, None) is None for task in tasks), "unfinished"


def turn(values, cos, sin):
    lane = lax.broadcasted_iota(jnp.int32, values.shape, 1)
    other = jnp.where(lane % HD < ROT // 2, pltpu.roll(values, E - ROT // 2, 1), pltpu.roll(values, ROT // 2, 1))
    return values * cos + other * sin


def split_heads(ref, at_rows, values):
    lane = lax.broadcasted_iota(jnp.int32, values.shape, 1)
    zero = jnp.zeros_like(values)
    ref[0, at_rows, :] = jnp.where(lane < HD, values, zero).astype(BF)
    ref[1, at_rows, :] = jnp.where(lane < HD, zero, values).astype(BF)


SCRATCH = dict(
    xall=((T, D), BF),
    gall=((T, D), BF),
    ain=((T, D), BF),
    mim=((T, D), BF),
    wq=((D, 3 * E), BF),
    wo=((E, D), BF),
    wu=((D, F), BF),
    wd=((F, D), BF),
    nb=((2, 8, D // 2), F32),
    mean=((T, 1), F32),
    inv=((T, 1), F32),
    hid=((T, F), BF),
    slope=((T, F), F32),
    segc=((T, 8), F32),
    nbs=((8, D // 2), F32),
    hpg=((T, F), BF),
    qs=((T, E), BF),
    qsm=((2, T, E), BF),
    km=((2, T, E), BF),
    vm=((2, T, E), BF),
    kt=((E, T), BF),
    vt=((E, T), BF),
    do=((T, E), BF),
    dom=((2, T, E), BF),
    probs=((2, 2560, B), F32),
    mt=((E, T), BF),
    mixed=((T, E), BF),
    dqt=((E, T), F32),
    cap=((T, B), F32),
    dk=((T, E), F32),
    dv=((T, E), F32),
    qkvg=((T, 3 * E), BF),
    op=((T, D), BF),
    ng=((T, D), BF),
    ctab=((T, E), F32),
    stab=((T, E), F32),
    ssend=((8, B), F32),
    srecv=((8, B), F32),
    g1=((F + E, D), BF),
    g2=((F, D), BF),
    g3=((3 * E, D), BF),
    f0=((2, 4, 2, (F + E) // 8, D // 2), BF),
    f1=((2, 4, 2, F // 8, D // 2), BF),
    f2=((2, 4, 2, 3 * E // 8, D // 2), BF),
    vec=((8, D), F32),
    vr=((10, 8, D), F32),
    vs=((4, 8, D), F32),
)
def scatter_scratch(yr):
    zr = B - yr
    return dict(
        ta=((yr, D // 2), BF),
        tb=((yr, D // 2), BF),
        inl=((yr, D), BF),
        inr=((yr, D), BF),
        ry=((4, zr, D // 2), BF),
        ta2=((zr, D // 4), BF),
        tb2=((zr, D // 4), BF),
        inl2=((zr, D // 2), BF),
        inr2=((zr, D // 2), BF),
        ysend=((2, yr, D // 2), BF),
        yrecv=((yr, D // 2), BF),
    )


def reduce_scratch(n):
    return dict(
        rc=((n // 2, D), BF),
        ta=((n // 8, D // 2), BF),
        tb=((n // 8, D // 2), BF),
        inl=((n // 8, D), BF),
        inr=((n // 8, D), BF),
        sy=((2, n // 8, D // 2), BF),
        ry=((3, n // 8, D // 2), BF),
    )


ROWS = (F + E, F, 3 * E)
for name in "on":
    SCRATCH.update({name + "_" + key: v for key, v in scatter_scratch(YROWS[name]).items()})
for k, n in enumerate(ROWS):
    SCRATCH.update({f"r{k}_{key}": spec for key, spec in reduce_scratch(n).items()})


def under(s, prefix, **more):
    picked = {k[len(prefix) :]: v for k, v in vars(s).items() if k.startswith(prefix)}
    return SimpleNamespace(**picked, **more)


def body(
    tok, cot, wqkv, wout, wup, wdown, bqkv, bup, bout, bdown, gain, bias, seg, ctab_h, stab_h,
    out, tgrad, f0_h, f1_h, f2_h, vout, *scratch,
):
    s = SimpleNamespace(**dict(zip(SCRATCH, scratch)))
    send, recv = scratch[len(SCRATCH) :]
    net = Net(send, recv)
    dp, row, col = lax.axis_index("dp"), lax.axis_index("row"), lax.axis_index("col")
    core, x, yh = lax.rem(dp, 2), lax.rem(dp // 2, 4), dp // 8
    half = D // 2

    def dev(core=core, x=x, yh=yh, row=row, col=col):
        return (yh * 8 + x * 2 + core, row, col)

    at = {"core": dev(core=1 - core)}
    for k in (1, 2, 3):
        at[f"x{k}"] = dev(x=lax.rem(x + k, 4))
        at[f"z{k}"] = dev(col=lax.rem(col + k, 4))
    at["y1"] = dev(row=1 - row)
    at["y2"] = dev(yh=1 - yh)
    at["y3"] = dev(yh=1 - yh, row=1 - row)
    y1 = at["y1"]

    s.nbs[...] = jnp.concatenate(
        [gain[...].astype(F32), bias[...].astype(F32), jnp.zeros((4, half), F32)]
    )
    barrier = pltpu.get_barrier_semaphore()
    for device in at.values():
        pl.semaphore_signal(barrier, inc=1, device_id=device, device_id_type=MESH)
    pl.semaphore_wait(barrier, len(at))

    tasks, done = [], set()
    add = tasks.append
    gather_tokens(net, add, done, "x.", ((), ()), tok, s.xall, at, half, col, row, YROWS["x"])
    gather_tokens(net, add, done, "g.", (("x.p4",), ("x.r3", "x.r4", "x.l3", "x.l4")), cot, s.gall, at, half, col, row, YROWS["g"])
    nbc = net.go(s.nbs, s.nb.at[row], y1)
    gather_weights(net, add, done, wqkv, wup, wout, wdown, s, at, core, row)
    tabs = [net.local(ctab_h, s.ctab), net.local(stab_h, s.stab)]
    def flat(values):
        values = values.astype(F32)
        return jnp.concatenate([values[k : k + 1, :] for k in range(values.shape[0])], axis=1)

    rowv = {}
    fcols = pl.ds(pl.multiple_of(row * F, F), F)
    gcols = pl.ds(pl.multiple_of(row * half, half), half)

    def wide(k):
        return jnp.concatenate([s.nb[0, k : k + 1, :], s.nb[1, k : k + 1, :]], axis=1)

    def params():
        yield ("x.r0", "x.p1"), 0.4
        s.nb[row] = s.nbs[...]
        s.vec[...] = jnp.zeros_like(s.vec)
        s.dk[...] = jnp.zeros_like(s.dk)
        s.dv[...] = jnp.zeros_like(s.dv)
        rowv["seg"] = flat(seg[...])
        s.segc[...] = jnp.broadcast_to(rowv["seg"], (8, T)).T
        bq_all, bu_all, mine = bqkv[...].astype(F32), flat(bup[...]), row == 0
        parts = [
            jnp.where(mine, bq_all[k : k + 1, :E], bq_all[k : k + 1, E:]) for k in range(3)
        ]
        rowv["bq"] = jnp.concatenate(parts, axis=1)
        rowv["bu"] = jnp.where(mine, bu_all[:, :F], bu_all[:, F:])
        yield (nbc,), 0.0
        nbc.wait_recv()
        for copy in tabs:
            copy.wait()
        done.add("nb")

    add(params())

    def norm(c):
        gain0, gain1, bias0, bias1 = wide(0), wide(1), wide(2), wide(3)

        @pl.loop(0, 2)
        def _(b):
            r = rows(c * 2 + b, 128)
            xv = s.xall[r, :].astype(F32)
            mean = jnp.sum(xv, axis=1, keepdims=True) * (1.0 / D)
            square = jnp.sum(xv * xv, axis=1, keepdims=True) * (1.0 / D)
            inv = lax.rsqrt(square - mean * mean + EPSILON)
            normed = (xv - mean) * inv
            s.mean[r, :] = mean
            s.inv[r, :] = inv
            s.ain[r, :] = (normed * gain0 + bias0).astype(BF)
            s.mim[r, :] = (normed * gain1 + bias1).astype(BF)

    def project(c):
        r = rows(c)
        pre = nn(s.ain[r, :], s.wq[...]) + rowv["bq"]
        cos, sin = s.ctab[r, :], s.stab[r, :]
        query = (turn(pre[:, :E], cos, sin)).astype(BF).astype(F32) * (1.0 / math.sqrt(HD))
        key = turn(pre[:, E : 2 * E], cos, sin).astype(BF).astype(F32)
        value = pre[:, 2 * E :].astype(BF).astype(F32)
        s.qs[r, :] = query.astype(BF)
        split_heads(s.qsm, r, query)
        split_heads(s.km, r, key)
        split_heads(s.vm, r, value)
        s.kt[:, r] = key.T.astype(BF)
        s.vt[:, r] = value.T.astype(BF)

    def expand(c):
        r = rows(c)
        pre = nn(s.mim[r, :], s.wu[...]) + rowv["bu"]
        cdf = 0.5 * (1.0 + lax.erf(pre * math.sqrt(0.5)))
        s.hid[r, :] = (pre * cdf).astype(BF)
        s.slope[r, :] = cdf + pre * jnp.exp(-0.5 * pre * pre) * (1.0 / math.sqrt(2.0 * math.pi))

    def contract(c):
        r = rows(c)
        back = (nt(s.gall[r, :], s.wd[...]) * s.slope[r, :]).astype(BF)
        s.hpg[r, :] = back
        s.vec[6:7, fcols] += jnp.sum(back.astype(F32), axis=0, keepdims=True)
        s.vec[4:5, gcols] += jnp.sum(s.gall[r, gcols].astype(F32), axis=0, keepdims=True)
        dout = nt(s.gall[r, :], s.wo[...]).astype(BF).astype(F32)
        s.do[r, :] = dout.astype(BF)
        split_heads(s.dom, r, dout)

    rb, lb, fb = lax.rem(col + 1, 4), lax.rem(col + 3, 4), lax.rem(col + 2, 4)
    blocks = {"own": col, "left": lb, "right": rb, "far": fb}
    outward = ("far", "right", "left", "own")

    def mark(flag, work, *args):
        def both():
            work(*args)
            done.add(flag)

        return both

    first = [0, 256, 768, 1536]

    def fold(values, how):
        return how(values.reshape(-1, 8, B), axis=0)

    def attend(i):
        q = pl.ds(i * B, B)
        for c in range(i + 1):
            kid = lax.broadcasted_iota(jnp.int32, (B, B), 0)
            qid = lax.broadcasted_iota(jnp.int32, (B, B), 1)
            allowed = s.segc[pl.ds(c * B, B), 0:1] == rowv["seg"][:, i * B : (i + 1) * B]
            allowed = allowed & (kid <= qid) if c == i else allowed
            s.cap[pl.ds(c * B, B), :] = jnp.where(allowed, 3e38, -1e30)

        for h in range(2):
            top = jnp.full((8, B), -1e30, F32)
            for c in range(i + 1):
                k, at_c = pl.ds(c * B, B), pl.ds(first[i] + c * B, B)
                scores = jnp.minimum(nt(s.km[h, k, :], s.qs[q, :]), s.cap[k, :])
                s.probs[h, at_c, :] = scores
                top = jnp.maximum(top, fold(scores, jnp.max))
            top = jnp.max(top, axis=0, keepdims=True)
            total = jnp.zeros((8, B), F32)
            for c in range(i + 1):
                at_c = pl.ds(first[i] + c * B, B)
                expo = jnp.exp(s.probs[h, at_c, :] - top)
                s.probs[h, at_c, :] = expo
                total = total + fold(expo, jnp.sum)
            inverse = 1.0 / jnp.sum(total, axis=0, keepdims=True)
            hrows = pl.ds(h * HD, HD)
            mix = jnp.zeros((HD, B), F32)
            for c in range(i + 1):
                at_c = pl.ds(first[i] + c * B, B)
                probs = s.probs[h, at_c, :] * inverse
                s.probs[h, at_c, :] = probs
                mix = mix + nn(s.vt[hrows, pl.ds(c * B, B)], probs.astype(BF))
            s.mt[hrows, q] = mix.astype(BF)

        s.mixed[q, :] = s.mt[:, q].astype(F32).T.astype(BF)

    def attend_back(i):
        q = pl.ds(i * B, B)

        for h in range(2):
            inner = jnp.zeros((8, B), F32)
            for c in range(i + 1):
                k, at_c = pl.ds(c * B, B), pl.ds(first[i] + c * B, B)
                probs = s.probs[h, at_c, :]
                dprob = nt(s.vm[h, k, :], s.do[q, :])
                s.cap[k, :] = dprob
                inner = inner + fold(probs * dprob, jnp.sum)
                s.dv[k, :] += nn(probs.astype(BF), s.dom[h, q, :])
            inner = jnp.sum(inner, axis=0, keepdims=True)
            hrows = pl.ds(h * HD, HD)
            dquery = jnp.zeros((HD, B), F32)
            for c in range(i + 1):
                k, at_c = pl.ds(c * B, B), pl.ds(first[i] + c * B, B)
                dscore = (s.probs[h, at_c, :] * (s.cap[k, :] - inner)).astype(BF)
                s.dk[k, :] += nn(dscore, s.qsm[h, q, :])
                dquery = dquery + nn(s.kt[hrows, k], dscore)
            s.dqt[hrows, q] = dquery * (1.0 / math.sqrt(HD))

    def branch(b):
        r = rows(b)
        s.op[r, :] = (nn(s.mixed[r, :], s.wo[...]) + nn(s.hid[r, :], s.wd[...])).astype(BF)

    def down_grad():
        @pl.loop(0, 4)
        def _(b):
            r = rows(b, 128)
            s.g1[r, :] = tn(s.hid[:, r], s.gall[...]).astype(BF)

        s.g1[F:, :] = nn(s.mt[...], s.gall[...]).astype(BF)

    def up_grad():
        @pl.loop(0, 4)
        def _(b):
            r = rows(b, 128)
            s.g2[r, :] = tn(s.hpg[:, r], s.mim[...]).astype(BF)

    def qkv_grad(b):
        r = rows(b)
        cos, sin = s.ctab[r, :], -s.stab[r, :]
        dq = turn(s.dqt[:, r].T, cos, sin).astype(BF)
        dk = turn(s.dk[r, :], cos, sin).astype(BF)
        dv = s.dv[r, :].astype(BF)
        both = jnp.concatenate([dq, dk, dv], axis=1)
        s.qkvg[r, :] = both
        ecols3 = pl.ds(pl.multiple_of(row * 3 * E, 3 * E), 3 * E)
        s.vec[5:6, ecols3] += jnp.sum(both.astype(F32), axis=0, keepdims=True)

    def qkv_weight_grad():
        @pl.loop(0, 3)
        def _(b):
            r = rows(b, E)
            s.g3[r, :] = tn(s.qkvg[:, r], s.ain[...]).astype(BF)

    def input_grad(b):
        r = rows(b)
        gain0, gain1 = wide(0), wide(1)
        attn = nt(s.qkvg[r, :], s.wq[...])
        mlp = nt(s.hpg[r, :], s.wu[...])
        normed = (s.xall[r, :].astype(F32) - s.mean[r, :]) * s.inv[r, :]
        s.ng[r, :] = (attn * gain0 + mlp * gain1).astype(BF)
        s.vec[0:1, :] += jnp.sum(attn * normed, axis=0, keepdims=True)
        s.vec[1:2, :] += jnp.sum(mlp * normed, axis=0, keepdims=True)
        s.vec[2:3, :] += jnp.sum(attn, axis=0, keepdims=True)
        s.vec[3:4, :] += jnp.sum(mlp, axis=0, keepdims=True)

    so, sn = under(s, "o_"), under(s, "n_")
    where = dict(core=core, x=x, row=row)
    sums = []
    ny = YROWS["n"]
    own = rows(col)

    def look(h, total):
        mean, inv = s.mean[own, :], s.inv[own, :]
        xv = s.xall[pl.ds(pl.multiple_of(col * B, B), ny), pl.ds(h * half, half)].astype(F32)
        normed = (xv - mean[:ny]) * inv[:ny]
        sums.append(jnp.sum(total, axis=1, keepdims=True))
        sums.append(jnp.sum(total * normed, axis=1, keepdims=True))

    def write_out():
        xv = s.xall[own, gcols].astype(F32) + (flat(bout[...]) + flat(bdown[...]))
        total = jnp.concatenate([total_y(so, row), total_z(s.op, so, col, row, YROWS["o"])])
        out[...] = (xv + total).astype(BF)

    def write_grad():
        yield ("n.y.sum", "n.y.end", "n.z.sum"), 0.4
        mean, inv = s.mean[own, :], s.inv[own, :]
        normed = (s.xall[own, gcols].astype(F32) - mean) * inv
        zsum = total_z(s.ng, sn, col, row, ny)
        first_sum = jnp.concatenate([sums[0] + sums[2], jnp.sum(zsum, axis=1, keepdims=True)])
        second = jnp.sum(zsum * normed[ny:], axis=1, keepdims=True)
        second_sum = jnp.concatenate([sums[1] + sums[3], second])
        lane = lax.broadcasted_iota(jnp.int32, (B, 128), 1)
        s.ssend[...] = jnp.where(lane < 4, first_sum, second_sum).T[:8, :]
        ys = net.go(s.ssend, s.srecv, y1)
        yield (ys,), 0.5
        ys.wait_recv()
        both = (s.ssend[...] + s.srecv[...]) * (1.0 / D)
        both = jnp.concatenate([both] * 16).T
        total = jnp.concatenate([total_y(sn, row), zsum])
        tgrad[...] = (
            s.gall[own, gcols].astype(F32) + inv * (total - both[:, 0:1] - normed * both[:, 4:5])
        ).astype(BF)

    def write_vectors():
        vout[0] = s.vs[2]
        vout[1] = s.vs[3]

    scatter(net, add, done, "o.", tuple("send." + b for b in outward), s.op, so, at, col, row, YROWS["o"])
    scatter(net, add, done, "n.", tuple("ng." + b for b in outward), s.ng, sn, at, col, row, ny, look)
    gate = ("g.r3", "g.r4", "g.l3", "g.l4")
    for b in outward:
        add(later(("op." + b,) + gate, 0.0, mark("send." + b, lambda: None)))
    reduce_weights(net, add, done, "a.", "g1", s.g1, under(s, "r0_", fin=s.f0), at, where, ROWS[0])
    reduce_weights(net, add, done, "b.", "g2", s.g2, under(s, "r1_", fin=s.f1), at, where, ROWS[1])
    reduce_weights(net, add, done, "c.", "g3", s.g3, under(s, "r2_", fin=s.f2), at, where, ROWS[2])
    writes = []

    def write_reduced(src, dst):
        writes.append(net.local(src, dst))

    for name, src, dst in (("a.", s.f0, f0_h), ("b.", s.f1, f1_h), ("c.", s.f2, f2_h)):
        add(later((name + "end",), 0.02, partial(write_reduced, src, dst)))
    add(reduce_vectors(net, done, s, at))
    add(later(("vsum",), 0.05, write_vectors))
    add(write_grad())
    for name, b in blocks.items():
        add(later(("nb", "x." + name), 0.5, mark("norm." + name, norm, b)))
        add(later(("wq", "norm." + name), 0.45, mark("proj." + name, project, b)))
    needs = tuple("proj." + name for name in blocks)
    for i in range(4):
        add(later(needs, 0.37 * (i + 1), mark(f"attf{i}", attend, i)))
        needs = (f"attf{i}",)
    for name, b in blocks.items():
        add(later(("wu", "norm." + name), 0.36, mark("exp." + name, expand, b)))
    for name in outward:
        needs = ("wo", "wd", "attf3", "exp." + name)
        add(later(needs, 0.55, mark("op." + name, branch, blocks[name])))
    for name, b in blocks.items():
        needs = ("wo", "wd", "g." + name, "exp." + name)
        add(later(needs, 0.43, mark("con." + name, contract, b)))
    allg = tuple("g." + name for name in blocks) + tuple("exp." + name for name in blocks)
    add(later(allg + ("attf3",), 2.5, mark("g1", down_grad)))
    allc = tuple("con." + name for name in blocks)
    add(later(allc, 2.2, mark("g2", up_grad)))
    needs = allc + ("attf3",)
    for i in range(4):
        add(later(needs, 0.43 * (i + 1), mark(f"attb{i}", attend_back, i)))
        needs = (f"attb{i}",)
    for name in outward:
        add(later(("attb3",), 0.26, mark("qg." + name, qkv_grad, blocks[name])))
    add(later(tuple("qg." + name for name in blocks), 1.4, mark("g3", qkv_weight_grad)))
    for name in outward:
        add(later(("qg." + name,), 0.68, mark("ng." + name, input_grad, blocks[name])))
    add(later(tuple("ng." + name for name in blocks), 0.0, mark("vec", lambda: None)))
    add(later(("o.y.end", "o.z.sum"), 0.3, mark("out", write_out)))
    run(tasks, done)
    for copy in writes:
        copy.wait()
    for copy in net.sent:
        copy.wait_send()


def tables():
    freq = np.arange(ROT // 2, dtype=np.float32)
    inverse = np.float32(10000.0) ** (np.float32(-2.0) * freq / np.float32(ROT))
    angle = np.arange(T, dtype=np.float32)[:, None] * inverse[None, :].astype(np.float32)
    cos, sin = np.cos(angle), np.sin(angle)
    ones, zeros = np.ones((T, HD - ROT), np.float32), np.zeros((T, HD - ROT), np.float32)
    ctab = np.concatenate([cos, cos, ones] * 2, axis=1)
    stab = np.concatenate([-sin, sin, zeros] * 2, axis=1)
    return ctab.astype(np.float32), stab.astype(np.float32)


def last(
    f0_h, f1_h, f2_h, vec_h, out_h, tgrad_h,
    out_o, tgrad_o, wq_o, bq_o, wo_o, bo_o, wu_o, bu_o, wd_o, bd_o, gain_o, bias_o,
    f0, f1, f2, vec, out, tgrad, wq, wo, wu, wd, sems,
):
    row = lax.axis_index("row")
    copies = []

    def write(src, dst):
        copy = pltpu.make_async_copy(src, dst, sems.at[len(copies)])
        copy.start()
        copies.append(copy)
        return copy

    pairs = ((f0_h, f0), (f1_h, f1), (f2_h, f2), (vec_h, vec), (out_h, out), (tgrad_h, tgrad))
    reads = [write(a, b) for a, b in pairs]
    reads[0].wait()
    for r in range(2):
        for k in range(8):
            piece = f0[k // 4, k % 4, r].astype(F32)
            n = piece.shape[0]
            inside = max(0, min(n, F - k * n))
            if inside:
                wd[pl.ds(r * F + k * n, inside), :] = piece[:inside]
            if inside < n:
                wo[pl.ds(r * E + k * n + inside - F, n - inside), :] = piece[inside:]
        write(wd.at[pl.ds(r * F, F)], wd_o.at[pl.ds(r * F, F)])
    write(wo, wo_o)
    reads[1].wait()
    for r in range(2):
        for k in range(4):
            pair = [f1[(2 * k + h) // 4, (2 * k + h) % 4, r].astype(F32) for h in range(2)]
            wu[:, pl.ds(r * F + k * E, E)] = jnp.concatenate(pair).T
        write(wu.at[:, pl.ds(r * F, F)], wu_o.at[:, pl.ds(r * F, F)])
    reads[2].wait()
    for r in range(2):
        whole = jnp.concatenate([f2[k // 4, k % 4, r].astype(F32) for k in range(8)])
        for k in range(3):
            wq[k, :, pl.ds(r * E, E)] = whole[k * E : (k + 1) * E].T
    write(wq, wq_o)
    for copy in reads[3:]:
        copy.wait()
    write(out, out_o)
    write(tgrad, tgrad_o)
    half = D // 2
    left = row == 0

    def cut(values):
        return jnp.where(left, values[:, :half], values[:, half:])

    bo_o[...] = cut(vec[0, 4:5, :])
    bd_o[...] = cut(vec[0, 4:5, :])
    for k in range(3):
        bq_o[k : k + 1, :E] = vec[0, 5:6, k * E : (k + 1) * E]
        bq_o[k : k + 1, E:] = vec[0, 5:6, (k + 3) * E : (k + 4) * E]
    bu_o[...] = vec[0, 6:7, :]
    gain_o[...] = cut(vec[1, 0:2, :])
    bias_o[...] = cut(vec[1, 2:4, :])
    for copy in copies[len(reads) :]:
        copy.wait()


def on_device(
    tokens, segment_ids, w_qkv, b_qkv, w_out, b_out, w_up, b_up, w_down, b_down, norm_gain, norm_bias, cotangent
):
    ctab, stab = tables()
    vmem = pl.BlockSpec(memory_space=pltpu.VMEM)
    hbm = pl.BlockSpec(memory_space=pl.ANY)
    shape = jax.ShapeDtypeStruct
    early = [
        shape((2, 4, 2, ROWS[0] // 8, D // 2), BF),
        shape((2, 4, 2, ROWS[1] // 8, D // 2), BF),
        shape((2, 4, 2, ROWS[2] // 8, D // 2), BF),
        shape((2, 8, D), F32),
    ]
    out, tgrad, f0, f1, f2, vec = pl.pallas_call(
        body,
        out_shape=[
            shape((B, D // 2), BF),
            shape((B, D // 2), BF),
            *early,
        ],
        in_specs=[hbm] * 6 + [vmem] * 7 + [hbm] * 2,
        out_specs=[vmem, vmem, hbm, hbm, hbm, vmem],
        scratch_shapes=[pltpu.VMEM(*spec) for spec in SCRATCH.values()]
        + [pltpu.SemaphoreType.DMA((NSEM,)), pltpu.SemaphoreType.DMA((NSEM,))],
        compiler_params=pltpu.CompilerParams(
            collective_id=0, has_side_effects=True, vmem_limit_bytes=60 * 1024 * 1024
        ),
        name="block",
    )(
        tokens, cotangent, w_qkv, w_out, w_up, w_down, b_qkv, b_up.reshape(8, 128),
        b_out.reshape(4, 128), b_down.reshape(4, 128), norm_gain, norm_bias,
        segment_ids.reshape(8, 128), jnp.asarray(ctab), jnp.asarray(stab),
    )
    big = [
        ((3, D // 2, 2 * E), F32),
        ((2 * E, D // 2), F32),
        ((D // 2, 2 * F), F32),
        ((2 * F, D // 2), F32),
    ]
    results = pl.pallas_call(
        last,
        out_shape=[
            shape((B, D // 2), BF),
            shape((B, D // 2), BF),
            shape(*big[0]),
            shape((3, 2 * E), F32),
            shape(*big[1]),
            shape((1, D // 2), F32),
            shape(*big[2]),
            shape((1, 2 * F), F32),
            shape(*big[3]),
            shape((1, D // 2), F32),
            shape((2, D // 2), F32),
            shape((2, D // 2), F32),
        ],
        in_specs=[hbm] * 6,
        out_specs=[hbm, hbm, hbm, vmem, hbm, vmem, hbm, vmem, hbm, vmem, vmem, vmem],
        scratch_shapes=[pltpu.VMEM(e.shape, e.dtype) for e in early]
        + [pltpu.VMEM((B, D // 2), BF)] * 2
        + [pltpu.VMEM(*spec) for spec in big]
        + [pltpu.SemaphoreType.DMA((16,))],
        compiler_params=pltpu.CompilerParams(vmem_limit_bytes=60 * 1024 * 1024),
        name="last",
    )(f0, f1, f2, vec, out, tgrad)
    out, tgrad, wq, bq, wo, bo, wu, bu, wd, bd, gain, bias = results
    bo, bu, bd = bo.reshape(-1), bu.reshape(-1), bd.reshape(-1)
    return (out, tgrad, wq, bq, wo, bo, wu, bu, wd, bd, gain, bias)


def solution(mesh):
    in_specs = (
        P(("dp", "col"), "row"),
        P("dp"),
        P(None, "row", "col"),
        P(None, "col"),
        P("col", "row"),
        P("row"),
        P("row", "col"),
        P("col"),
        P("col", "row"),
        P("row"),
        P(None, "row"),
        P(None, "row"),
        P(("dp", "col"), "row"),
    )
    out_specs = (
        P(("dp", "col"), "row"),
        P(("dp", "col"), "row"),
        P(None, "row", "col"),
        P(None, "col"),
        P("col", "row"),
        P("row"),
        P("row", "col"),
        P("col"),
        P("col", "row"),
        P("row"),
        P(None, "row"),
        P(None, "row"),
    )
    return jax.shard_map(
        on_device, mesh=mesh, in_specs=in_specs, out_specs=out_specs, check_vma=False
    )
```

```python
from functools import partial
from types import SimpleNamespace
import math

import numpy as np
import jax
import jax.numpy as jnp
from jax import lax
from jax.experimental import pallas as pl
from jax.experimental.pallas import tpu as pltpu
from jax.sharding import PartitionSpec as P

MESH = pl.DeviceIdType.MESH
BF = jnp.bfloat16
F32 = jnp.float32
T = 1024
D = 1024
HD = 64
ROT = 16
E = 128
F = 512
B = 256
EPSILON = 1e-05
NSEM = 200
YROWS = dict(x=112, g=128, o=160, n=208)


ORDER = (
    1, 4, 3, 5, 0, 8, 2, 9, 44, 44, 2, 6, 10, 4, 12, 3, 7, 11, 40, 5, 13, 9, 8, 16, 131, 40, 132, 6,
    14, 21, 23, 24, 25, 29, 10, 12, 18, 135, 136, 41, 7, 15, 20, 22, 28, 42, 13, 11, 17, 133, 14,
    41, 134, 145, 42, 144, 143, 23, 31, 24, 32, 27, 15, 19, 137, 146, 138, 139, 43, 140, 25, 33,
    141, 22, 29, 30, 26, 142, 43, 27, 35, 148, 147, 28, 36, 151, 149, 150, 33, 26, 80, 34, 50, 46,
    82, 48, 81, 47, 79, 45, 49, 53, 31, 52, 51, 30, 37, 152, 32, 38, 153, 155, 34, 35, 39, 154, 156,
    83, 157, 53, 97, 46, 52, 56, 54, 158, 48, 159, 83, 85, 84, 88, 86, 87, 160, 47, 57, 97, 100, 99,
    98, 101, 102, 161, 45, 88, 55, 59, 58, 54, 61, 162, 167, 66, 62, 163, 87, 89, 164, 165, 166, 59,
    58, 60, 111, 168, 63, 67, 69, 101, 102, 103, 169, 64, 68, 70, 170, 89, 90, 61, 171, 128, 65,
    111, 112, 113, 114, 115, 62, 72, 116, 69, 63, 73, 70, 75, 71, 103, 104, 128, 60, 172, 64, 74,
    76, 115, 116, 117, 90, 91, 92, 65, 128, 75, 76, 77, 117, 118, 91, 93, 92, 94, 95, 104, 106, 105,
    94, 93, 71, 78, 128, 77, 95, 96, 118, 119, 120, 105, 107, 106, 109, 108, 96, 125, 107, 108, 128,
    129, 119, 121, 120, 122, 123, 121, 122, 78, 130, 109, 110, 123, 124, 130, 110, 126, 124, 127,
)


def nn(a, b):
    return jnp.dot(a, b, preferred_element_type=F32)


def nt(a, b):
    return lax.dot_general(a, b, (((1,), (1,)), ((), ())), preferred_element_type=F32)


def tn(a, b):
    return lax.dot_general(a, b, (((0,), (0,)), ((), ())), preferred_element_type=F32)


def rows(block, size=B):
    return pl.ds(pl.multiple_of(block * size, size), size)


class Net:
    def __init__(self, send, recv):
        self.send, self.recv, self.count, self.sent = send, recv, 0, []

    def go(self, src, dst, device):
        k = self.count
        self.count += 1
        assert k < NSEM
        copy = pltpu.make_async_remote_copy(
            src_ref=src,
            dst_ref=dst,
            send_sem=self.send.at[k],
            recv_sem=self.recv.at[k],
            device_id=device,
            device_id_type=MESH,
        )
        copy.start()
        self.sent.append(copy)
        return copy

    def local(self, src, dst):
        k = self.count
        self.count += 1
        assert k < NSEM
        copy = pltpu.make_async_copy(src, dst, self.send.at[k])
        copy.start()
        return copy


def later(deps, cost, work):
    yield deps, cost
    work()


def gather_tokens(net, add, done, name, begin, own, full, at, half, col, row, yr):
    right, left, peer = at["z1"], at["z3"], at["y1"]
    zr = B - yr
    part = zr // 32 * 16
    cut = yr + part
    c = {}

    def place(b, h, start=0, size=B):
        r = pl.ds(pl.multiple_of(b * B + start, 16), size)
        return full.at[r, pl.ds(pl.multiple_of(h * half, half), half)]

    def move(key, device, *where):
        c[key] = net.go(place(*where), place(*where), device)
        done.add(name + key)

    def send(key, device, start, size):
        c[key] = net.go(own.at[pl.ds(start, size)], place(col, row, start, size), device)
        done.add(name + key)

    lcol, rcol, fcol = lax.rem(col + 3, 4), lax.rem(col + 1, 4), lax.rem(col + 2, 4)

    def begin_y():
        yield begin[0], 0.1
        c["keep"] = net.local(own, place(col, row))
        send("p0", peer, 0, yr)
        send("p1", peer, yr, zr)
        c["keep"].wait()
        done.add(name + "keep")

    def begin_z():
        yield begin[1], 0.1
        send("r1", right, yr, zr)
        send("l1", left, yr, zr)
        send("r0", right, 0, yr)
        send("l0", left, 0, yr)

    def hop(keys, *work):
        yield tuple(name + k for k in keys), 0.0
        yield tuple(c[k] for k in keys), 0.05
        for k in keys:
            c[k].wait_recv()
        for w in work:
            move(*w)
        done.update(name + k + "!" for k in keys)

    def whole(flag, keys):
        yield tuple(name + k + ("" if k == "keep" else "!") for k in keys), 0.0
        done.add(name + flag)

    add(begin_y())
    add(begin_z())
    add(hop(["p0"], ("r2", right, col, 1 - row, 0, yr), ("l2", left, col, 1 - row, 0, yr)))
    add(hop(["r1"], ("r3", right, lcol, row, yr, part), ("p2", peer, lcol, row, yr, zr)))
    add(hop(["l1"], ("l3", left, rcol, row, cut, B - cut), ("p3", peer, rcol, row, yr, zr)))
    add(hop(["r0"], ("r4", right, lcol, row, 0, yr)))
    add(hop(["l2"], ("l4", left, rcol, 1 - row, 0, yr)))
    add(hop(["r3", "l3"], ("p4", peer, fcol, row, yr, zr)))
    add(hop(["p1"]))
    add(hop(["l0"]))
    add(hop(["r2"]))
    add(hop(["p2"]))
    add(hop(["p3"]))
    add(hop(["r4"]))
    add(hop(["l4"]))
    add(hop(["p4"]))
    add(whole("own", ["p0", "p1", "keep"]))
    add(whole("left", ["r0", "r1", "r2", "p2"]))
    add(whole("right", ["l0", "l1", "l2", "p3"]))
    add(whole("far", ["r3", "r4", "l3", "l4", "p4"]))


def gather_weights(net, add, done, wqkv, wup, wout, wdown, s, at, core, row):
    half, part = D // 2, D // 4
    mine, theirs = row, 1 - row
    drows, ocols = rows(row, half), rows(1 - row, half)

    def cut(which, size):
        return pl.ds(pl.multiple_of(which * size, size), size)

    local = {}
    for k in range(3):
        kcols = pl.ds(k * E, E)
        local[k] = net.local(wqkv.at[k, :, cut(mine, E)], s.wq.at[drows, kcols])
    local["u"] = net.local(wup.at[:, cut(mine, F)], s.wu.at[drows])
    local["o"] = net.local(wout.at[cut(mine, E)], s.wo.at[:, drows])
    local["d"] = net.local(wdown.at[cut(mine, F)], s.wd.at[:, drows])
    src, dst, got = cut(core, part), cut(row * 2 + core, part), cut((1 - row) * 2 + core, part)
    far, near = at["y3"], at["core"]
    q = [
        net.go(wqkv.at[k, src, cut(theirs, E)], s.wq.at[dst, pl.ds(k * E, E)], far)
        for k in range(3)
    ]
    u = net.go(wup.at[src, cut(theirs, F)], s.wu.at[dst], far)
    o = net.go(wout.at[cut(theirs * 2 + core, E // 2)], s.wo.at[cut(core, E // 2), drows], far)
    d = net.go(wdown.at[cut(theirs * 2 + core, F // 2)], s.wd.at[cut(core, F // 2), drows], far)

    def share(flag, copies, view, locals_):
        yield tuple(copies), 0.05
        for copy in copies:
            copy.wait_recv()
        second = net.go(view, view, near)
        yield (second,), 0.0
        second.wait_recv()
        for k in locals_:
            local[k].wait()
        done.add(flag)

    add(share("wq", q, s.wq.at[got], range(3)))
    add(share("wu", [u], s.wu.at[got], "u"))
    add(share("wo", [o], s.wo.at[cut(core, E // 2), ocols], "o"))
    add(share("wd", [d], s.wd.at[cut(core, F // 2), ocols], "d"))


def ring_scatter(net, add, done, name, part, bufs, me, right, left, width, ready):
    ta, tb, inl, inr = bufs
    lo, hi = pl.ds(0, width), pl.ds(width, width)
    far, rb, lb = lax.rem(me + 2, 4), lax.rem(me + 1, 4), lax.rem(me + 3, 4)
    c = {}

    def send(deps, *sends):
        yield deps, 0.05
        for key, src, dst, device in sends:
            c[key] = net.go(src, dst, device)
            done.add(name + key)

    def through(came, flag, buf, view, key, dst, device):
        yield (name + came, flag), 0.0
        yield (c[came],), 0.15
        c[came].wait_recv()
        view[...] = (view[...].astype(F32) + buf[...].astype(F32)).astype(BF)
        c[key] = net.go(view, dst, device)
        done.add(name + key)

    def finish():
        yield tuple(name + k for k in "cdef") + (ready[3],), 0.0
        yield tuple(c[k] for k in "cdef"), 0.0
        for k in "cdef":
            c[k].wait_recv()
        done.add(name + "sum")

    add(send((ready[0],), ("a", part(far, lo), ta, right), ("b", part(far, hi), tb, left)))
    add(send((ready[1],), ("c", part(rb, hi), inl.at[:, hi], right)))
    add(send((ready[2],), ("d", part(lb, lo), inr.at[:, lo], left)))
    add(through("a", ready[1], ta, part(rb, lo), "e", inl.at[:, lo], right))
    add(through("b", ready[2], tb, part(lb, hi), "f", inr.at[:, hi], left))
    add(finish())


def reduce_weights(net, add, done, name, begin, grad, s, at, me, n):
    core, x, row = me["core"], me["x"], me["row"]
    half, size = n // 2, n // 8
    base, away = core * half, (1 - core) * half
    x1, x3, near = at["x1"], at["x3"], at["core"]
    lx, rx, fx = lax.rem(x + 3, 4), lax.rem(x + 1, 4), lax.rem(x + 2, 4)
    c = {}

    def start():
        yield (begin,), 0.05
        copy = net.go(grad.at[pl.ds(pl.multiple_of(away, half), half)], s.rc, near)
        yield (copy,), 0.4 * n / 640
        copy.wait_recv()
        own = grad.at[pl.ds(pl.multiple_of(base, half), half)]
        own[...] = (own[...].astype(F32) + s.rc[...].astype(F32)).astype(BF)
        done.add(name + "core")

    def part(block, cols):
        return grad.at[pl.ds(pl.multiple_of(base + block * size, size), size), cols]

    def across():
        yield (name + "sum",), 0.2
        for h in range(2):
            cols = pl.ds(h * (D // 2), D // 2)
            total = part(x, cols)[...].astype(F32) + s.inl[:, cols].astype(F32)
            s.sy[h] = (total + s.inr[:, cols].astype(F32)).astype(BF)
        g0 = net.go(s.sy.at[row], s.ry.at[0], at["y2"])
        g1 = net.go(s.sy.at[1 - row], s.ry.at[1], at["y1"])
        g2 = net.go(s.sy.at[1 - row], s.ry.at[2], at["y3"])
        yield (g0, g1, g2), 0.15
        for copy in (g0, g1, g2):
            copy.wait_recv()
        s.fin[core, x, row] = (s.sy[row].astype(F32) + s.ry[0].astype(F32)).astype(BF)
        s.fin[core, x, 1 - row] = (s.ry[1].astype(F32) + s.ry[2].astype(F32)).astype(BF)
        for key, h, device in (("a", 0, x1), ("b", 1, x3), ("c", 1, x1), ("d", 0, x3)):
            view = s.fin.at[core, x, h]
            c[key] = net.go(view, view, device)
        view = s.fin.at[core, x]
        c["k"] = net.go(view, view, near)
        done.add(name + "sent")

    def hop(keys, flag, view, device, key, need=()):
        yield (name + flag,) + tuple(name + k + "!" for k in need), 0.0
        yield tuple(c[k] for k in keys), 0.05
        for k in keys:
            c[k].wait_recv()
        c[key] = net.go(view, view, device)
        done.update(name + k + "!" for k in keys)
        done.add(name + key)

    def end():
        yield tuple(name + k for k in ("l", "m", "n")), 0.0
        yield tuple(c[k] for k in "klmn"), 0.0
        for k in "klmn":
            c[k].wait_recv()
        done.add(name + "end")

    ready = (name + "core",) * 4
    add(start())
    ring_scatter(
        net, add, done, name, part, (s.ta, s.tb, s.inl, s.inr), x, x1, x3, D // 2, ready
    )
    add(across())
    add(hop("a", "sent", s.fin.at[core, lx, 0], x1, "p"))
    add(hop("b", "sent", s.fin.at[core, rx, 1], x3, "q"))
    add(hop("c", "sent", s.fin.at[core, lx], near, "l", "a"))
    add(hop("d", "sent", s.fin.at[core, rx], near, "m", "b"))
    add(hop("pq", "p", s.fin.at[core, fx], near, "n", "b"))
    add(end())


def reduce_vectors(net, done, s, at):
    yield ("vec",), 0.0
    c = net.go(s.vec, s.vr.at[0], at["core"])
    yield (c,), 0.05
    c.wait_recv()
    s.vs[0] = s.vec[...] + s.vr[0]
    for n, axis in enumerate("xyz"):
        copies = [net.go(s.vs.at[n], s.vr.at[3 * n + k], at[axis + str(k)]) for k in (1, 2, 3)]
        yield tuple(copies), 0.05
        for copy in copies:
            copy.wait_recv()
        s.vs[n + 1] = (s.vs[n] + s.vr[3 * n + 1]) + (s.vr[3 * n + 2] + s.vr[3 * n + 3])
    done.add("vsum")


def scatter(net, add, done, name, ready, p, s, at, col, row, yr, look=None):
    half, zr = D // 2, B - yr
    far, rb, lb = lax.rem(col + 2, 4), lax.rem(col + 1, 4), lax.rem(col + 3, 4)
    mcols, ocols = rows(row, half), rows(1 - row, half)
    right, left, peer = at["z1"], at["z3"], at["y1"]

    def yrows(b):
        return pl.ds(pl.multiple_of(b * B, B), yr)

    def zrows(b):
        return pl.ds(pl.multiple_of(b * B + yr, 16), zr)

    def zpart(b, cols):
        return p.at[zrows(b), pl.ds(pl.multiple_of(row * half + cols.start, 256), cols.size)]

    def pair(k, b):
        yield (ready[k],), 0.05
        copy = net.go(p.at[zrows(b), ocols], s.ry.at[k], peer)
        yield (copy,), 0.15
        copy.wait_recv()
        view = p.at[zrows(b), mcols]
        view[...] = (view[...].astype(F32) + s.ry[k].astype(F32)).astype(BF)
        done.add(name + "z" + str(k))

    def last():
        yield (name + "y.sum",), 0.3
        for h in range(2):
            cols = pl.ds(h * half, half)
            total = p[yrows(col), cols].astype(F32) + s.inl[:, cols].astype(F32)
            total += s.inr[:, cols].astype(F32)
            s.ysend[h] = total.astype(BF)
            if look is not None:
                look(h, total)
        copy = net.go(s.ysend.at[1 - row], s.yrecv, peer)
        yield (copy,), 0.0
        copy.wait_recv()
        done.add(name + "y.end")

    for k, b in enumerate((far, rb, lb, col)):
        add(pair(k, b))
    ring_scatter(
        net, add, done, name + "y.", lambda b, cols: p.at[yrows(b), cols],
        (s.ta, s.tb, s.inl, s.inr), col, right, left, half, ready,
    )
    ring_scatter(
        net, add, done, name + "z.", zpart,
        (s.ta2, s.tb2, s.inl2, s.inr2), col, right, left, half // 2,
        tuple(name + "z" + str(k) for k in range(4)),
    )
    add(last())


def total_y(s, row):
    return s.ysend[row].astype(F32) + s.yrecv[...].astype(F32)


def total_z(p, s, col, row, yr):
    own = p[pl.ds(pl.multiple_of(col * B + yr, 16), B - yr), rows(row, D // 2)]
    return own.astype(F32) + s.inl2[...].astype(F32) + s.inr2[...].astype(F32)


def run(tasks, done):
    asked = [next(task)[0] for task in tasks]
    for k in ORDER:
        for need in asked[k]:
            assert not isinstance(need, str) or need in done, "order"
        asked[k] = next(tasks[k], ((),))[0]
    assert all(next(task, None) is None for task in tasks), "unfinished"


def turn(values, cos, sin):
    lane = lax.broadcasted_iota(jnp.int32, values.shape, 1)
    other = jnp.where(lane % HD < ROT // 2, pltpu.roll(values, E - ROT // 2, 1), pltpu.roll(values, ROT // 2, 1))
    return values * cos + other * sin


def split_heads(ref, at_rows, values):
    lane = lax.broadcasted_iota(jnp.int32, values.shape, 1)
    zero = jnp.zeros_like(values)
    ref[0, at_rows, :] = jnp.where(lane < HD, values, zero).astype(BF)
    ref[1, at_rows, :] = jnp.where(lane < HD, zero, values).astype(BF)


SCRATCH = dict(
    xall=((T, D), BF),
    gall=((T, D), BF),
    ain=((T, D), BF),
    mim=((T, D), BF),
    wq=((D, 3 * E), BF),
    wo=((E, D), BF),
    wu=((D, F), BF),
    wd=((F, D), BF),
    nb=((2, 8, D // 2), F32),
    mean=((T, 1), F32),
    inv=((T, 1), F32),
    hid=((T, F), BF),
    slope=((T, F), F32),
    segc=((T, 8), F32),
    nbs=((8, D // 2), F32),
    hpg=((T, F), BF),
    qs=((T, E), BF),
    qsm=((2, T, E), BF),
    km=((2, T, E), BF),
    vm=((2, T, E), BF),
    kt=((E, T), BF),
    vt=((E, T), BF),
    do=((T, E), BF),
    dom=((2, T, E), BF),
    probs=((2, 2560, B), F32),
    mt=((E, T), BF),
    mixed=((T, E), BF),
    dqt=((E, T), F32),
    cap=((T, B), F32),
    acc=((F, D), F32),
    dk=((T, E), F32),
    dv=((T, E), F32),
    qkvg=((T, 3 * E), BF),
    op=((T, D), BF),
    ng=((T, D), BF),
    ctab=((T, E), F32),
    stab=((T, E), F32),
    ssend=((8, B), F32),
    srecv=((8, B), F32),
    g1=((F + E, D), BF),
    g2=((F, D), BF),
    g3=((3 * E, D), BF),
    f0=((2, 4, 2, (F + E) // 8, D // 2), BF),
    f1=((2, 4, 2, F // 8, D // 2), BF),
    f2=((2, 4, 2, 3 * E // 8, D // 2), BF),
    vec=((8, D), F32),
    vr=((10, 8, D), F32),
    vs=((4, 8, D), F32),
)
def scatter_scratch(yr):
    zr = B - yr
    return dict(
        ta=((yr, D // 2), BF),
        tb=((yr, D // 2), BF),
        inl=((yr, D), BF),
        inr=((yr, D), BF),
        ry=((4, zr, D // 2), BF),
        ta2=((zr, D // 4), BF),
        tb2=((zr, D // 4), BF),
        inl2=((zr, D // 2), BF),
        inr2=((zr, D // 2), BF),
        ysend=((2, yr, D // 2), BF),
        yrecv=((yr, D // 2), BF),
    )


def reduce_scratch(n):
    return dict(
        rc=((n // 2, D), BF),
        ta=((n // 8, D // 2), BF),
        tb=((n // 8, D // 2), BF),
        inl=((n // 8, D), BF),
        inr=((n // 8, D), BF),
        sy=((2, n // 8, D // 2), BF),
        ry=((3, n // 8, D // 2), BF),
    )


ROWS = (F + E, F, 3 * E)
for name in "on":
    SCRATCH.update({name + "_" + key: v for key, v in scatter_scratch(YROWS[name]).items()})
for k, n in enumerate(ROWS):
    SCRATCH.update({f"r{k}_{key}": spec for key, spec in reduce_scratch(n).items()})


def under(s, prefix, **more):
    picked = {k[len(prefix) :]: v for k, v in vars(s).items() if k.startswith(prefix)}
    return SimpleNamespace(**picked, **more)


def body(
    tok, cot, wqkv, wout, wup, wdown, bqkv, bup, bout, bdown, gain, bias, seg, ctab_h, stab_h,
    out, tgrad, f0_h, f1_h, f2_h, vout, *scratch,
):
    s = SimpleNamespace(**dict(zip(SCRATCH, scratch)))
    send, recv = scratch[len(SCRATCH) :]
    net = Net(send, recv)
    dp, row, col = lax.axis_index("dp"), lax.axis_index("row"), lax.axis_index("col")
    core, x, yh = lax.rem(dp, 2), lax.rem(dp // 2, 4), dp // 8
    half = D // 2

    def dev(core=core, x=x, yh=yh, row=row, col=col):
        return (yh * 8 + x * 2 + core, row, col)

    at = {"core": dev(core=1 - core)}
    for k in (1, 2, 3):
        at[f"x{k}"] = dev(x=lax.rem(x + k, 4))
        at[f"z{k}"] = dev(col=lax.rem(col + k, 4))
    at["y1"] = dev(row=1 - row)
    at["y2"] = dev(yh=1 - yh)
    at["y3"] = dev(yh=1 - yh, row=1 - row)
    y1 = at["y1"]

    s.nbs[...] = jnp.concatenate(
        [gain[...].astype(F32), bias[...].astype(F32), jnp.zeros((4, half), F32)]
    )
    barrier = pltpu.get_barrier_semaphore()
    for device in at.values():
        pl.semaphore_signal(barrier, inc=1, device_id=device, device_id_type=MESH)
    pl.semaphore_wait(barrier, len(at))

    tasks, done = [], set()
    add = tasks.append
    gather_tokens(net, add, done, "x.", ((), ()), tok, s.xall, at, half, col, row, YROWS["x"])
    gather_tokens(net, add, done, "g.", (("x.p4",), ("x.r3", "x.r4", "x.l3", "x.l4")), cot, s.gall, at, half, col, row, YROWS["g"])
    nbc = net.go(s.nbs, s.nb.at[row], y1)
    gather_weights(net, add, done, wqkv, wup, wout, wdown, s, at, core, row)
    tabs = [net.local(ctab_h, s.ctab), net.local(stab_h, s.stab)]
    def flat(values):
        values = values.astype(F32)
        return jnp.concatenate([values[k : k + 1, :] for k in range(values.shape[0])], axis=1)

    rowv = {}
    fcols = pl.ds(pl.multiple_of(row * F, F), F)
    gcols = pl.ds(pl.multiple_of(row * half, half), half)

    def wide(k):
        return jnp.concatenate([s.nb[0, k : k + 1, :], s.nb[1, k : k + 1, :]], axis=1)

    def params():
        yield ("x.r0", "x.p1"), 0.4
        s.nb[row] = s.nbs[...]
        s.vec[...] = jnp.zeros_like(s.vec)
        s.dk[...] = jnp.zeros_like(s.dk)
        s.dv[...] = jnp.zeros_like(s.dv)
        rowv["seg"] = flat(seg[...])
        s.segc[...] = jnp.broadcast_to(rowv["seg"], (8, T)).T
        bq_all, bu_all, mine = bqkv[...].astype(F32), flat(bup[...]), row == 0
        parts = [
            jnp.where(mine, bq_all[k : k + 1, :E], bq_all[k : k + 1, E:]) for k in range(3)
        ]
        rowv["bq"] = jnp.concatenate(parts, axis=1)
        rowv["bu"] = jnp.where(mine, bu_all[:, :F], bu_all[:, F:])
        yield (nbc,), 0.0
        nbc.wait_recv()
        for copy in tabs:
            copy.wait()
        done.add("nb")

    add(params())

    def norm(c):
        gain0, gain1, bias0, bias1 = wide(0), wide(1), wide(2), wide(3)

        @pl.loop(0, 2)
        def _(b):
            r = rows(c * 2 + b, 128)
            xv = s.xall[r, :].astype(F32)
            mean = jnp.sum(xv, axis=1, keepdims=True) * (1.0 / D)
            square = jnp.sum(xv * xv, axis=1, keepdims=True) * (1.0 / D)
            inv = lax.rsqrt(square - mean * mean + EPSILON)
            normed = (xv - mean) * inv
            s.mean[r, :] = mean
            s.inv[r, :] = inv
            s.ain[r, :] = (normed * gain0 + bias0).astype(BF)
            s.mim[r, :] = (normed * gain1 + bias1).astype(BF)

    def project(c):
        r = rows(c)
        pre = nn(s.ain[r, :], s.wq[...]) + rowv["bq"]
        cos, sin = s.ctab[r, :], s.stab[r, :]
        query = (turn(pre[:, :E], cos, sin)).astype(BF).astype(F32) * (1.0 / math.sqrt(HD))
        key = turn(pre[:, E : 2 * E], cos, sin).astype(BF).astype(F32)
        value = pre[:, 2 * E :].astype(BF).astype(F32)
        s.qs[r, :] = query.astype(BF)
        split_heads(s.qsm, r, query)
        split_heads(s.km, r, key)
        split_heads(s.vm, r, value)
        s.kt[:, r] = key.T.astype(BF)
        s.vt[:, r] = value.T.astype(BF)

    def expand(c):
        r = rows(c)
        pre = nn(s.mim[r, :], s.wu[...]) + rowv["bu"]
        cdf = 0.5 * (1.0 + lax.erf(pre * math.sqrt(0.5)))
        s.hid[r, :] = (pre * cdf).astype(BF)
        s.slope[r, :] = cdf + pre * jnp.exp(-0.5 * pre * pre) * (1.0 / math.sqrt(2.0 * math.pi))

    def contract(c):
        r = rows(c)
        back = (nt(s.gall[r, :], s.wd[...]) * s.slope[r, :]).astype(BF)
        s.hpg[r, :] = back
        s.vec[6:7, fcols] += jnp.sum(back.astype(F32), axis=0, keepdims=True)
        s.vec[4:5, gcols] += jnp.sum(s.gall[r, gcols].astype(F32), axis=0, keepdims=True)
        dout = nt(s.gall[r, :], s.wo[...]).astype(BF).astype(F32)
        s.do[r, :] = dout.astype(BF)
        split_heads(s.dom, r, dout)

    rb, lb, fb = lax.rem(col + 1, 4), lax.rem(col + 3, 4), lax.rem(col + 2, 4)
    blocks = {"own": col, "left": lb, "right": rb, "far": fb}
    outward = ("far", "right", "left", "own")

    def mark(flag, work, *args):
        def both():
            work(*args)
            done.add(flag)

        return both

    first = [0, 256, 768, 1536]

    def fold(values, how):
        return how(values.reshape(-1, 8, B), axis=0)

    def attend(i):
        q = pl.ds(i * B, B)
        for c in range(i + 1):
            kid = lax.broadcasted_iota(jnp.int32, (B, B), 0)
            qid = lax.broadcasted_iota(jnp.int32, (B, B), 1)
            allowed = s.segc[pl.ds(c * B, B), 0:1] == rowv["seg"][:, i * B : (i + 1) * B]
            allowed = allowed & (kid <= qid) if c == i else allowed
            s.cap[pl.ds(c * B, B), :] = jnp.where(allowed, 3e38, -1e30)

        for h in range(2):
            top = jnp.full((8, B), -1e30, F32)
            for c in range(i + 1):
                k, at_c = pl.ds(c * B, B), pl.ds(first[i] + c * B, B)
                scores = jnp.minimum(nt(s.km[h, k, :], s.qs[q, :]), s.cap[k, :])
                s.probs[h, at_c, :] = scores
                top = jnp.maximum(top, fold(scores, jnp.max))
            top = jnp.max(top, axis=0, keepdims=True)
            total = jnp.zeros((8, B), F32)
            for c in range(i + 1):
                at_c = pl.ds(first[i] + c * B, B)
                expo = jnp.exp(s.probs[h, at_c, :] - top)
                s.probs[h, at_c, :] = expo
                total = total + fold(expo, jnp.sum)
            inverse = 1.0 / jnp.sum(total, axis=0, keepdims=True)
            hrows = pl.ds(h * HD, HD)
            mix = jnp.zeros((HD, B), F32)
            for c in range(i + 1):
                at_c = pl.ds(first[i] + c * B, B)
                probs = s.probs[h, at_c, :] * inverse
                s.probs[h, at_c, :] = probs
                mix = mix + nn(s.vt[hrows, pl.ds(c * B, B)], probs.astype(BF))
            s.mt[hrows, q] = mix.astype(BF)

        s.mixed[q, :] = s.mt[:, q].astype(F32).T.astype(BF)

    def attend_back(i):
        q = pl.ds(i * B, B)

        for h in range(2):
            inner = jnp.zeros((8, B), F32)
            for c in range(i + 1):
                k, at_c = pl.ds(c * B, B), pl.ds(first[i] + c * B, B)
                probs = s.probs[h, at_c, :]
                dprob = nt(s.vm[h, k, :], s.do[q, :])
                s.cap[k, :] = dprob
                inner = inner + fold(probs * dprob, jnp.sum)
                s.dv[k, :] += nn(probs.astype(BF), s.dom[h, q, :])
            inner = jnp.sum(inner, axis=0, keepdims=True)
            hrows = pl.ds(h * HD, HD)
            dquery = jnp.zeros((HD, B), F32)
            for c in range(i + 1):
                k, at_c = pl.ds(c * B, B), pl.ds(first[i] + c * B, B)
                dscore = (s.probs[h, at_c, :] * (s.cap[k, :] - inner)).astype(BF)
                s.dk[k, :] += nn(dscore, s.qsm[h, q, :])
                dquery = dquery + nn(s.kt[hrows, k], dscore)
            s.dqt[hrows, q] = dquery * (1.0 / math.sqrt(HD))

    def branch(b):
        r = rows(b)
        s.op[r, :] = (nn(s.mixed[r, :], s.wo[...]) + nn(s.hid[r, :], s.wd[...])).astype(BF)

    def down_early():
        gall = jnp.concatenate([s.gall[rows(b), :] for b in (col, lb, rb)])

        @pl.loop(0, 4)
        def _(f):
            r = rows(f, 128)
            hid = jnp.concatenate([s.hid[rows(b), r] for b in (col, lb, rb)])
            s.acc[r, :] = tn(hid, gall)

    def down_grad():
        @pl.loop(0, 4)
        def _(f):
            r = rows(f, 128)
            s.g1[r, :] = (s.acc[r, :] + tn(s.hid[rows(fb), r], s.gall[rows(fb), :])).astype(BF)

        s.g1[F:, :] = nn(s.mt[...], s.gall[...]).astype(BF)

    def up_grad():
        @pl.loop(0, 4)
        def _(b):
            r = rows(b, 128)
            s.g2[r, :] = tn(s.hpg[:, r], s.mim[...]).astype(BF)

    def qkv_grad(b):
        r = rows(b)
        cos, sin = s.ctab[r, :], -s.stab[r, :]
        dq = turn(s.dqt[:, r].T, cos, sin).astype(BF)
        dk = turn(s.dk[r, :], cos, sin).astype(BF)
        dv = s.dv[r, :].astype(BF)
        both = jnp.concatenate([dq, dk, dv], axis=1)
        s.qkvg[r, :] = both
        ecols3 = pl.ds(pl.multiple_of(row * 3 * E, 3 * E), 3 * E)
        s.vec[5:6, ecols3] += jnp.sum(both.astype(F32), axis=0, keepdims=True)

    def qkv_weight_grad():
        @pl.loop(0, 3)
        def _(b):
            r = rows(b, E)
            s.g3[r, :] = tn(s.qkvg[:, r], s.ain[...]).astype(BF)

    def input_grad(b):
        r = rows(b)
        gain0, gain1 = wide(0), wide(1)
        attn = nt(s.qkvg[r, :], s.wq[...])
        mlp = nt(s.hpg[r, :], s.wu[...])
        normed = (s.xall[r, :].astype(F32) - s.mean[r, :]) * s.inv[r, :]
        s.ng[r, :] = (attn * gain0 + mlp * gain1).astype(BF)
        s.vec[0:1, :] += jnp.sum(attn * normed, axis=0, keepdims=True)
        s.vec[1:2, :] += jnp.sum(mlp * normed, axis=0, keepdims=True)
        s.vec[2:3, :] += jnp.sum(attn, axis=0, keepdims=True)
        s.vec[3:4, :] += jnp.sum(mlp, axis=0, keepdims=True)

    so, sn = under(s, "o_"), under(s, "n_")
    where = dict(core=core, x=x, row=row)
    sums = []
    ny = YROWS["n"]
    own = rows(col)

    def look(h, total):
        mean, inv = s.mean[own, :], s.inv[own, :]
        xv = s.xall[pl.ds(pl.multiple_of(col * B, B), ny), pl.ds(h * half, half)].astype(F32)
        normed = (xv - mean[:ny]) * inv[:ny]
        sums.append(jnp.sum(total, axis=1, keepdims=True))
        sums.append(jnp.sum(total * normed, axis=1, keepdims=True))

    def write_out():
        xv = s.xall[own, gcols].astype(F32) + (flat(bout[...]) + flat(bdown[...]))
        total = jnp.concatenate([total_y(so, row), total_z(s.op, so, col, row, YROWS["o"])])
        out[...] = (xv + total).astype(BF)

    def write_grad():
        yield ("n.y.sum", "n.y.end", "n.z.sum"), 0.4
        mean, inv = s.mean[own, :], s.inv[own, :]
        normed = (s.xall[own, gcols].astype(F32) - mean) * inv
        zsum = total_z(s.ng, sn, col, row, ny)
        first_sum = jnp.concatenate([sums[0] + sums[2], jnp.sum(zsum, axis=1, keepdims=True)])
        second = jnp.sum(zsum * normed[ny:], axis=1, keepdims=True)
        second_sum = jnp.concatenate([sums[1] + sums[3], second])
        lane = lax.broadcasted_iota(jnp.int32, (B, 128), 1)
        s.ssend[...] = jnp.where(lane < 4, first_sum, second_sum).T[:8, :]
        ys = net.go(s.ssend, s.srecv, y1)
        yield (ys,), 0.5
        ys.wait_recv()
        both = (s.ssend[...] + s.srecv[...]) * (1.0 / D)
        both = jnp.concatenate([both] * 16).T
        total = jnp.concatenate([total_y(sn, row), zsum])
        tgrad[...] = (
            s.gall[own, gcols].astype(F32) + inv * (total - both[:, 0:1] - normed * both[:, 4:5])
        ).astype(BF)

    def write_vectors():
        vout[0] = s.vs[2]
        vout[1] = s.vs[3]

    scatter(net, add, done, "o.", tuple("send." + b for b in outward), s.op, so, at, col, row, YROWS["o"])
    scatter(net, add, done, "n.", tuple("ng." + b for b in outward), s.ng, sn, at, col, row, ny, look)
    gate = ("g.r3", "g.r4", "g.l3", "g.l4")
    for b in outward:
        add(later(("op." + b,) + gate, 0.0, mark("send." + b, lambda: None)))
    reduce_weights(net, add, done, "a.", "g1", s.g1, under(s, "r0_", fin=s.f0), at, where, ROWS[0])
    reduce_weights(net, add, done, "b.", "g2", s.g2, under(s, "r1_", fin=s.f1), at, where, ROWS[1])
    reduce_weights(net, add, done, "c.", "g3", s.g3, under(s, "r2_", fin=s.f2), at, where, ROWS[2])
    writes = []

    def write_reduced(src, dst):
        writes.append(net.local(src, dst))

    for name, src, dst in (("a.", s.f0, f0_h), ("b.", s.f1, f1_h), ("c.", s.f2, f2_h)):
        add(later((name + "end",), 0.02, partial(write_reduced, src, dst)))
    add(reduce_vectors(net, done, s, at))
    add(later(("vsum",), 0.05, write_vectors))
    add(write_grad())
    for name, b in blocks.items():
        add(later(("nb", "x." + name), 0.5, mark("norm." + name, norm, b)))
        add(later(("wq", "norm." + name), 0.45, mark("proj." + name, project, b)))
    needs = tuple("proj." + name for name in blocks)
    for i in range(4):
        add(later(needs, 0.37 * (i + 1), mark(f"attf{i}", attend, i)))
        needs = (f"attf{i}",)
    for name, b in blocks.items():
        add(later(("wu", "norm." + name), 0.36, mark("exp." + name, expand, b)))
    for name in outward:
        needs = ("wo", "wd", "attf3", "exp." + name)
        add(later(needs, 0.55, mark("op." + name, branch, blocks[name])))
    for name, b in blocks.items():
        needs = ("wo", "wd", "g." + name, "exp." + name)
        add(later(needs, 0.43, mark("con." + name, contract, b)))
    near = ("own", "left", "right")
    needs = tuple("g." + name for name in near) + tuple("exp." + name for name in near)
    add(later(needs, 1.9, mark("g1early", down_early)))
    add(later(("g1early", "g.far", "exp.far", "attf3"), 0.95, mark("g1", down_grad)))
    allc = tuple("con." + name for name in blocks)
    add(later(allc, 2.2, mark("g2", up_grad)))
    needs = allc + ("attf3",)
    for i in range(4):
        add(later(needs, 0.43 * (i + 1), mark(f"attb{i}", attend_back, i)))
        needs = (f"attb{i}",)
    for name in outward:
        add(later(("attb3",), 0.26, mark("qg." + name, qkv_grad, blocks[name])))
    add(later(tuple("qg." + name for name in blocks), 1.4, mark("g3", qkv_weight_grad)))
    for name in outward:
        add(later(("qg." + name,), 0.68, mark("ng." + name, input_grad, blocks[name])))
    add(later(tuple("ng." + name for name in blocks), 0.0, mark("vec", lambda: None)))
    add(later(("o.y.end", "o.z.sum"), 0.3, mark("out", write_out)))
    run(tasks, done)
    for copy in writes:
        copy.wait()
    for copy in net.sent:
        copy.wait_send()


def tables():
    freq = np.arange(ROT // 2, dtype=np.float32)
    inverse = np.float32(10000.0) ** (np.float32(-2.0) * freq / np.float32(ROT))
    angle = np.arange(T, dtype=np.float32)[:, None] * inverse[None, :].astype(np.float32)
    cos, sin = np.cos(angle), np.sin(angle)
    ones, zeros = np.ones((T, HD - ROT), np.float32), np.zeros((T, HD - ROT), np.float32)
    ctab = np.concatenate([cos, cos, ones] * 2, axis=1)
    stab = np.concatenate([-sin, sin, zeros] * 2, axis=1)
    return ctab.astype(np.float32), stab.astype(np.float32)


def last(
    f0_h, f1_h, f2_h, vec_h, out_h, tgrad_h,
    out_o, tgrad_o, wq_o, bq_o, wo_o, bo_o, wu_o, bu_o, wd_o, bd_o, gain_o, bias_o,
    f0, f1, f2, vec, out, tgrad, wq, wo, wu, wd, bq, bo, bu, gain, bias, sems,
):
    row = lax.axis_index("row")
    copies = []

    def write(src, dst):
        copy = pltpu.make_async_copy(src, dst, sems.at[len(copies)])
        copy.start()
        copies.append(copy)
        return copy

    pairs = ((f0_h, f0), (f1_h, f1), (f2_h, f2), (vec_h, vec), (out_h, out), (tgrad_h, tgrad))
    reads = [write(a, b) for a, b in pairs]
    reads[0].wait()
    for r in range(2):
        for k in range(8):
            piece = f0[k // 4, k % 4, r].astype(F32)
            n = piece.shape[0]
            inside = max(0, min(n, F - k * n))
            if inside:
                wd[pl.ds(r * F + k * n, inside), :] = piece[:inside]
            if inside < n:
                wo[pl.ds(r * E + k * n + inside - F, n - inside), :] = piece[inside:]
        write(wd.at[pl.ds(r * F, F)], wd_o.at[pl.ds(r * F, F)])
    write(wo, wo_o)
    reads[1].wait()
    for r in range(2):
        for k in range(4):
            pair = [f1[(2 * k + h) // 4, (2 * k + h) % 4, r].astype(F32) for h in range(2)]
            wu[:, pl.ds(r * F + k * E, E)] = jnp.concatenate(pair).T
        write(wu.at[:, pl.ds(r * F, F)], wu_o.at[:, pl.ds(r * F, F)])
    reads[2].wait()
    for r in range(2):
        whole = jnp.concatenate([f2[k // 4, k % 4, r].astype(F32) for k in range(8)])
        for k in range(3):
            wq[k, :, pl.ds(r * E, E)] = whole[k * E : (k + 1) * E].T
    write(wq, wq_o)
    for copy in reads[3:]:
        copy.wait()
    write(out, out_o)
    write(tgrad, tgrad_o)
    half = D // 2
    left = row == 0

    def cut(values):
        return jnp.where(left, values[:, :half], values[:, half:])

    bo[...] = cut(vec[0, 4:5, :])
    for k in range(3):
        bq[k : k + 1, :E] = vec[0, 5:6, k * E : (k + 1) * E]
        bq[k : k + 1, E:] = vec[0, 5:6, (k + 3) * E : (k + 4) * E]
    bu[...] = vec[0, 6:7, :]
    gain[...] = cut(vec[1, 0:2, :])
    bias[...] = cut(vec[1, 2:4, :])
    for a, b in ((bq, bq_o), (bo, bo_o), (bo, bd_o), (bu, bu_o), (gain, gain_o), (bias, bias_o)):
        write(a, b)
    for copy in copies[len(reads) :]:
        copy.wait()


def on_device(
    tokens, segment_ids, w_qkv, b_qkv, w_out, b_out, w_up, b_up, w_down, b_down, norm_gain, norm_bias, cotangent
):
    ctab, stab = tables()
    vmem = pl.BlockSpec(memory_space=pltpu.VMEM)
    hbm = pl.BlockSpec(memory_space=pl.ANY)
    shape = jax.ShapeDtypeStruct
    early = [
        shape((2, 4, 2, ROWS[0] // 8, D // 2), BF),
        shape((2, 4, 2, ROWS[1] // 8, D // 2), BF),
        shape((2, 4, 2, ROWS[2] // 8, D // 2), BF),
        shape((2, 8, D), F32),
    ]
    out, tgrad, f0, f1, f2, vec = pl.pallas_call(
        body,
        out_shape=[
            shape((B, D // 2), BF),
            shape((B, D // 2), BF),
            *early,
        ],
        in_specs=[hbm] * 6 + [vmem] * 7 + [hbm] * 2,
        out_specs=[vmem, vmem, hbm, hbm, hbm, vmem],
        scratch_shapes=[pltpu.VMEM(*spec) for spec in SCRATCH.values()]
        + [pltpu.SemaphoreType.DMA((NSEM,)), pltpu.SemaphoreType.DMA((NSEM,))],
        compiler_params=pltpu.CompilerParams(
            collective_id=0, has_side_effects=True, vmem_limit_bytes=60 * 1024 * 1024
        ),
        name="block",
    )(
        tokens, cotangent, w_qkv, w_out, w_up, w_down, b_qkv, b_up.reshape(8, 128),
        b_out.reshape(4, 128), b_down.reshape(4, 128), norm_gain, norm_bias,
        segment_ids.reshape(8, 128), jnp.asarray(ctab), jnp.asarray(stab),
    )
    big = [
        ((3, D // 2, 2 * E), F32),
        ((2 * E, D // 2), F32),
        ((D // 2, 2 * F), F32),
        ((2 * F, D // 2), F32),
    ]
    small = [((3, 2 * E), F32), ((1, D // 2), F32), ((1, 2 * F), F32)] + [((2, D // 2), F32)] * 2
    results = pl.pallas_call(
        last,
        out_shape=[
            shape((B, D // 2), BF),
            shape((B, D // 2), BF),
            shape(*big[0]),
            shape((3, 2 * E), F32),
            shape(*big[1]),
            shape((1, D // 2), F32),
            shape(*big[2]),
            shape((1, 2 * F), F32),
            shape(*big[3]),
            shape((1, D // 2), F32),
            shape((2, D // 2), F32),
            shape((2, D // 2), F32),
        ],
        in_specs=[hbm] * 6,
        out_specs=[hbm] * 12,
        scratch_shapes=[pltpu.VMEM(e.shape, e.dtype) for e in early]
        + [pltpu.VMEM((B, D // 2), BF)] * 2
        + [pltpu.VMEM(*spec) for spec in big + small]
        + [pltpu.SemaphoreType.DMA((24,))],
        compiler_params=pltpu.CompilerParams(vmem_limit_bytes=60 * 1024 * 1024),
        name="last",
    )(f0, f1, f2, vec, out, tgrad)
    out, tgrad, wq, bq, wo, bo, wu, bu, wd, bd, gain, bias = results
    bo, bu, bd = bo.reshape(-1), bu.reshape(-1), bd.reshape(-1)
    return (out, tgrad, wq, bq, wo, bo, wu, bu, wd, bd, gain, bias)


def solution(mesh):
    in_specs = (
        P(("dp", "col"), "row"),
        P("dp"),
        P(None, "row", "col"),
        P(None, "col"),
        P("col", "row"),
        P("row"),
        P("row", "col"),
        P("col"),
        P("col", "row"),
        P("row"),
        P(None, "row"),
        P(None, "row"),
        P(("dp", "col"), "row"),
    )
    out_specs = (
        P(("dp", "col"), "row"),
        P(("dp", "col"), "row"),
        P(None, "row", "col"),
        P(None, "col"),
        P("col", "row"),
        P("row"),
        P("row", "col"),
        P("col"),
        P("col", "row"),
        P("row"),
        P(None, "row"),
        P(None, "row"),
    )
    return jax.shard_map(
        on_device, mesh=mesh, in_specs=in_specs, out_specs=out_specs, check_vma=False
    )
```

```python
from functools import partial
from types import SimpleNamespace
import math

import numpy as np
import jax
import jax.numpy as jnp
from jax import lax
from jax.experimental import pallas as pl
from jax.experimental.pallas import tpu as pltpu
from jax.sharding import PartitionSpec as P

MESH = pl.DeviceIdType.MESH
BF = jnp.bfloat16
F32 = jnp.float32
T = 1024
D = 1024
HD = 64
ROT = 16
E = 128
F = 512
B = 256
EPSILON = 1e-05
NSEM = 200
YROWS = dict(x=112, g=128, o=160, n=208)


ORDER = (
    1, 4, 3, 5, 0, 8, 2, 9, 44, 44, 2, 6, 10, 4, 12, 3, 7, 11, 40, 5, 13, 9, 8, 16, 131, 40, 132, 6,
    14, 21, 23, 24, 25, 29, 10, 12, 18, 135, 136, 41, 7, 15, 20, 22, 28, 42, 13, 11, 17, 133, 14,
    41, 134, 145, 42, 144, 143, 23, 31, 24, 32, 27, 15, 19, 137, 146, 138, 139, 43, 140, 25, 33,
    141, 22, 29, 30, 26, 142, 43, 27, 35, 148, 147, 28, 36, 151, 149, 150, 33, 26, 80, 34, 50, 46,
    82, 48, 81, 47, 79, 45, 49, 53, 31, 52, 51, 30, 37, 152, 32, 38, 153, 155, 34, 35, 39, 154, 156,
    83, 157, 53, 97, 46, 52, 56, 54, 158, 48, 159, 83, 85, 84, 88, 86, 87, 160, 47, 57, 97, 100, 99,
    98, 101, 102, 161, 45, 88, 55, 59, 58, 54, 61, 162, 167, 66, 62, 163, 87, 89, 164, 165, 166, 59,
    58, 60, 111, 168, 63, 67, 69, 101, 102, 103, 169, 64, 68, 70, 170, 89, 90, 61, 171, 128, 65,
    111, 112, 113, 114, 115, 62, 72, 116, 69, 63, 73, 70, 75, 71, 103, 104, 128, 60, 172, 64, 74,
    76, 115, 116, 117, 90, 91, 92, 65, 128, 75, 76, 77, 117, 118, 91, 93, 92, 94, 95, 104, 106, 105,
    94, 93, 71, 78, 128, 77, 95, 96, 118, 119, 120, 105, 107, 106, 109, 108, 96, 125, 107, 108, 128,
    129, 119, 121, 120, 122, 123, 121, 122, 78, 130, 109, 110, 123, 124, 130, 110, 126, 124, 127,
)


def nn(a, b):
    return jnp.dot(a, b, preferred_element_type=F32)


def nt(a, b):
    return lax.dot_general(a, b, (((1,), (1,)), ((), ())), preferred_element_type=F32)


def tn(a, b):
    return lax.dot_general(a, b, (((0,), (0,)), ((), ())), preferred_element_type=F32)


def rows(block, size=B):
    return pl.ds(pl.multiple_of(block * size, size), size)


class Net:
    def __init__(self, send, recv):
        self.send, self.recv, self.count, self.sent = send, recv, 0, []

    def go(self, src, dst, device):
        k = self.count
        self.count += 1
        assert k < NSEM
        copy = pltpu.make_async_remote_copy(
            src_ref=src,
            dst_ref=dst,
            send_sem=self.send.at[k],
            recv_sem=self.recv.at[k],
            device_id=device,
            device_id_type=MESH,
        )
        copy.start()
        self.sent.append(copy)
        return copy

    def local(self, src, dst):
        k = self.count
        self.count += 1
        assert k < NSEM
        copy = pltpu.make_async_copy(src, dst, self.send.at[k])
        copy.start()
        return copy


def later(deps, cost, work):
    yield deps, cost
    work()


def gather_tokens(net, add, done, name, begin, own, full, at, half, col, row, yr):
    right, left, peer = at["z1"], at["z3"], at["y1"]
    zr = B - yr
    part = zr // 32 * 16
    cut = yr + part
    c = {}

    def place(b, h, start=0, size=B):
        r = pl.ds(pl.multiple_of(b * B + start, 16), size)
        return full.at[r, pl.ds(pl.multiple_of(h * half, half), half)]

    def move(key, device, *where):
        c[key] = net.go(place(*where), place(*where), device)
        done.add(name + key)

    def send(key, device, start, size):
        c[key] = net.go(own.at[pl.ds(start, size)], place(col, row, start, size), device)
        done.add(name + key)

    lcol, rcol, fcol = lax.rem(col + 3, 4), lax.rem(col + 1, 4), lax.rem(col + 2, 4)

    def begin_y():
        yield begin[0], 0.1
        c["keep"] = net.local(own, place(col, row))
        send("p0", peer, 0, yr)
        send("p1", peer, yr, zr)
        c["keep"].wait()
        done.add(name + "keep")

    def begin_z():
        yield begin[1], 0.1
        send("r1", right, yr, zr)
        send("l1", left, yr, zr)
        send("r0", right, 0, yr)
        send("l0", left, 0, yr)

    def hop(keys, *work):
        yield tuple(name + k for k in keys), 0.0
        yield tuple(c[k] for k in keys), 0.05
        for k in keys:
            c[k].wait_recv()
        for w in work:
            move(*w)
        done.update(name + k + "!" for k in keys)

    def whole(flag, keys):
        yield tuple(name + k + ("" if k == "keep" else "!") for k in keys), 0.0
        done.add(name + flag)

    add(begin_y())
    add(begin_z())
    add(hop(["p0"], ("r2", right, col, 1 - row, 0, yr), ("l2", left, col, 1 - row, 0, yr)))
    add(hop(["r1"], ("r3", right, lcol, row, yr, part), ("p2", peer, lcol, row, yr, zr)))
    add(hop(["l1"], ("l3", left, rcol, row, cut, B - cut), ("p3", peer, rcol, row, yr, zr)))
    add(hop(["r0"], ("r4", right, lcol, row, 0, yr)))
    add(hop(["l2"], ("l4", left, rcol, 1 - row, 0, yr)))
    add(hop(["r3", "l3"], ("p4", peer, fcol, row, yr, zr)))
    add(hop(["p1"]))
    add(hop(["l0"]))
    add(hop(["r2"]))
    add(hop(["p2"]))
    add(hop(["p3"]))
    add(hop(["r4"]))
    add(hop(["l4"]))
    add(hop(["p4"]))
    add(whole("own", ["p0", "p1", "keep"]))
    add(whole("left", ["r0", "r1", "r2", "p2"]))
    add(whole("right", ["l0", "l1", "l2", "p3"]))
    add(whole("far", ["r3", "r4", "l3", "l4", "p4"]))


def gather_weights(net, add, done, wqkv, wup, wout, wdown, s, at, core, row):
    half, part = D // 2, D // 4
    mine, theirs = row, 1 - row
    drows, ocols = rows(row, half), rows(1 - row, half)

    def cut(which, size):
        return pl.ds(pl.multiple_of(which * size, size), size)

    local = {}
    for k in range(3):
        kcols = pl.ds(k * E, E)
        local[k] = net.local(wqkv.at[k, :, cut(mine, E)], s.wq.at[drows, kcols])
    local["u"] = net.local(wup.at[:, cut(mine, F)], s.wu.at[drows])
    local["o"] = net.local(wout.at[cut(mine, E)], s.wo.at[:, drows])
    local["d"] = net.local(wdown.at[cut(mine, F)], s.wd.at[:, drows])
    src, dst, got = cut(core, part), cut(row * 2 + core, part), cut((1 - row) * 2 + core, part)
    far, near = at["y3"], at["core"]
    q = [
        net.go(wqkv.at[k, src, cut(theirs, E)], s.wq.at[dst, pl.ds(k * E, E)], far)
        for k in range(3)
    ]
    u = net.go(wup.at[src, cut(theirs, F)], s.wu.at[dst], far)
    o = net.go(wout.at[cut(theirs * 2 + core, E // 2)], s.wo.at[cut(core, E // 2), drows], far)
    d = net.go(wdown.at[cut(theirs * 2 + core, F // 2)], s.wd.at[cut(core, F // 2), drows], far)

    def share(flag, copies, view, locals_):
        yield tuple(copies), 0.05
        for copy in copies:
            copy.wait_recv()
        second = net.go(view, view, near)
        yield (second,), 0.0
        second.wait_recv()
        for k in locals_:
            local[k].wait()
        done.add(flag)

    add(share("wq", q, s.wq.at[got], range(3)))
    add(share("wu", [u], s.wu.at[got], "u"))
    add(share("wo", [o], s.wo.at[cut(core, E // 2), ocols], "o"))
    add(share("wd", [d], s.wd.at[cut(core, F // 2), ocols], "d"))


def ring_scatter(net, add, done, name, part, bufs, me, right, left, width, ready):
    ta, tb, inl, inr = bufs
    lo, hi = pl.ds(0, width), pl.ds(width, width)
    far, rb, lb = lax.rem(me + 2, 4), lax.rem(me + 1, 4), lax.rem(me + 3, 4)
    c = {}

    def send(deps, *sends):
        yield deps, 0.05
        for key, src, dst, device in sends:
            c[key] = net.go(src, dst, device)
            done.add(name + key)

    def through(came, flag, buf, view, key, dst, device):
        yield (name + came, flag), 0.0
        yield (c[came],), 0.15
        c[came].wait_recv()
        view[...] = (view[...].astype(F32) + buf[...].astype(F32)).astype(BF)
        c[key] = net.go(view, dst, device)
        done.add(name + key)

    def finish():
        yield tuple(name + k for k in "cdef") + (ready[3],), 0.0
        yield tuple(c[k] for k in "cdef"), 0.0
        for k in "cdef":
            c[k].wait_recv()
        done.add(name + "sum")

    add(send((ready[0],), ("a", part(far, lo), ta, right), ("b", part(far, hi), tb, left)))
    add(send((ready[1],), ("c", part(rb, hi), inl.at[:, hi], right)))
    add(send((ready[2],), ("d", part(lb, lo), inr.at[:, lo], left)))
    add(through("a", ready[1], ta, part(rb, lo), "e", inl.at[:, lo], right))
    add(through("b", ready[2], tb, part(lb, hi), "f", inr.at[:, hi], left))
    add(finish())


def reduce_weights(net, add, done, name, begin, grad, s, at, me, n):
    core, x, row = me["core"], me["x"], me["row"]
    half, size = n // 2, n // 8
    base, away = core * half, (1 - core) * half
    x1, x3, near = at["x1"], at["x3"], at["core"]
    lx, rx, fx = lax.rem(x + 3, 4), lax.rem(x + 1, 4), lax.rem(x + 2, 4)
    c = {}

    def start():
        yield (begin,), 0.05
        copy = net.go(grad.at[pl.ds(pl.multiple_of(away, half), half)], s.rc, near)
        yield (copy,), 0.4 * n / 640
        copy.wait_recv()
        own = grad.at[pl.ds(pl.multiple_of(base, half), half)]
        own[...] = (own[...].astype(F32) + s.rc[...].astype(F32)).astype(BF)
        done.add(name + "core")

    def part(block, cols):
        return grad.at[pl.ds(pl.multiple_of(base + block * size, size), size), cols]

    def across():
        yield (name + "sum",), 0.2
        for h in range(2):
            cols = pl.ds(h * (D // 2), D // 2)
            total = part(x, cols)[...].astype(F32) + s.inl[:, cols].astype(F32)
            s.sy[h] = (total + s.inr[:, cols].astype(F32)).astype(BF)
        g0 = net.go(s.sy.at[row], s.ry.at[0], at["y2"])
        g1 = net.go(s.sy.at[1 - row], s.ry.at[1], at["y1"])
        g2 = net.go(s.sy.at[1 - row], s.ry.at[2], at["y3"])
        yield (g0, g1, g2), 0.15
        for copy in (g0, g1, g2):
            copy.wait_recv()
        s.fin[core, x, row] = (s.sy[row].astype(F32) + s.ry[0].astype(F32)).astype(BF)
        s.fin[core, x, 1 - row] = (s.ry[1].astype(F32) + s.ry[2].astype(F32)).astype(BF)
        for key, h, device in (("a", 0, x1), ("b", 1, x3), ("c", 1, x1), ("d", 0, x3)):
            view = s.fin.at[core, x, h]
            c[key] = net.go(view, view, device)
        view = s.fin.at[core, x]
        c["k"] = net.go(view, view, near)
        done.add(name + "sent")

    def hop(keys, flag, view, device, key, need=()):
        yield (name + flag,) + tuple(name + k + "!" for k in need), 0.0
        yield tuple(c[k] for k in keys), 0.05
        for k in keys:
            c[k].wait_recv()
        c[key] = net.go(view, view, device)
        done.update(name + k + "!" for k in keys)
        done.add(name + key)

    def end():
        yield tuple(name + k for k in ("l", "m", "n")), 0.0
        yield tuple(c[k] for k in "klmn"), 0.0
        for k in "klmn":
            c[k].wait_recv()
        done.add(name + "end")

    ready = (name + "core",) * 4
    add(start())
    ring_scatter(
        net, add, done, name, part, (s.ta, s.tb, s.inl, s.inr), x, x1, x3, D // 2, ready
    )
    add(across())
    add(hop("a", "sent", s.fin.at[core, lx, 0], x1, "p"))
    add(hop("b", "sent", s.fin.at[core, rx, 1], x3, "q"))
    add(hop("c", "sent", s.fin.at[core, lx], near, "l", "a"))
    add(hop("d", "sent", s.fin.at[core, rx], near, "m", "b"))
    add(hop("pq", "p", s.fin.at[core, fx], near, "n", "b"))
    add(end())


def reduce_vectors(net, done, s, at):
    yield ("vec",), 0.0
    c = net.go(s.vec, s.vr.at[0], at["core"])
    yield (c,), 0.05
    c.wait_recv()
    s.vs[0] = s.vec[...] + s.vr[0]
    for n, axis in enumerate("xyz"):
        copies = [net.go(s.vs.at[n], s.vr.at[3 * n + k], at[axis + str(k)]) for k in (1, 2, 3)]
        yield tuple(copies), 0.05
        for copy in copies:
            copy.wait_recv()
        s.vs[n + 1] = (s.vs[n] + s.vr[3 * n + 1]) + (s.vr[3 * n + 2] + s.vr[3 * n + 3])
    done.add("vsum")


def scatter(net, add, done, name, ready, p, s, at, col, row, yr, look=None):
    half, zr = D // 2, B - yr
    far, rb, lb = lax.rem(col + 2, 4), lax.rem(col + 1, 4), lax.rem(col + 3, 4)
    mcols, ocols = rows(row, half), rows(1 - row, half)
    right, left, peer = at["z1"], at["z3"], at["y1"]

    def yrows(b):
        return pl.ds(pl.multiple_of(b * B, B), yr)

    def zrows(b):
        return pl.ds(pl.multiple_of(b * B + yr, 16), zr)

    def zpart(b, cols):
        return p.at[zrows(b), pl.ds(pl.multiple_of(row * half + cols.start, 256), cols.size)]

    def pair(k, b):
        yield (ready[k],), 0.05
        copy = net.go(p.at[zrows(b), ocols], s.ry.at[k], peer)
        yield (copy,), 0.15
        copy.wait_recv()
        view = p.at[zrows(b), mcols]
        view[...] = (view[...].astype(F32) + s.ry[k].astype(F32)).astype(BF)
        done.add(name + "z" + str(k))

    def last():
        yield (name + "y.sum",), 0.3
        for h in range(2):
            cols = pl.ds(h * half, half)
            total = p[yrows(col), cols].astype(F32) + s.inl[:, cols].astype(F32)
            total += s.inr[:, cols].astype(F32)
            s.ysend[h] = total.astype(BF)
            if look is not None:
                look(h, total)
        copy = net.go(s.ysend.at[1 - row], s.yrecv, peer)
        yield (copy,), 0.0
        copy.wait_recv()
        done.add(name + "y.end")

    for k, b in enumerate((far, rb, lb, col)):
        add(pair(k, b))
    ring_scatter(
        net, add, done, name + "y.", lambda b, cols: p.at[yrows(b), cols],
        (s.ta, s.tb, s.inl, s.inr), col, right, left, half, ready,
    )
    ring_scatter(
        net, add, done, name + "z.", zpart,
        (s.ta2, s.tb2, s.inl2, s.inr2), col, right, left, half // 2,
        tuple(name + "z" + str(k) for k in range(4)),
    )
    add(last())


def total_y(s, row):
    return s.ysend[row].astype(F32) + s.yrecv[...].astype(F32)


def total_z(p, s, col, row, yr):
    own = p[pl.ds(pl.multiple_of(col * B + yr, 16), B - yr), rows(row, D // 2)]
    return own.astype(F32) + s.inl2[...].astype(F32) + s.inr2[...].astype(F32)


def run(tasks, done):
    asked = [next(task)[0] for task in tasks]
    for k in ORDER:
        for need in asked[k]:
            assert not isinstance(need, str) or need in done, "order"
        asked[k] = next(tasks[k], ((),))[0]
    assert all(next(task, None) is None for task in tasks), "unfinished"


def turn(values, cos, sin):
    lane = lax.broadcasted_iota(jnp.int32, values.shape, 1)
    other = jnp.where(lane % HD < ROT // 2, pltpu.roll(values, E - ROT // 2, 1), pltpu.roll(values, ROT // 2, 1))
    return values * cos + other * sin


def split_heads(ref, at_rows, values):
    lane = lax.broadcasted_iota(jnp.int32, values.shape, 1)
    zero = jnp.zeros_like(values)
    ref[0, at_rows, :] = jnp.where(lane < HD, values, zero).astype(BF)
    ref[1, at_rows, :] = jnp.where(lane < HD, zero, values).astype(BF)


SCRATCH = dict(
    xall=((T, D), BF),
    gall=((T, D), BF),
    ain=((T, D), BF),
    mim=((T, D), BF),
    wq=((D, 3 * E), BF),
    wo=((E, D), BF),
    wu=((D, F), BF),
    wd=((F, D), BF),
    nb=((2, 8, D // 2), F32),
    mean=((T, 1), F32),
    inv=((T, 1), F32),
    hid=((T, F), BF),
    slope=((T, F), F32),
    segc=((T, 8), F32),
    nbs=((8, D // 2), F32),
    hpg=((T, F), BF),
    qs=((T, E), BF),
    qsm=((2, T, E), BF),
    km=((2, T, E), BF),
    vm=((2, T, E), BF),
    kt=((E, T), BF),
    vt=((E, T), BF),
    do=((T, E), BF),
    dom=((2, T, E), BF),
    probs=((2, 2560, B), F32),
    mt=((E, T), BF),
    mixed=((T, E), BF),
    dqt=((E, T), F32),
    cap=((T, B), F32),
    acc=((F, D), F32),
    dk=((T, E), F32),
    dv=((T, E), F32),
    qkvg=((T, 3 * E), BF),
    op=((T, D), BF),
    ng=((T, D), BF),
    ctab=((T, E), F32),
    stab=((T, E), F32),
    ssend=((8, B), F32),
    srecv=((8, B), F32),
    g1=((F + E, D), BF),
    g2=((F, D), BF),
    g3=((3 * E, D), BF),
    f0=((2, 4, 2, (F + E) // 8, D // 2), BF),
    f1=((2, 4, 2, F // 8, D // 2), BF),
    f2=((2, 4, 2, 3 * E // 8, D // 2), BF),
    vec=((8, D), F32),
    vr=((10, 8, D), F32),
    vs=((4, 8, D), F32),
)
def scatter_scratch(yr):
    zr = B - yr
    return dict(
        ta=((yr, D // 2), BF),
        tb=((yr, D // 2), BF),
        inl=((yr, D), BF),
        inr=((yr, D), BF),
        ry=((4, zr, D // 2), BF),
        ta2=((zr, D // 4), BF),
        tb2=((zr, D // 4), BF),
        inl2=((zr, D // 2), BF),
        inr2=((zr, D // 2), BF),
        ysend=((2, yr, D // 2), BF),
        yrecv=((yr, D // 2), BF),
    )


def reduce_scratch(n):
    return dict(
        rc=((n // 2, D), BF),
        ta=((n // 8, D // 2), BF),
        tb=((n // 8, D // 2), BF),
        inl=((n // 8, D), BF),
        inr=((n // 8, D), BF),
        sy=((2, n // 8, D // 2), BF),
        ry=((3, n // 8, D // 2), BF),
    )


ROWS = (F + E, F, 3 * E)
for name in "on":
    SCRATCH.update({name + "_" + key: v for key, v in scatter_scratch(YROWS[name]).items()})
for k, n in enumerate(ROWS):
    SCRATCH.update({f"r{k}_{key}": spec for key, spec in reduce_scratch(n).items()})


def under(s, prefix, **more):
    picked = {k[len(prefix) :]: v for k, v in vars(s).items() if k.startswith(prefix)}
    return SimpleNamespace(**picked, **more)


def body(
    tok, cot, wqkv, wout, wup, wdown, bqkv, bup, bout, bdown, gain, bias, seg, ctab_h, stab_h,
    out, tgrad, f0_h, f1_h, f2_h, vout, *scratch,
):
    s = SimpleNamespace(**dict(zip(SCRATCH, scratch)))
    send, recv = scratch[len(SCRATCH) :]
    net = Net(send, recv)
    dp, row, col = lax.axis_index("dp"), lax.axis_index("row"), lax.axis_index("col")
    core, x, yh = lax.rem(dp, 2), lax.rem(dp // 2, 4), dp // 8
    half = D // 2

    def dev(core=core, x=x, yh=yh, row=row, col=col):
        return (yh * 8 + x * 2 + core, row, col)

    at = {"core": dev(core=1 - core)}
    for k in (1, 2, 3):
        at[f"x{k}"] = dev(x=lax.rem(x + k, 4))
        at[f"z{k}"] = dev(col=lax.rem(col + k, 4))
    at["y1"] = dev(row=1 - row)
    at["y2"] = dev(yh=1 - yh)
    at["y3"] = dev(yh=1 - yh, row=1 - row)
    y1 = at["y1"]

    s.nbs[...] = jnp.concatenate(
        [gain[...].astype(F32), bias[...].astype(F32), jnp.zeros((4, half), F32)]
    )
    barrier = pltpu.get_barrier_semaphore()
    for device in at.values():
        pl.semaphore_signal(barrier, inc=1, device_id=device, device_id_type=MESH)
    pl.semaphore_wait(barrier, len(at))

    tasks, done = [], set()
    add = tasks.append
    gather_tokens(net, add, done, "x.", ((), ()), tok, s.xall, at, half, col, row, YROWS["x"])
    gather_tokens(net, add, done, "g.", (("x.p4",), ("x.r3", "x.r4", "x.l3", "x.l4")), cot, s.gall, at, half, col, row, YROWS["g"])
    nbc = net.go(s.nbs, s.nb.at[row], y1)
    gather_weights(net, add, done, wqkv, wup, wout, wdown, s, at, core, row)
    tabs = [net.local(ctab_h, s.ctab), net.local(stab_h, s.stab)]
    def flat(values):
        values = values.astype(F32)
        return jnp.concatenate([values[k : k + 1, :] for k in range(values.shape[0])], axis=1)

    rowv = {}
    fcols = pl.ds(pl.multiple_of(row * F, F), F)
    gcols = pl.ds(pl.multiple_of(row * half, half), half)

    def wide(k):
        return jnp.concatenate([s.nb[0, k : k + 1, :], s.nb[1, k : k + 1, :]], axis=1)

    def params():
        yield ("x.r0", "x.p1"), 0.4
        s.nb[row] = s.nbs[...]
        s.vec[...] = jnp.zeros_like(s.vec)
        s.dk[...] = jnp.zeros_like(s.dk)
        s.dv[...] = jnp.zeros_like(s.dv)
        rowv["seg"] = flat(seg[...])
        s.segc[...] = jnp.broadcast_to(rowv["seg"], (8, T)).T
        bq_all, bu_all, mine = bqkv[...].astype(F32), flat(bup[...]), row == 0
        parts = [
            jnp.where(mine, bq_all[k : k + 1, :E], bq_all[k : k + 1, E:]) for k in range(3)
        ]
        rowv["bq"] = jnp.concatenate(parts, axis=1)
        rowv["bu"] = jnp.where(mine, bu_all[:, :F], bu_all[:, F:])
        yield (nbc,), 0.0
        nbc.wait_recv()
        for copy in tabs:
            copy.wait()
        done.add("nb")

    add(params())

    def norm(c):
        gain0, gain1, bias0, bias1 = wide(0), wide(1), wide(2), wide(3)

        @pl.loop(0, 2)
        def _(b):
            r = rows(c * 2 + b, 128)
            xv = s.xall[r, :].astype(F32)
            mean = jnp.sum(xv, axis=1, keepdims=True) * (1.0 / D)
            square = jnp.sum(xv * xv, axis=1, keepdims=True) * (1.0 / D)
            inv = lax.rsqrt(square - mean * mean + EPSILON)
            normed = (xv - mean) * inv
            s.mean[r, :] = mean
            s.inv[r, :] = inv
            s.ain[r, :] = (normed * gain0 + bias0).astype(BF)
            s.mim[r, :] = (normed * gain1 + bias1).astype(BF)

    def project(c):
        r = rows(c)
        pre = nn(s.ain[r, :], s.wq[...]) + rowv["bq"]
        cos, sin = s.ctab[r, :], s.stab[r, :]
        query = (turn(pre[:, :E], cos, sin)).astype(BF).astype(F32) * (1.0 / math.sqrt(HD))
        key = turn(pre[:, E : 2 * E], cos, sin).astype(BF).astype(F32)
        value = pre[:, 2 * E :].astype(BF).astype(F32)
        s.qs[r, :] = query.astype(BF)
        split_heads(s.qsm, r, query)
        split_heads(s.km, r, key)
        split_heads(s.vm, r, value)
        s.kt[:, r] = key.T.astype(BF)
        s.vt[:, r] = value.T.astype(BF)

    def expand(c):
        r = rows(c)
        pre = nn(s.mim[r, :], s.wu[...]) + rowv["bu"]
        cdf = 0.5 * (1.0 + lax.erf(pre * math.sqrt(0.5)))
        s.hid[r, :] = (pre * cdf).astype(BF)
        s.slope[r, :] = cdf + pre * jnp.exp(-0.5 * pre * pre) * (1.0 / math.sqrt(2.0 * math.pi))

    def contract(c):
        r = rows(c)
        back = (nt(s.gall[r, :], s.wd[...]) * s.slope[r, :]).astype(BF)
        s.hpg[r, :] = back
        s.vec[6:7, fcols] += jnp.sum(back.astype(F32), axis=0, keepdims=True)
        s.vec[4:5, gcols] += jnp.sum(s.gall[r, gcols].astype(F32), axis=0, keepdims=True)
        dout = nt(s.gall[r, :], s.wo[...]).astype(BF).astype(F32)
        s.do[r, :] = dout.astype(BF)
        split_heads(s.dom, r, dout)

    rb, lb, fb = lax.rem(col + 1, 4), lax.rem(col + 3, 4), lax.rem(col + 2, 4)
    blocks = {"own": col, "left": lb, "right": rb, "far": fb}
    outward = ("far", "right", "left", "own")

    def mark(flag, work, *args):
        def both():
            work(*args)
            done.add(flag)

        return both

    first = [0, 256, 768, 1536]

    def fold(values, how):
        return how(values.reshape(-1, 8, B), axis=0)

    def attend(i):
        q = pl.ds(i * B, B)
        for c in range(i + 1):
            kid = lax.broadcasted_iota(jnp.int32, (B, B), 0)
            qid = lax.broadcasted_iota(jnp.int32, (B, B), 1)
            allowed = s.segc[pl.ds(c * B, B), 0:1] == rowv["seg"][:, i * B : (i + 1) * B]
            allowed = allowed & (kid <= qid) if c == i else allowed
            s.cap[pl.ds(c * B, B), :] = jnp.where(allowed, 3e38, -1e30)

        for h in range(2):
            top = jnp.full((8, B), -1e30, F32)
            for c in range(i + 1):
                k, at_c = pl.ds(c * B, B), pl.ds(first[i] + c * B, B)
                scores = jnp.minimum(nt(s.km[h, k, :], s.qs[q, :]), s.cap[k, :])
                s.probs[h, at_c, :] = scores
                top = jnp.maximum(top, fold(scores, jnp.max))
            top = jnp.max(top, axis=0, keepdims=True)
            total = jnp.zeros((8, B), F32)
            for c in range(i + 1):
                at_c = pl.ds(first[i] + c * B, B)
                expo = jnp.exp(s.probs[h, at_c, :] - top)
                s.probs[h, at_c, :] = expo
                total = total + fold(expo, jnp.sum)
            inverse = 1.0 / jnp.sum(total, axis=0, keepdims=True)
            hrows = pl.ds(h * HD, HD)
            mix = jnp.zeros((HD, B), F32)
            for c in range(i + 1):
                at_c = pl.ds(first[i] + c * B, B)
                probs = s.probs[h, at_c, :] * inverse
                s.probs[h, at_c, :] = probs
                mix = mix + nn(s.vt[hrows, pl.ds(c * B, B)], probs.astype(BF))
            s.mt[hrows, q] = mix.astype(BF)

        s.mixed[q, :] = s.mt[:, q].astype(F32).T.astype(BF)

    def attend_back(i):
        q = pl.ds(i * B, B)

        for h in range(2):
            inner = jnp.zeros((8, B), F32)
            for c in range(i + 1):
                k, at_c = pl.ds(c * B, B), pl.ds(first[i] + c * B, B)
                probs = s.probs[h, at_c, :]
                dprob = nt(s.vm[h, k, :], s.do[q, :])
                s.cap[k, :] = dprob
                inner = inner + fold(probs * dprob, jnp.sum)
                s.dv[k, :] += nn(probs.astype(BF), s.dom[h, q, :])
            inner = jnp.sum(inner, axis=0, keepdims=True)
            hrows = pl.ds(h * HD, HD)
            dquery = jnp.zeros((HD, B), F32)
            for c in range(i + 1):
                k, at_c = pl.ds(c * B, B), pl.ds(first[i] + c * B, B)
                dscore = (s.probs[h, at_c, :] * (s.cap[k, :] - inner)).astype(BF)
                s.dk[k, :] += nn(dscore, s.qsm[h, q, :])
                dquery = dquery + nn(s.kt[hrows, k], dscore)
            s.dqt[hrows, q] = dquery * (1.0 / math.sqrt(HD))

    def branch(b):
        r = rows(b)
        s.op[r, :] = (nn(s.mixed[r, :], s.wo[...]) + nn(s.hid[r, :], s.wd[...])).astype(BF)

    def down_early():
        gall = jnp.concatenate([s.gall[rows(b), :] for b in (col, lb, rb)])

        @pl.loop(0, 4)
        def _(f):
            r = rows(f, 128)
            hid = jnp.concatenate([s.hid[rows(b), r] for b in (col, lb, rb)])
            s.acc[r, :] = tn(hid, gall)

    def down_grad():
        @pl.loop(0, 4)
        def _(f):
            r = rows(f, 128)
            s.g1[r, :] = (s.acc[r, :] + tn(s.hid[rows(fb), r], s.gall[rows(fb), :])).astype(BF)

        s.g1[F:, :] = nn(s.mt[...], s.gall[...]).astype(BF)

    def up_grad():
        @pl.loop(0, 4)
        def _(b):
            r = rows(b, 128)
            s.g2[r, :] = tn(s.hpg[:, r], s.mim[...]).astype(BF)

    def qkv_grad(b):
        r = rows(b)
        cos, sin = s.ctab[r, :], -s.stab[r, :]
        dq = turn(s.dqt[:, r].T, cos, sin).astype(BF)
        dk = turn(s.dk[r, :], cos, sin).astype(BF)
        dv = s.dv[r, :].astype(BF)
        both = jnp.concatenate([dq, dk, dv], axis=1)
        s.qkvg[r, :] = both
        ecols3 = pl.ds(pl.multiple_of(row * 3 * E, 3 * E), 3 * E)
        s.vec[5:6, ecols3] += jnp.sum(both.astype(F32), axis=0, keepdims=True)

    def qkv_weight_grad():
        @pl.loop(0, 3)
        def _(b):
            r = rows(b, E)
            s.g3[r, :] = tn(s.qkvg[:, r], s.ain[...]).astype(BF)

    def input_grad(b):
        r = rows(b)
        gain0, gain1 = wide(0), wide(1)
        attn = nt(s.qkvg[r, :], s.wq[...])
        mlp = nt(s.hpg[r, :], s.wu[...])
        normed = (s.xall[r, :].astype(F32) - s.mean[r, :]) * s.inv[r, :]
        s.ng[r, :] = (attn * gain0 + mlp * gain1).astype(BF)
        s.vec[0:1, :] += jnp.sum(attn * normed, axis=0, keepdims=True)
        s.vec[1:2, :] += jnp.sum(mlp * normed, axis=0, keepdims=True)
        s.vec[2:3, :] += jnp.sum(attn, axis=0, keepdims=True)
        s.vec[3:4, :] += jnp.sum(mlp, axis=0, keepdims=True)

    so, sn = under(s, "o_"), under(s, "n_")
    where = dict(core=core, x=x, row=row)
    sums = []
    ny = YROWS["n"]
    own = rows(col)

    def look(h, total):
        mean, inv = s.mean[own, :], s.inv[own, :]
        xv = s.xall[pl.ds(pl.multiple_of(col * B, B), ny), pl.ds(h * half, half)].astype(F32)
        normed = (xv - mean[:ny]) * inv[:ny]
        sums.append(jnp.sum(total, axis=1, keepdims=True))
        sums.append(jnp.sum(total * normed, axis=1, keepdims=True))

    def write_out():
        xv = s.xall[own, gcols].astype(F32) + (flat(bout[...]) + flat(bdown[...]))
        total = jnp.concatenate([total_y(so, row), total_z(s.op, so, col, row, YROWS["o"])])
        out[...] = (xv + total).astype(BF)

    def write_grad():
        yield ("n.y.sum", "n.y.end", "n.z.sum"), 0.4
        mean, inv = s.mean[own, :], s.inv[own, :]
        normed = (s.xall[own, gcols].astype(F32) - mean) * inv
        zsum = total_z(s.ng, sn, col, row, ny)
        first_sum = jnp.concatenate([sums[0] + sums[2], jnp.sum(zsum, axis=1, keepdims=True)])
        second = jnp.sum(zsum * normed[ny:], axis=1, keepdims=True)
        second_sum = jnp.concatenate([sums[1] + sums[3], second])
        lane = lax.broadcasted_iota(jnp.int32, (B, 128), 1)
        s.ssend[...] = jnp.where(lane < 4, first_sum, second_sum).T[:8, :]
        ys = net.go(s.ssend, s.srecv, y1)
        yield (ys,), 0.5
        ys.wait_recv()
        both = (s.ssend[...] + s.srecv[...]) * (1.0 / D)
        both = jnp.concatenate([both] * 16).T
        total = jnp.concatenate([total_y(sn, row), zsum])
        tgrad[...] = (
            s.gall[own, gcols].astype(F32) + inv * (total - both[:, 0:1] - normed * both[:, 4:5])
        ).astype(BF)

    def write_vectors():
        vout[0] = s.vs[2]
        vout[1] = s.vs[3]

    scatter(net, add, done, "o.", tuple("send." + b for b in outward), s.op, so, at, col, row, YROWS["o"])
    scatter(net, add, done, "n.", tuple("ng." + b for b in outward), s.ng, sn, at, col, row, ny, look)
    gate = ("g.r3", "g.r4", "g.l3", "g.l4")
    for b in outward:
        add(later(("op." + b,) + gate, 0.0, mark("send." + b, lambda: None)))
    reduce_weights(net, add, done, "a.", "g1", s.g1, under(s, "r0_", fin=s.f0), at, where, ROWS[0])
    reduce_weights(net, add, done, "b.", "g2", s.g2, under(s, "r1_", fin=s.f1), at, where, ROWS[1])
    reduce_weights(net, add, done, "c.", "g3", s.g3, under(s, "r2_", fin=s.f2), at, where, ROWS[2])
    writes = []

    def write_reduced(src, dst):
        writes.append(net.local(src, dst))

    for name, src, dst in (("a.", s.f0, f0_h), ("b.", s.f1, f1_h), ("c.", s.f2, f2_h)):
        add(later((name + "end",), 0.02, partial(write_reduced, src, dst)))
    add(reduce_vectors(net, done, s, at))
    add(later(("vsum",), 0.05, write_vectors))
    add(write_grad())
    for name, b in blocks.items():
        add(later(("nb", "x." + name), 0.5, mark("norm." + name, norm, b)))
        add(later(("wq", "norm." + name), 0.45, mark("proj." + name, project, b)))
    needs = tuple("proj." + name for name in blocks)
    for i in range(4):
        add(later(needs, 0.37 * (i + 1), mark(f"attf{i}", attend, i)))
        needs = (f"attf{i}",)
    for name, b in blocks.items():
        add(later(("wu", "norm." + name), 0.36, mark("exp." + name, expand, b)))
    for name in outward:
        needs = ("wo", "wd", "attf3", "exp." + name)
        add(later(needs, 0.55, mark("op." + name, branch, blocks[name])))
    for name, b in blocks.items():
        needs = ("wo", "wd", "g." + name, "exp." + name)
        add(later(needs, 0.43, mark("con." + name, contract, b)))
    near = ("own", "left", "right")
    needs = tuple("g." + name for name in near) + tuple("exp." + name for name in near)
    add(later(needs, 1.9, mark("g1early", down_early)))
    add(later(("g1early", "g.far", "exp.far", "attf3"), 0.95, mark("g1", down_grad)))
    allc = tuple("con." + name for name in blocks)
    add(later(allc, 2.2, mark("g2", up_grad)))
    needs = allc + ("attf3",)
    for i in range(4):
        add(later(needs, 0.43 * (i + 1), mark(f"attb{i}", attend_back, i)))
        needs = (f"attb{i}",)
    for name in outward:
        add(later(("attb3",), 0.26, mark("qg." + name, qkv_grad, blocks[name])))
    add(later(tuple("qg." + name for name in blocks), 1.4, mark("g3", qkv_weight_grad)))
    for name in outward:
        add(later(("qg." + name,), 0.68, mark("ng." + name, input_grad, blocks[name])))
    add(later(tuple("ng." + name for name in blocks), 0.0, mark("vec", lambda: None)))
    add(later(("o.y.end", "o.z.sum"), 0.3, mark("out", write_out)))
    run(tasks, done)
    for copy in writes:
        copy.wait()
    for copy in net.sent:
        copy.wait_send()


def tables():
    freq = np.arange(ROT // 2, dtype=np.float32)
    inverse = np.float32(10000.0) ** (np.float32(-2.0) * freq / np.float32(ROT))
    angle = np.arange(T, dtype=np.float32)[:, None] * inverse[None, :].astype(np.float32)
    cos, sin = np.cos(angle), np.sin(angle)
    ones, zeros = np.ones((T, HD - ROT), np.float32), np.zeros((T, HD - ROT), np.float32)
    ctab = np.concatenate([cos, cos, ones] * 2, axis=1)
    stab = np.concatenate([-sin, sin, zeros] * 2, axis=1)
    return ctab.astype(np.float32), stab.astype(np.float32)


def last(
    f0_h, f1_h, f2_h, vec_h, out_h, tgrad_h,
    out_o, tgrad_o, wq_o, bq_o, wo_o, bo_o, wu_o, bu_o, wd_o, bd_o, gain_o, bias_o,
    f0, f1, f2, vec, out, tgrad, wq, wo, wu, wd, bq, bo, bu, gain, bias, sems,
):
    row = lax.axis_index("row")
    copies = []

    def write(src, dst):
        copy = pltpu.make_async_copy(src, dst, sems.at[len(copies)])
        copy.start()
        copies.append(copy)
        return copy

    pairs = ((f0_h.at[0], f0.at[0]), (f0_h.at[1], f0.at[1]), (f1_h.at[0], f1.at[0]), (f1_h.at[1], f1.at[1]), (f2_h, f2), (vec_h, vec), (out_h, out), (tgrad_h, tgrad))
    reads = [write(a, b) for a, b in pairs]
    for core in range(2):
        reads[core].wait()
        for r in range(2):
            for k in range(4 * core, 4 * core + 4):
                piece = f0[core, k % 4, r].astype(F32)
                n = piece.shape[0]
                inside = max(0, min(n, F - k * n))
                if inside:
                    wd[pl.ds(r * F + k * n, inside), :] = piece[:inside]
                if inside < n:
                    wo[pl.ds(r * E + k * n + inside - F, n - inside), :] = piece[inside:]
            first, end = 4 * core * n, min(F, 4 * (core + 1) * n)
            done = pl.ds(r * F + first, end - first)
            write(wd.at[done], wd_o.at[done])
    write(wo, wo_o)
    for core in range(2):
        reads[2 + core].wait()
        for r in range(2):
            for k in (2 * core, 2 * core + 1):
                pair = [f1[core, (2 * k + h) % 4, r].astype(F32) for h in range(2)]
                wu[:, pl.ds(r * F + k * E, E)] = jnp.concatenate(pair).T
            done = pl.ds(r * F + 2 * core * E, 2 * E)
            write(wu.at[:, done], wu_o.at[:, done])
    reads[4].wait()
    for r in range(2):
        whole = jnp.concatenate([f2[k // 4, k % 4, r].astype(F32) for k in range(8)])
        for k in range(3):
            wq[k, :, pl.ds(r * E, E)] = whole[k * E : (k + 1) * E].T
    write(wq, wq_o)
    for copy in reads[5:]:
        copy.wait()
    write(out, out_o)
    write(tgrad, tgrad_o)
    half = D // 2
    left = row == 0

    def cut(values):
        return jnp.where(left, values[:, :half], values[:, half:])

    bo[...] = cut(vec[0, 4:5, :])
    for k in range(3):
        bq[k : k + 1, :E] = vec[0, 5:6, k * E : (k + 1) * E]
        bq[k : k + 1, E:] = vec[0, 5:6, (k + 3) * E : (k + 4) * E]
    bu[...] = vec[0, 6:7, :]
    gain[...] = cut(vec[1, 0:2, :])
    bias[...] = cut(vec[1, 2:4, :])
    for a, b in ((bq, bq_o), (bo, bo_o), (bo, bd_o), (bu, bu_o), (gain, gain_o), (bias, bias_o)):
        write(a, b)
    for copy in copies[len(reads) :]:
        copy.wait()


def on_device(
    tokens, segment_ids, w_qkv, b_qkv, w_out, b_out, w_up, b_up, w_down, b_down, norm_gain, norm_bias, cotangent
):
    ctab, stab = tables()
    vmem = pl.BlockSpec(memory_space=pltpu.VMEM)
    hbm = pl.BlockSpec(memory_space=pl.ANY)
    shape = jax.ShapeDtypeStruct
    early = [
        shape((2, 4, 2, ROWS[0] // 8, D // 2), BF),
        shape((2, 4, 2, ROWS[1] // 8, D // 2), BF),
        shape((2, 4, 2, ROWS[2] // 8, D // 2), BF),
        shape((2, 8, D), F32),
    ]
    out, tgrad, f0, f1, f2, vec = pl.pallas_call(
        body,
        out_shape=[
            shape((B, D // 2), BF),
            shape((B, D // 2), BF),
            *early,
        ],
        in_specs=[hbm] * 6 + [vmem] * 7 + [hbm] * 2,
        out_specs=[vmem, vmem, hbm, hbm, hbm, vmem],
        scratch_shapes=[pltpu.VMEM(*spec) for spec in SCRATCH.values()]
        + [pltpu.SemaphoreType.DMA((NSEM,)), pltpu.SemaphoreType.DMA((NSEM,))],
        compiler_params=pltpu.CompilerParams(
            collective_id=0, has_side_effects=True, vmem_limit_bytes=60 * 1024 * 1024
        ),
        name="block",
    )(
        tokens, cotangent, w_qkv, w_out, w_up, w_down, b_qkv, b_up.reshape(8, 128),
        b_out.reshape(4, 128), b_down.reshape(4, 128), norm_gain, norm_bias,
        segment_ids.reshape(8, 128), jnp.asarray(ctab), jnp.asarray(stab),
    )
    big = [
        ((3, D // 2, 2 * E), F32),
        ((2 * E, D // 2), F32),
        ((D // 2, 2 * F), F32),
        ((2 * F, D // 2), F32),
    ]
    small = [((3, 2 * E), F32), ((1, D // 2), F32), ((1, 2 * F), F32)] + [((2, D // 2), F32)] * 2
    results = pl.pallas_call(
        last,
        out_shape=[
            shape((B, D // 2), BF),
            shape((B, D // 2), BF),
            shape(*big[0]),
            shape((3, 2 * E), F32),
            shape(*big[1]),
            shape((1, D // 2), F32),
            shape(*big[2]),
            shape((1, 2 * F), F32),
            shape(*big[3]),
            shape((1, D // 2), F32),
            shape((2, D // 2), F32),
            shape((2, D // 2), F32),
        ],
        in_specs=[hbm] * 6,
        out_specs=[hbm] * 12,
        scratch_shapes=[pltpu.VMEM(e.shape, e.dtype) for e in early]
        + [pltpu.VMEM((B, D // 2), BF)] * 2
        + [pltpu.VMEM(*spec) for spec in big + small]
        + [pltpu.SemaphoreType.DMA((32,))],
        compiler_params=pltpu.CompilerParams(vmem_limit_bytes=60 * 1024 * 1024),
        name="last",
    )(f0, f1, f2, vec, out, tgrad)
    out, tgrad, wq, bq, wo, bo, wu, bu, wd, bd, gain, bias = results
    bo, bu, bd = bo.reshape(-1), bu.reshape(-1), bd.reshape(-1)
    return (out, tgrad, wq, bq, wo, bo, wu, bu, wd, bd, gain, bias)


def solution(mesh):
    in_specs = (
        P(("dp", "col"), "row"),
        P("dp"),
        P(None, "row", "col"),
        P(None, "col"),
        P("col", "row"),
        P("row"),
        P("row", "col"),
        P("col"),
        P("col", "row"),
        P("row"),
        P(None, "row"),
        P(None, "row"),
        P(("dp", "col"), "row"),
    )
    out_specs = (
        P(("dp", "col"), "row"),
        P(("dp", "col"), "row"),
        P(None, "row", "col"),
        P(None, "col"),
        P("col", "row"),
        P("row"),
        P("row", "col"),
        P("col"),
        P("col", "row"),
        P("row"),
        P(None, "row"),
        P(None, "row"),
    )
    return jax.shard_map(
        on_device, mesh=mesh, in_specs=in_specs, out_specs=out_specs, check_vma=False
    )
```
